32 devices in a mesh: sec: 8 (over z, core), patch: 4 (over y, x).
Axes of the slice: x: 2, y: 2, z: 4, core: 2. Of those that a mesh axis runs over, the one named last changes fastest.
Arguments:
- rhs: bfloat16 [24, 196608], P(None, ('sec', 'patch')), may hold values from -6 to 6
- curl_blocks: bfloat16 [2048, 4, 9216], P(('sec', 'patch')), may hold values from -0.3125 to 0.3125
- block_cols: int32 [2048, 4], P(('sec', 'patch')), may hold values from 0 to 63
- hole_mask: int32 [2048], P(('sec', 'patch')), may hold values 0 or 1
- edge_flip: int32 [196608], P(('sec', 'patch')), may hold values from 0 to 1
- send_list: int32 [8, 4, 4, 8], P('sec', 'patch'), may hold values from 0 to 63
- send_count: int32 [8, 4, 4], P('sec', 'patch'), may hold values from 5 to 8
- recv_list: int32 [8, 4, 4, 8], P('sec', 'patch'), may hold values from 0 to 63
- dtn_blocks: bfloat16 [8, 4, 4, 8, 9216], P('sec', 'patch'), may hold values from -0.4375 to 0.4375
Outputs:
- state: float32 [24, 196608], P(None, ('sec', 'patch'))
The draws below stay inside these ranges and needn't reach their ends.
Inputs may be any that keep to these rules, and one draw needn't show every extreme that they name: Slots f >= send_count carry no block.
All inputs are finite; a program needn't handle non-finite values. No bound on the sum of `hole_mask` on one device may be relied on, other than what follows from the above.
Results may differ from the reference program's by a relative error of at most 0.029.
Values may be sent and summed in bfloat16 or wider, within the bound.
No kernel may reach another device: no remote copies, remote signals or barrier semaphores. Data moves between devices by JAX's collectives and lax.ppermute only.
A program may use at most 64 MiB of HBM per device.

```python
import jax
import jax.numpy as jnp
from jax import lax

BS = 96
COLS = 24
NB = 64
K = 4
F = 8
NI = 8
ITERS = 8
TICKS = 2
BLOCKS = 2048
EDGES = 196608
N_SEC = 8
N_PATCH = 4


def with_ends(entries, stream_key, least, top_value):
    place = [jax.random.randint(jax.random.fold_in(stream_key, axis), (), 0, length) for axis, length in enumerate(entries.shape)]
    widest = entries.shape.index(max(entries.shape))
    next_to = place[:widest] + [(place[widest] + 1) % entries.shape[widest]] + place[widest + 1:]
    return entries.at[tuple(place)].set(least).at[tuple(next_to)].set(top_value)


def block_scale(rng, extent, shards, smallest, top_value):
    level, own = 1.0, jax.random.fold_in(rng, 6)
    for dim, shards_of in shards:
        draws = jnp.exp(jax.random.uniform(jax.random.fold_in(own, dim), (shards_of,), jnp.float32, smallest / len(shards), top_value / len(shards)))
        level = level * jnp.repeat(draws, extent[dim] // shards_of).reshape([-1 if axis == dim else 1 for axis in range(len(extent))])
    return level


def normal_values(rng, extent, scale, bound, shards=(), kind=jnp.bfloat16):
    level = block_scale(rng, extent, shards, -0.22, 0.18) if shards else 1.0
    drawn = jax.random.normal(rng, extent, jnp.float32) * scale * level
    return jnp.minimum(jnp.maximum(drawn, -bound), bound).astype(kind)


def setup_inputs(seed: int = 0) -> dict:
    streams_of = jax.random.split(jax.random.key(seed), 10)
    return {
        "rhs": normal_values(streams_of[0], (COLS, EDGES), 1.0, 6.0, ((1, 32),)),
        "curl_blocks": normal_values(streams_of[1], (BLOCKS, K, BS * BS), (K * BS) ** -0.5, 0.3125, ((0, 32),)),
        "block_cols": with_ends(jax.random.randint(streams_of[2], (BLOCKS, K), 0, NB), jax.random.fold_in(streams_of[2], 1), 0, NB - 1).astype(jnp.int32),
        "hole_mask": with_ends((jax.random.randint(streams_of[3], (BLOCKS,), 0, 8) < 7).astype(jnp.int32), jax.random.fold_in(streams_of[3], 1), 0, 1),
        "edge_flip": with_ends(jax.random.randint(streams_of[4], (EDGES,), 0, 2), jax.random.fold_in(streams_of[4], 1), 0, 1).astype(jnp.int32),
        "send_list": with_ends(jax.random.randint(streams_of[5], (N_SEC, N_PATCH, N_PATCH, F), 0, NB), jax.random.fold_in(streams_of[5], 1), 0, NB - 1).astype(jnp.int32),
        "send_count": with_ends(jax.random.randint(streams_of[6], (N_SEC, N_PATCH, N_PATCH), F - F // 4 - 1, F + 1), jax.random.fold_in(streams_of[6], 1), F - F // 4 - 1, F).astype(jnp.int32),
        "recv_list": with_ends(jax.random.randint(streams_of[7], (N_SEC, N_PATCH, N_PATCH, F), 0, NB), jax.random.fold_in(streams_of[7], 1), 0, NB - 1).astype(jnp.int32),
        "dtn_blocks": normal_values(streams_of[8], (N_SEC, N_PATCH, N_PATCH, F, BS * BS), (2 * BS) ** -0.5, 0.4375, ((0, 8), (1, 4))),
    }


def apply_curl(matrices, columns, state_bf):
    nearby = state_bf[:, columns]
    return jnp.einsum('nked,cnkd->cne', matrices.astype(jnp.float32), nearby, precision=lax.Precision.HIGHEST)


def apply_faces(received, dtn_mats, onehot):
    products = jnp.einsum('qfed,qfcd->qfce', dtn_mats.astype(jnp.float32), received, precision=lax.Precision.HIGHEST)
    products = lax.optimization_barrier(products.astype(jnp.bfloat16)).astype(jnp.float32)
    return jnp.einsum('qfn,qfce->cne', onehot, products, precision=lax.Precision.HIGHEST)


def pick_rows(table, index):
    return table[index]


def reference(rhs, curl_blocks, block_cols, hole_mask, edge_flip, send_list, send_count, recv_list, dtn_blocks):
    coupling = 0.85
    devs = N_SEC * N_PATCH
    source = rhs.astype(jnp.float32).reshape(COLS, N_SEC, N_PATCH, NB, BS).transpose(1, 2, 0, 3, 4)
    matrices = curl_blocks.reshape(devs, NB, K, BS, BS)
    columns = block_cols.reshape(devs, NB, K)
    keepers = hole_mask.reshape(N_SEC, N_PATCH, 1, NB, 1).astype(jnp.float32)
    edge_sign = (1 - 2 * edge_flip).astype(jnp.float32).reshape(N_SEC, N_PATCH, NB, BS)
    dtn_mats = dtn_blocks.reshape(devs, N_PATCH, F, BS, BS)
    filled = (jnp.arange(F)[None, None, None, :] < send_count[..., None]).astype(jnp.float32)
    onehot = (recv_list[..., None] == jnp.arange(NB)[None, None, None, None, :]).astype(jnp.float32)
    onehot = onehot.reshape(devs, N_PATCH, F, NB)
    state = keepers * source
    from_left = jnp.zeros((N_SEC, N_PATCH, COLS, NI, BS), jnp.float32)
    from_right = jnp.zeros((N_SEC, N_PATCH, COLS, NI, BS), jnp.float32)
    for segment in range(TICKS):
        state_bf = lax.optimization_barrier(state.astype(jnp.bfloat16)).astype(jnp.float32)
        by_block = state_bf.transpose(0, 1, 3, 2, 4)
        picked = jax.vmap(jax.vmap(pick_rows))(by_block, send_list)
        flips = jax.vmap(jax.vmap(pick_rows))(edge_sign, send_list)
        sent = picked * flips[:, :, :, :, None, :] * filled[..., None, None]
        received = sent.transpose(0, 2, 1, 3, 4, 5).reshape(devs, N_PATCH, F, COLS, BS)
        face_terms = lax.map(lambda group: apply_faces(group[0], group[1], group[2]), (received, dtn_mats, onehot))
        forcing = source + face_terms.reshape(N_SEC, N_PATCH, COLS, NB, BS)
        forcing = forcing.at[:, :, :, :NI].add(from_left)
        forcing = forcing.at[:, :, :, NB - NI:].add(from_right)
        for sweep_idx in range(ITERS):
            state_bf = lax.optimization_barrier(state.astype(jnp.bfloat16)).astype(jnp.float32)
            image = lax.map(lambda group: apply_curl(group[0], group[1], group[2]), (matrices, columns, state_bf.reshape(devs, COLS, NB, BS)))
            state = keepers * (forcing - coupling * image.reshape(N_SEC, N_PATCH, COLS, NB, BS))
        if segment < TICKS - 1:
            to_right = lax.optimization_barrier(state[:, :, :, NB - NI:].astype(jnp.bfloat16)).astype(jnp.float32)
            to_left = lax.optimization_barrier(state[:, :, :, :NI].astype(jnp.bfloat16)).astype(jnp.float32)
            from_left = jnp.concatenate([jnp.zeros_like(to_right[:1]), to_right[:-1]], axis=0)
            from_right = jnp.concatenate([to_left[1:], jnp.zeros_like(to_left[:1])], axis=0)
    return state.transpose(2, 0, 1, 3, 4).reshape(COLS, EDGES)
```

```python
import functools

import jax
import jax.numpy as jnp
from jax import lax
from jax.experimental import pallas as pl
from jax.experimental.pallas import tpu as pltpu
from jax.sharding import PartitionSpec as P

BS = 96
COLS = 24
NB = 64
K = 4
F = 8
NI = 8
ITERS = 8
TICKS = 2
COUPLING = 0.85

LANES = 128
PAD = 128
QUAD = 4
TILES = 3
VMEM_LIMIT = 30 * 2**20
UNROLL = 32

VMEM = pl.BlockSpec(memory_space=pltpu.VMEM)
SMEM = pl.BlockSpec(memory_space=pltpu.SMEM)


def params():
    return pltpu.CompilerParams(vmem_limit_bytes=VMEM_LIMIT)


def cost(flops, size):
    return pl.CostEstimate(flops=flops, bytes_accessed=size, transcendentals=0)


def iota(shape, axis):
    return lax.broadcasted_iota(jnp.int32, shape, axis)


def split_quad(tiles):
    first, second, third = tiles
    lane = iota(first.shape, 1)
    parts = (
        first,
        jnp.where(lane < 64, second, first),
        jnp.where(lane < 64, third, second),
        third,
    )
    keep = lane < BS
    return [
        jnp.where(keep, pltpu.roll(part, 32 * j, 1) if j else part, 0.0)
        for j, part in enumerate(parts)
    ]


def join_quad(blocks):
    lane = iota(blocks[0].shape, 1)
    parts = [
        pltpu.roll(block, LANES - 32 * j, 1) if j else block for j, block in enumerate(blocks)
    ]
    return [
        jnp.where(lane < 96, parts[0], parts[1]),
        jnp.where(lane < 64, parts[1], parts[2]),
        jnp.where(lane < 32, parts[2], parts[3]),
    ]


def write_sent(peers, send_ref, count_ref, sign_ref, state_ref, sent_ref):
    for q in range(peers):
        for f in range(F):
            block = send_ref[q, f]
            scale = jnp.where(f < count_ref[q], 1.0, 0.0).astype(jnp.float32)
            sign = sign_ref[block % QUAD, pl.ds(block // QUAD, 1), :] * scale
            picked = state_ref[block].astype(jnp.float32) * sign
            sent_ref[q * F + f] = picked.astype(jnp.bfloat16)


def prep_kernel(
    peers, send_ref, count_ref, hole_ref, flip_ref, rhs_ref, source_ref, state_ref, sign_ref, sent_ref
):
    quads = NB // QUAD
    flips = [
        1.0 - 2.0 * flip_ref[pl.ds(u, quads, stride=TILES), :].astype(jnp.float32)
        for u in range(TILES)
    ]
    for j, sign in enumerate(split_quad(flips)):
        sign_ref[j] = sign
    for q in range(quads):
        at = q * TILES * LANES
        tiles = [
            rhs_ref[:, at + u * LANES : at + (u + 1) * LANES].astype(jnp.float32)
            for u in range(TILES)
        ]
        for j, block in enumerate(split_quad(tiles)):
            n = q * QUAD + j
            source_ref[n] = block
            keep = hole_ref[n].astype(jnp.float32)
            state_ref[n] = (keep * block).astype(jnp.bfloat16)
    write_sent(peers, send_ref, count_ref, sign_ref, state_ref, sent_ref)


def picker(group):
    depth = 8 * TILES * group
    row = iota((32 * group, 2 * depth), 0)
    at = iota((32 * group, 2 * depth), 1)
    member, e = row // 32, row % 32
    r, j = e // QUAD, e % QUAD
    low = jnp.where(j == 0, 0, jnp.where(j == 1, 1, 2))
    high = jnp.where(j < 2, 0, j - 1)
    want_low = (r * TILES + low) * group + member
    want_high = (r * TILES + high) * group + member + depth
    return ((at == want_low) | (at == want_high)).astype(jnp.float32).astype(jnp.bfloat16)


def spread(select, rows, group):
    depth = 8 * TILES * group
    parts = [rows[g * depth : (g + 1) * depth] for g in range(3)]
    wide = jnp.concatenate(parts, axis=1)
    high = iota(wide.shape, 1) % LANES >= 64
    zero = jnp.zeros_like(wide)
    stacked = jnp.concatenate([jnp.where(high, zero, wide), jnp.where(high, wide, zero)], axis=0)
    picked = jnp.dot(select, stacked, preferred_element_type=jnp.float32).astype(jnp.bfloat16)
    pad = jnp.zeros((PAD - BS, LANES), jnp.bfloat16)
    phase = iota((32, LANES), 1) % QUAD
    results = []
    for member in range(group):
        mine = picked[32 * member : 32 * (member + 1)]
        square = jnp.concatenate(
            [mine[:, g * LANES : (g + 1) * LANES] for g in range(3)] + [pad], axis=0
        )
        turned = square.T
        bands = [turned[32 * a : 32 * (a + 1)] for a in range(4)]
        fixed = []
        for a in range(4):
            band = bands[a]
            for j in range(1, QUAD):
                band = jnp.where(phase == j, bands[(a - j) % 4], band)
            fixed.append(band)
        results.append(jnp.concatenate(fixed, axis=0))
    return results


def spread_kernel(peers, curl_ref, dtn_ref, matrix_ref, face_ref):
    select = picker(K)

    def curl_step(n, carry):
        for k, block in enumerate(spread(select, curl_ref[n], K)):
            matrix_ref[n, k * PAD : (k + 1) * PAD] = block
        return carry

    lax.fori_loop(0, NB, curl_step, 0, unroll=2)
    select_faces = picker(F)

    def face_step(q, carry):
        for f, block in enumerate(spread(select_faces, dtn_ref[q], F)):
            face_ref[q * F + f] = block
        return carry

    lax.fori_loop(0, peers, face_step, 0)


def add_faces(peers, target_ref, hole_ref, received_ref, face_ref, forcing_ref):
    products = []
    for i in range(peers * F):
        product = jnp.dot(received_ref[i], face_ref[i], preferred_element_type=jnp.float32)
        products.append(product.astype(jnp.bfloat16).astype(jnp.float32))
    for i, product in enumerate(products):
        n = target_ref[i // F, i % F]
        forcing_ref[n] = forcing_ref[n] + product
    for n in range(NB):
        forcing_ref[n] = forcing_ref[n] * hole_ref[n].astype(jnp.float32)


def sweep(cols_ref, hole_ref, matrix_ref, forcing_ref, old_ref, new_ref):
    def body(i, carry):
        images = []
        for step in range(UNROLL):
            n = i * UNROLL + step
            nearby = jnp.concatenate([old_ref[cols_ref[k, n]] for k in range(K)], axis=1)
            images.append(jnp.dot(nearby, matrix_ref[n], preferred_element_type=jnp.float32))
        for step in range(UNROLL):
            n = i * UNROLL + step
            scale = COUPLING * hole_ref[n].astype(jnp.float32)
            new_ref[n] = (forcing_ref[n] - scale * images[step]).astype(new_ref.dtype)
        return carry

    lax.fori_loop(0, NB // UNROLL, body, 0)


def first_tick_kernel(
    peers, cols_ref, hole_ref, target_ref, send_ref, count_ref, sign_ref, matrix_ref, face_ref,
    received_ref, source_ref, start_ref, state_ref, sent_ref, left_ref, right_ref, forcing_ref,
    other_ref,
):
    forcing_ref[...] = source_ref[...]
    add_faces(peers, target_ref, hole_ref, received_ref, face_ref, forcing_ref)
    state_ref[...] = start_ref[...]

    def two(i, carry):
        sweep(cols_ref, hole_ref, matrix_ref, forcing_ref, state_ref, other_ref)
        sweep(cols_ref, hole_ref, matrix_ref, forcing_ref, other_ref, state_ref)
        return carry

    lax.fori_loop(0, ITERS // 2, two, 0)
    left_ref[...] = state_ref[:NI]
    right_ref[...] = state_ref[NB - NI :]
    write_sent(peers, send_ref, count_ref, sign_ref, state_ref, sent_ref)


def last_tick_kernel(
    peers, cols_ref, hole_ref, target_ref, matrix_ref, face_ref, received_ref, source_ref, start_ref,
    from_left_ref, from_right_ref, out_ref, forcing_ref, state_ref, other_ref, final_ref,
):
    forcing_ref[...] = source_ref[...]
    forcing_ref[:NI] = forcing_ref[:NI] + from_left_ref[...].astype(jnp.float32)
    forcing_ref[NB - NI :] = forcing_ref[NB - NI :] + from_right_ref[...].astype(jnp.float32)
    add_faces(peers, target_ref, hole_ref, received_ref, face_ref, forcing_ref)
    state_ref[...] = start_ref[...]

    def two(i, carry):
        sweep(cols_ref, hole_ref, matrix_ref, forcing_ref, state_ref, other_ref)
        sweep(cols_ref, hole_ref, matrix_ref, forcing_ref, other_ref, state_ref)
        return carry

    lax.fori_loop(0, ITERS // 2 - 1, two, 0)
    sweep(cols_ref, hole_ref, matrix_ref, forcing_ref, state_ref, other_ref)
    sweep(cols_ref, hole_ref, matrix_ref, forcing_ref, other_ref, final_ref)
    for q in range(NB // QUAD):
        tiles = join_quad([final_ref[q * QUAD + j] for j in range(QUAD)])
        for u, tile in enumerate(tiles):
            at = (q * TILES + u) * LANES
            out_ref[:, at : at + LANES] = tile


def shifted(x, axis, by):
    size = lax.axis_size(axis)
    pairs = [(i, i + by) for i in range(size) if 0 <= i + by < size]
    return lax.ppermute(x, axis, pairs)


def shape(dims, dtype):
    return jax.ShapeDtypeStruct(dims, dtype)


def shards(
    rhs, curl_blocks, block_cols, hole_mask, edge_flip, send_list, send_count, recv_list, dtn_blocks
):
    peers = send_list.shape[2]
    f32, bf16 = jnp.float32, jnp.bfloat16
    tiles = BS * BS // LANES
    cols = block_cols.T
    sends, counts, targets = send_list[0, 0], send_count[0, 0], recv_list[0, 0]
    flips = edge_flip.reshape(NB * BS // LANES, LANES)
    curl_rows = curl_blocks.reshape(NB, K, tiles, LANES).transpose(0, 2, 1, 3)
    curl_rows = curl_rows.reshape(NB, tiles * K, LANES)
    dtn_rows = dtn_blocks[0, 0].reshape(peers, F, tiles, LANES).transpose(0, 2, 1, 3)
    dtn_rows = dtn_rows.reshape(peers, tiles * F, LANES)

    block_shape = (NB, COLS, PAD)
    face_shape = (peers * F, COLS, PAD)
    source, start, sign, sent = pl.pallas_call(
        functools.partial(prep_kernel, peers),
        out_shape=(
            shape(block_shape, f32),
            shape(block_shape, bf16),
            shape((QUAD, NB // QUAD, LANES), f32),
            shape(face_shape, bf16),
        ),
        in_specs=[SMEM] * 3 + [VMEM] * 2,
        out_specs=[VMEM] * 4,
        compiler_params=params(),
        cost_estimate=cost(10**6, 10**6),
    )(sends, counts, hole_mask, flips, rhs)

    matrices, faces = pl.pallas_call(
        functools.partial(spread_kernel, peers),
        out_shape=(shape((NB, K * PAD, PAD), bf16), shape((peers * F, PAD, PAD), bf16)),
        in_specs=[VMEM] * 2,
        out_specs=[VMEM] * 2,
        compiler_params=params(),
        cost_estimate=cost(4 * 10**9, 16 * 10**6),
    )(curl_rows, dtn_rows)

    def exchange(sent):
        sent = sent.reshape((peers, F, COLS, PAD))
        received = lax.all_to_all(sent, "patch", split_axis=0, concat_axis=0, tiled=True)
        return received.reshape(face_shape)

    received = exchange(sent)
    state, sent, to_left, to_right = pl.pallas_call(
        functools.partial(first_tick_kernel, peers),
        out_shape=(
            shape(block_shape, bf16),
            shape(face_shape, bf16),
            shape((NI, COLS, PAD), bf16),
            shape((NI, COLS, PAD), bf16),
        ),
        in_specs=[SMEM] * 5 + [VMEM] * 6,
        out_specs=[VMEM] * 4,
        scratch_shapes=[pltpu.VMEM(block_shape, f32), pltpu.VMEM(block_shape, bf16)],
        compiler_params=params(),
        cost_estimate=cost(10**10, 16 * 10**6),
    )(cols, hole_mask, targets, sends, counts, sign, matrices, faces, received, source, start)

    received = exchange(sent)
    from_left = shifted(to_right, "sec", 1)
    from_right = shifted(to_left, "sec", -1)
    return pl.pallas_call(
        functools.partial(last_tick_kernel, peers),
        out_shape=shape((COLS, NB * BS), f32),
        in_specs=[SMEM] * 3 + [VMEM] * 7,
        out_specs=VMEM,
        scratch_shapes=[
            pltpu.VMEM(block_shape, f32),
            pltpu.VMEM(block_shape, bf16),
            pltpu.VMEM(block_shape, bf16),
            pltpu.VMEM(block_shape, f32),
        ],
        compiler_params=params(),
        cost_estimate=cost(10**10, 16 * 10**6),
    )(cols, hole_mask, targets, matrices, faces, received, source, state, from_left, from_right)


def solution(mesh):
    in_specs = (
        P(None, ("sec", "patch")),
        P(("sec", "patch"), None, None),
        P(("sec", "patch"), None),
        P(("sec", "patch")),
        P(("sec", "patch")),
        P("sec", "patch", None, None),
        P("sec", "patch", None),
        P("sec", "patch", None, None),
        P("sec", "patch", None, None, None),
    )
    out_specs = P(None, ("sec", "patch"))
    return jax.shard_map(shards, mesh=mesh, in_specs=in_specs, out_specs=out_specs, check_vma=False)
```

```python
import functools

import jax
import jax.numpy as jnp
from jax import lax
from jax.experimental import pallas as pl
from jax.experimental.pallas import tpu as pltpu
from jax.sharding import PartitionSpec as P

BS = 96
COLS = 24
NB = 64
K = 4
F = 8
NI = 8
ITERS = 8
TICKS = 2
COUPLING = 0.85

LANES = 128
PAD = 128
QUAD = 4
TILES = 3
VMEM_LIMIT = 30 * 2**20
GROUP = 8

VMEM = pl.BlockSpec(memory_space=pltpu.VMEM)
SMEM = pl.BlockSpec(memory_space=pltpu.SMEM)
HBM = pl.BlockSpec(memory_space=pltpu.HBM)


def params():
    return pltpu.CompilerParams(vmem_limit_bytes=VMEM_LIMIT)


def cost(flops, size):
    return pl.CostEstimate(flops=flops, bytes_accessed=size, transcendentals=0)


def iota(shape, axis):
    return lax.broadcasted_iota(jnp.int32, shape, axis)


def split_quad(tiles):
    first, second, third = tiles
    lane = iota(first.shape, 1)
    parts = (
        first,
        jnp.where(lane < 64, second, first),
        jnp.where(lane < 64, third, second),
        third,
    )
    keep = lane < BS
    return [
        jnp.where(keep, pltpu.roll(part, 32 * j, 1) if j else part, 0.0)
        for j, part in enumerate(parts)
    ]


def join_quad(blocks):
    lane = iota(blocks[0].shape, 1)
    parts = [
        pltpu.roll(block, LANES - 32 * j, 1) if j else block for j, block in enumerate(blocks)
    ]
    return [
        jnp.where(lane < 96, parts[0], parts[1]),
        jnp.where(lane < 64, parts[1], parts[2]),
        jnp.where(lane < 32, parts[2], parts[3]),
    ]


def write_sent(peers, send_ref, count_ref, sign_ref, state_ref, sent_refs):
    me = lax.axis_index("patch")
    for i in range(peers):
        q = lax.rem(me + i, peers)
        for f in range(F):
            block = send_ref[q, f]
            scale = jnp.where(f < count_ref[q], 1.0, 0.0).astype(jnp.float32)
            sign = sign_ref[lax.rem(block, QUAD), pl.ds(lax.div(block, QUAD), 1), :] * scale
            picked = state_ref[block].astype(jnp.float32) * sign
            sent_refs[i][f] = picked.astype(jnp.bfloat16)


def copies(sources, targets, sems):
    started = [
        pltpu.make_async_copy(source, target, sems.at[i])
        for i, (source, target) in enumerate(zip(sources, targets))
    ]
    for one in started:
        one.start()
    return started


def prep_kernel(peers, *refs):
    sources = refs[:5]
    state_ref, sign_ref = refs[5:7]
    sent_refs = refs[7 : 7 + peers]
    held, sems = refs[7 + peers : -1], refs[-1]
    send_ref, count_ref, hole_ref, flip_ref, rhs_ref = held
    for one in copies(sources, held, sems):
        one.wait()
    quads = NB // QUAD
    flips = [
        1.0 - 2.0 * flip_ref[pl.ds(u, quads, stride=TILES), :].astype(jnp.float32)
        for u in range(TILES)
    ]
    for j, sign in enumerate(split_quad(flips)):
        sign_ref[j] = sign
    for q in range(quads):
        at = q * TILES * LANES
        tiles = [
            rhs_ref[:, at + u * LANES : at + (u + 1) * LANES].astype(jnp.float32)
            for u in range(TILES)
        ]
        for j, block in enumerate(split_quad(tiles)):
            n = q * QUAD + j
            keep = hole_ref[n].astype(jnp.float32)
            state_ref[n] = (keep * block).astype(jnp.bfloat16)
    write_sent(peers, send_ref, count_ref, sign_ref, state_ref, sent_refs)


def picker(group):
    depth = 8 * TILES * group
    row = iota((32 * group, 2 * depth), 0)
    at = iota((32 * group, 2 * depth), 1)
    member, e = row // 32, row % 32
    r, j = e // QUAD, e % QUAD
    low = jnp.where(j == 0, 0, jnp.where(j == 1, 1, 2))
    high = jnp.where(j < 2, 0, j - 1)
    want_low = (r * TILES + low) * group + member
    want_high = (r * TILES + high) * group + member + depth
    return ((at == want_low) | (at == want_high)).astype(jnp.float32).astype(jnp.bfloat16)


def stack(select, rows, group):
    depth = 8 * TILES * group
    wide = jnp.concatenate([rows[g * depth : (g + 1) * depth] for g in range(3)], axis=1)
    high = iota(wide.shape, 1) % LANES >= 64
    zero = jnp.zeros_like(wide)
    both = jnp.concatenate([jnp.where(high, zero, wide), jnp.where(high, wide, zero)], axis=0)
    return jnp.dot(select, both, preferred_element_type=jnp.float32).astype(jnp.bfloat16)


def unstack(picked, member):
    mine = picked[32 * member : 32 * (member + 1)]
    return jnp.concatenate([mine[:, g * LANES : (g + 1) * LANES] for g in range(3)], axis=0)


def turn(square):
    pad = jnp.zeros((PAD - BS, LANES), jnp.bfloat16)
    turned = jnp.concatenate([square, pad], axis=0).T
    bands = [turned[32 * a : 32 * (a + 1)] for a in range(4)]
    lane = iota((32, LANES), 1)
    for bit in (1, 2):
        odd = lane & bit == bit
        bands = [jnp.where(odd, bands[(a - bit) % 4], bands[a]) for a in range(4)]
    return jnp.concatenate(bands, axis=0)


def spread_kernel(
    peers, curl_hbm, dtn_hbm, matrix_ref, face_ref, curl_ref, dtn_ref, even_ref, odd_ref, sems
):
    groups = NB // GROUP
    started = copies(
        [curl_hbm.at[pl.ds(i * GROUP, GROUP)] for i in range(groups)] + [dtn_hbm],
        [curl_ref.at[pl.ds(i * GROUP, GROUP)] for i in range(groups)] + [dtn_ref],
        sems,
    )
    select = picker(K)

    def stacked(i):
        return [stack(select, curl_ref[i * GROUP + step], K) for step in range(GROUP)]

    def store(results, held_ref):
        for step, picked in enumerate(results):
            for k in range(K):
                held_ref[step * K + k] = unstack(picked, k)

    def finish(i, held_ref):
        for step in range(GROUP):
            for k in range(K):
                matrix_ref[i * GROUP + step, k * PAD : (k + 1) * PAD] = turn(held_ref[step * K + k])

    held = (even_ref, odd_ref)
    started[0].wait()
    store(stacked(0), even_ref)
    for i in range(groups):
        if i + 1 < groups:
            started[i + 1].wait()
            results = stacked(i + 1)
        finish(i, held[i % 2])
        if i + 1 < groups:
            store(results, held[(i + 1) % 2])
    started[groups].wait()
    select_faces = picker(F)

    def face_step(q, carry):
        picked = stack(select_faces, dtn_ref[q], F)
        for f in range(F):
            face_ref[q * F + f] = turn(unstack(picked, f))
        return carry

    lax.fori_loop(0, peers, face_step, 0)


def add_faces(peers, target_ref, hole_ref, received_refs, face_ref, forcing_ref):
    me = lax.axis_index("patch")
    products = []
    for i in range(peers):
        q = lax.rem(me + peers - i, peers)
        for f in range(F):
            product = jnp.dot(
                received_refs[i][f], face_ref[q * F + f], preferred_element_type=jnp.float32
            )
            products.append((q, f, product.astype(jnp.bfloat16).astype(jnp.float32)))
    for q, f, product in products:
        n = target_ref[q, f]
        forcing_ref[n] = forcing_ref[n] + hole_ref[n].astype(jnp.float32) * product


def sweep(cols_ref, hole_ref, matrix_ref, forcing_ref, old_ref, new_ref):
    images = []
    for n in range(NB):
        nearby = jnp.concatenate([old_ref[cols_ref[k, n]] for k in range(K)], axis=1)
        images.append(jnp.dot(nearby, matrix_ref[n], preferred_element_type=jnp.float32))
    for n in range(NB):
        scale = COUPLING * hole_ref[n].astype(jnp.float32)
        new_ref[n] = (forcing_ref[n] - scale * images[n]).astype(new_ref.dtype)


def first_tick_kernel(peers, *refs):
    cols_ref, hole_ref, target_ref, send_ref, count_ref = refs[:5]
    sign_ref, matrix_ref, face_ref, begin_ref, start_ref = refs[5:10]
    received_refs = refs[10 : 10 + peers]
    state_ref, left_ref, right_ref = refs[10 + peers : 13 + peers]
    sent_refs = refs[13 + peers : 13 + 2 * peers]
    forcing_ref, other_ref = refs[13 + 2 * peers :]
    forcing_ref[...] = begin_ref[...].astype(jnp.float32)
    add_faces(peers, target_ref, hole_ref, received_refs, face_ref, forcing_ref)
    state_ref[...] = start_ref[...]

    def two(i, carry):
        sweep(cols_ref, hole_ref, matrix_ref, forcing_ref, state_ref, other_ref)
        sweep(cols_ref, hole_ref, matrix_ref, forcing_ref, other_ref, state_ref)
        return carry

    lax.fori_loop(0, ITERS // 2, two, 0)
    left_ref[...] = state_ref[:NI]
    right_ref[...] = state_ref[NB - NI :]
    write_sent(peers, send_ref, count_ref, sign_ref, state_ref, sent_refs)


def last_tick_kernel(peers, *refs):
    cols_ref, hole_ref, target_ref, matrix_ref, face_ref, begin_ref, start_ref = refs[:7]
    from_left_ref, from_right_ref = refs[7:9]
    received_refs = refs[9 : 9 + peers]
    out_ref, forcing_ref, state_ref, other_ref, final_ref = refs[9 + peers :]
    forcing_ref[...] = begin_ref[...].astype(jnp.float32)
    for n in range(NI):
        for block, arrived in ((n, from_left_ref[n]), (NB - NI + n, from_right_ref[n])):
            keep = hole_ref[block].astype(jnp.float32)
            forcing_ref[block] = forcing_ref[block] + keep * arrived.astype(jnp.float32)
    add_faces(peers, target_ref, hole_ref, received_refs, face_ref, forcing_ref)
    state_ref[...] = start_ref[...]

    def two(i, carry):
        sweep(cols_ref, hole_ref, matrix_ref, forcing_ref, state_ref, other_ref)
        sweep(cols_ref, hole_ref, matrix_ref, forcing_ref, other_ref, state_ref)
        return carry

    lax.fori_loop(0, ITERS // 2 - 1, two, 0)
    sweep(cols_ref, hole_ref, matrix_ref, forcing_ref, state_ref, other_ref)
    sweep(cols_ref, hole_ref, matrix_ref, forcing_ref, other_ref, final_ref)
    for q in range(NB // QUAD):
        tiles = join_quad([final_ref[q * QUAD + j] for j in range(QUAD)])
        for u, tile in enumerate(tiles):
            at = (q * TILES + u) * LANES
            out_ref[:, at : at + LANES] = tile


def shifted(x, axis, by):
    size = lax.axis_size(axis)
    pairs = [(i, i + by) for i in range(size) if 0 <= i + by < size]
    return lax.ppermute(x, axis, pairs)


def shape(dims, dtype):
    return jax.ShapeDtypeStruct(dims, dtype)


def shards(
    rhs, curl_blocks, block_cols, hole_mask, edge_flip, send_list, send_count, recv_list, dtn_blocks
):
    peers = send_list.shape[2]
    f32, bf16 = jnp.float32, jnp.bfloat16
    tiles = BS * BS // LANES
    cols = block_cols.T
    sends, counts, targets = send_list[0, 0], send_count[0, 0], recv_list[0, 0]
    flips = edge_flip.reshape(NB * BS // LANES, LANES)
    curl_rows = curl_blocks.reshape(NB, K, tiles, LANES).transpose(0, 2, 1, 3)
    curl_rows = curl_rows.reshape(NB, tiles * K, LANES)
    dtn_rows = dtn_blocks[0, 0].reshape(peers, F, tiles, LANES).transpose(0, 2, 1, 3)
    dtn_rows = dtn_rows.reshape(peers, tiles * F, LANES)

    block_shape = (NB, COLS, PAD)
    face = shape((F, COLS, PAD), bf16)
    ends = shape((NI, COLS, PAD), bf16)
    state, sign, *sent = pl.pallas_call(
        functools.partial(prep_kernel, peers),
        out_shape=(shape(block_shape, bf16), shape((QUAD, NB // QUAD, LANES), f32)) + (face,) * peers,
        in_specs=[HBM] * 5,
        out_specs=[VMEM] * (2 + peers),
        scratch_shapes=[
            pltpu.SMEM(sends.shape, jnp.int32),
            pltpu.SMEM(counts.shape, jnp.int32),
            pltpu.SMEM(hole_mask.shape, jnp.int32),
            pltpu.VMEM(flips.shape, jnp.int32),
            pltpu.VMEM(rhs.shape, bf16),
            pltpu.SemaphoreType.DMA((5,)),
        ],
        compiler_params=params(),
        cost_estimate=cost(10**6, 10**6),
    )(sends, counts, hole_mask, flips, rhs)

    matrices, faces = pl.pallas_call(
        functools.partial(spread_kernel, peers),
        out_shape=(shape((NB, K * PAD, PAD), bf16), shape((peers * F, PAD, PAD), bf16)),
        in_specs=[HBM] * 2,
        out_specs=[VMEM] * 2,
        scratch_shapes=[
            pltpu.VMEM(curl_rows.shape, bf16),
            pltpu.VMEM(dtn_rows.shape, bf16),
            pltpu.VMEM((GROUP * K, BS, LANES), bf16),
            pltpu.VMEM((GROUP * K, BS, LANES), bf16),
            pltpu.SemaphoreType.DMA((NB // GROUP + 1,)),
        ],
        compiler_params=params(),
        cost_estimate=cost(4 * 10**9, 16 * 10**6),
    )(curl_rows, dtn_rows)

    def exchange(sent):
        pairs = [[(p, (p + i) % peers) for p in range(peers)] for i in range(peers)]
        return [sent[0]] + [lax.ppermute(sent[i], "patch", pairs[i]) for i in range(1, peers)]

    received = exchange(sent)
    begin = state
    state, to_left, to_right, *sent = pl.pallas_call(
        functools.partial(first_tick_kernel, peers),
        out_shape=(shape(block_shape, bf16), ends, ends) + (face,) * peers,
        in_specs=[SMEM] * 5 + [VMEM] * (5 + peers),
        out_specs=[VMEM] * (3 + peers),
        scratch_shapes=[pltpu.VMEM(block_shape, f32), pltpu.VMEM(block_shape, bf16)],
        compiler_params=params(),
        cost_estimate=cost(10**10, 16 * 10**6),
    )(cols, hole_mask, targets, sends, counts, sign, matrices, faces, begin, begin, *received)

    received = exchange(sent)
    from_left = shifted(to_right, "sec", 1)
    from_right = shifted(to_left, "sec", -1)
    return pl.pallas_call(
        functools.partial(last_tick_kernel, peers),
        out_shape=shape((COLS, NB * BS), f32),
        in_specs=[SMEM] * 3 + [VMEM] * (6 + peers),
        out_specs=VMEM,
        scratch_shapes=[
            pltpu.VMEM(block_shape, f32),
            pltpu.VMEM(block_shape, bf16),
            pltpu.VMEM(block_shape, bf16),
            pltpu.VMEM(block_shape, f32),
        ],
        compiler_params=params(),
        cost_estimate=cost(10**10, 16 * 10**6),
    )(cols, hole_mask, targets, matrices, faces, begin, state, from_left, from_right, *received)


def solution(mesh):
    in_specs = (
        P(None, ("sec", "patch")),
        P(("sec", "patch"), None, None),
        P(("sec", "patch"), None),
        P(("sec", "patch")),
        P(("sec", "patch")),
        P("sec", "patch", None, None),
        P("sec", "patch", None),
        P("sec", "patch", None, None),
        P("sec", "patch", None, None, None),
    )
    out_specs = P(None, ("sec", "patch"))
    return jax.shard_map(shards, mesh=mesh, in_specs=in_specs, out_specs=out_specs, check_vma=False)
```

```python
import functools

import jax
import jax.numpy as jnp
from jax import lax
from jax.experimental import pallas as pl
from jax.experimental.pallas import tpu as pltpu
from jax.sharding import PartitionSpec as P

BS = 96
COLS = 24
NB = 64
K = 4
F = 8
NI = 8
ITERS = 8
TICKS = 2
COUPLING = 0.85

LANES = 128
PAD = 128
QUAD = 4
TILES = 3
VMEM_LIMIT = 30 * 2**20
GROUP = 8
CHUNK = 32

VMEM = pl.BlockSpec(memory_space=pltpu.VMEM)
SMEM = pl.BlockSpec(memory_space=pltpu.SMEM)
HBM = pl.BlockSpec(memory_space=pltpu.HBM)


def params():
    return pltpu.CompilerParams(vmem_limit_bytes=VMEM_LIMIT)


def cost(flops, size):
    return pl.CostEstimate(flops=flops, bytes_accessed=size, transcendentals=0)


def iota(shape, axis):
    return lax.broadcasted_iota(jnp.int32, shape, axis)


def split_quad(tiles):
    first, second, third = tiles
    lane = iota(first.shape, 1)
    parts = (
        first,
        jnp.where(lane < 64, second, first),
        jnp.where(lane < 64, third, second),
        third,
    )
    keep = lane < BS
    return [
        jnp.where(keep, pltpu.roll(part, 32 * j, 1) if j else part, 0.0)
        for j, part in enumerate(parts)
    ]


def join_quad(blocks):
    lane = iota(blocks[0].shape, 1)
    parts = [
        pltpu.roll(block, LANES - 32 * j, 1) if j else block for j, block in enumerate(blocks)
    ]
    return [
        jnp.where(lane < 96, parts[0], parts[1]),
        jnp.where(lane < 64, parts[1], parts[2]),
        jnp.where(lane < 32, parts[2], parts[3]),
    ]


def write_sent(peers, send_ref, count_ref, sign_ref, state_ref, sent_refs):
    me = lax.axis_index("patch")
    for i in range(peers):
        q = me ^ i
        for f in range(F):
            block = send_ref[q, f]
            scale = jnp.where(f < count_ref[q], 1.0, 0.0).astype(jnp.float32)
            sign = sign_ref[lax.rem(block, QUAD), pl.ds(lax.div(block, QUAD), 1), :] * scale
            picked = state_ref[block].astype(jnp.float32) * sign
            sent_refs[i][f] = picked.astype(jnp.bfloat16)


def copies(sources, targets, sems):
    started = [
        pltpu.make_async_copy(source, target, sems.at[i])
        for i, (source, target) in enumerate(zip(sources, targets))
    ]
    for one in started:
        one.start()
    return started


def prep_kernel(peers, *refs):
    sources = refs[:5]
    state_ref, sign_ref = refs[5:7]
    sent_refs = refs[7 : 7 + peers]
    held, sems = refs[7 + peers : -1], refs[-1]
    send_ref, count_ref, hole_ref, flip_ref, rhs_ref = held
    for one in copies(sources, held, sems):
        one.wait()
    quads = NB // QUAD
    flips = [
        1.0 - 2.0 * flip_ref[pl.ds(u, quads, stride=TILES), :].astype(jnp.float32)
        for u in range(TILES)
    ]
    for j, sign in enumerate(split_quad(flips)):
        sign_ref[j] = sign
    for q in range(quads):
        at = q * TILES * LANES
        tiles = [
            rhs_ref[:, at + u * LANES : at + (u + 1) * LANES].astype(jnp.float32)
            for u in range(TILES)
        ]
        for j, block in enumerate(split_quad(tiles)):
            n = q * QUAD + j
            keep = hole_ref[n].astype(jnp.float32)
            state_ref[n] = (keep * block).astype(jnp.bfloat16)
    write_sent(peers, send_ref, count_ref, sign_ref, state_ref, sent_refs)


def picker(group):
    depth = 8 * TILES * group
    row = iota((32 * group, 2 * depth), 0)
    at = iota((32 * group, 2 * depth), 1)
    member, e = row // 32, row % 32
    r, j = e // QUAD, e % QUAD
    low = jnp.where(j == 0, 0, jnp.where(j == 1, 1, 2))
    high = jnp.where(j < 2, 0, j - 1)
    want_low = (r * TILES + low) * group + member
    want_high = (r * TILES + high) * group + member + depth
    return ((at == want_low) | (at == want_high)).astype(jnp.float32).astype(jnp.bfloat16)


def stack(select, rows, group):
    depth = 8 * TILES * group
    wide = jnp.concatenate([rows[g * depth : (g + 1) * depth] for g in range(3)], axis=1)
    high = iota(wide.shape, 1) % LANES >= 64
    zero = jnp.zeros_like(wide)
    both = jnp.concatenate([jnp.where(high, zero, wide), jnp.where(high, wide, zero)], axis=0)
    return jnp.dot(select, both, preferred_element_type=jnp.float32).astype(jnp.bfloat16)


def unstack(picked, member):
    mine = picked[32 * member : 32 * (member + 1)]
    return jnp.concatenate([mine[:, g * LANES : (g + 1) * LANES] for g in range(3)], axis=0)


def turn(square):
    pad = jnp.zeros((PAD - BS, LANES), jnp.bfloat16)
    turned = jnp.concatenate([square, pad], axis=0).T
    bands = [turned[32 * a : 32 * (a + 1)] for a in range(4)]
    lane = iota((32, LANES), 1)
    for bit in (1, 2):
        odd = lane & bit == bit
        bands = [jnp.where(odd, bands[(a - bit) % 4], bands[a]) for a in range(4)]
    return jnp.concatenate(bands[: BS // 32], axis=0)


def spread_kernel(
    peers, curl_hbm, dtn_hbm, matrix_ref, face_ref, curl_ref, dtn_ref, even_ref, odd_ref, sems
):
    groups = NB // GROUP
    started = copies(
        [curl_hbm.at[pl.ds(i * GROUP, GROUP)] for i in range(groups)] + [dtn_hbm],
        [curl_ref.at[pl.ds(i * GROUP, GROUP)] for i in range(groups)] + [dtn_ref],
        sems,
    )
    select, select_faces = picker(K), picker(F)
    tasks = [
        ([started[i]], [(select, curl_ref, i * GROUP + step, K) for step in range(GROUP)])
        for i in range(groups)
    ]
    quarter = GROUP * K // F
    for first in range(0, peers, quarter):
        waits = [started[groups]] if first == 0 else []
        members = range(first, min(first + quarter, peers))
        tasks.append((waits, [(select_faces, dtn_ref, q, F) for q in members]))

    def gather(task):
        waits, items = task
        for one in waits:
            one.wait()
        return [(rows, n, size, stack(pick, rows[n], size)) for pick, rows, n, size in items]

    def store(results, held_ref):
        for at, (_, _, size, picked) in enumerate(results):
            for member in range(size):
                held_ref[at * size + member] = unstack(picked, member)

    def finish(results, held_ref):
        for at, (rows, n, size, _) in enumerate(results):
            for member in range(size):
                half, side = member // 2, slice(member % 2 * PAD, (member % 2 + 1) * PAD)
                block = turn(held_ref[at * size + member])
                if rows is curl_ref:
                    matrix_ref[n, half, :, side] = block
                else:
                    face_ref[n, half, :, side] = block

    held = (even_ref, odd_ref)
    results = gather(tasks[0])
    store(results, held[0])
    for i in range(len(tasks)):
        upcoming = gather(tasks[i + 1]) if i + 1 < len(tasks) else []
        finish(results, held[i % 2])
        store(upcoming, held[(i + 1) % 2])
        results = upcoming


def paired(left, right, matrices):
    both = jnp.concatenate([left, right], axis=0)[:, :BS]
    wide = jnp.dot(both, matrices, preferred_element_type=jnp.float32)
    return wide[:COLS, :PAD], wide[COLS:, PAD:]


def add_faces(peers, target_ref, hole_ref, received_refs, face_ref, forcing_ref):
    me = lax.axis_index("patch")
    products = []
    for i in range(peers):
        q = me ^ i
        for f in range(0, F, 2):
            pair = paired(received_refs[i][f], received_refs[i][f + 1], face_ref[q, f // 2])
            for step, product in enumerate(pair):
                products.append((q, f + step, product.astype(jnp.bfloat16).astype(jnp.float32)))
    for q, f, product in products:
        n = target_ref[q, f]
        forcing_ref[n] = forcing_ref[n] + hole_ref[n].astype(jnp.float32) * product


def image_of(cols_ref, matrix_ref, old_ref, n):
    total = None
    for half in range(K // 2):
        nearby = [old_ref[cols_ref[2 * half + side, n]] for side in range(2)]
        left, right = paired(nearby[0], nearby[1], matrix_ref[n, half])
        total = left + right if total is None else total + (left + right)
    return total


def sweep(cols_ref, hole_ref, matrix_ref, forcing_ref, old_ref, new_ref):
    for first in range(0, NB, CHUNK):
        chunk = range(first, first + CHUNK)
        images = [image_of(cols_ref, matrix_ref, old_ref, n) for n in chunk]
        for n, image in zip(chunk, images):
            scale = COUPLING * hole_ref[n].astype(jnp.float32)
            new_ref[n] = (forcing_ref[n] - scale * image).astype(new_ref.dtype)


def first_tick_kernel(peers, *refs):
    cols_ref, hole_ref, target_ref, send_ref, count_ref = refs[:5]
    sign_ref, matrix_ref, face_ref, begin_ref, start_ref = refs[5:10]
    received_refs = refs[10 : 10 + peers]
    state_ref, swap_in_ref, swap_out_ref = refs[10 + peers : 13 + peers]
    sent_refs = refs[13 + peers : 13 + 2 * peers]
    forcing_ref, other_ref = refs[13 + 2 * peers :]
    forcing_ref[...] = begin_ref[...].astype(jnp.float32)
    add_faces(peers, target_ref, hole_ref, received_refs, face_ref, forcing_ref)
    state_ref[...] = start_ref[...]

    def two(i, carry):
        sweep(cols_ref, hole_ref, matrix_ref, forcing_ref, state_ref, other_ref)
        sweep(cols_ref, hole_ref, matrix_ref, forcing_ref, other_ref, state_ref)
        return carry

    lax.fori_loop(0, ITERS // 2, two, 0)
    low, high = state_ref[:NI], state_ref[NB - NI :]
    even = lax.rem(lax.axis_index("sec"), 2) == 0
    swap_in_ref[...] = jnp.where(even, high, low)
    swap_out_ref[...] = jnp.where(even, low, high)
    write_sent(peers, send_ref, count_ref, sign_ref, state_ref, sent_refs)


def first_image_kernel(cols_ref, matrix_ref, state_ref, image_ref):
    for n in range(NB):
        image_ref[n] = image_of(cols_ref, matrix_ref, state_ref, n)


def last_tick_kernel(peers, *refs):
    cols_ref, hole_ref, target_ref, matrix_ref, face_ref, begin_ref, image_ref = refs[:7]
    swap_in_ref, swap_out_ref = refs[7:9]
    received_refs = refs[9 : 9 + peers]
    out_ref, forcing_ref, state_ref, other_ref, final_ref = refs[9 + peers :]
    forcing_ref[...] = begin_ref[...].astype(jnp.float32)
    even = lax.rem(lax.axis_index("sec"), 2) == 0
    for n in range(NI):
        inner, outer = swap_in_ref[n], swap_out_ref[n]
        from_left = jnp.where(even, outer, inner)
        from_right = jnp.where(even, inner, outer)
        for block, arrived in ((n, from_left), (NB - NI + n, from_right)):
            keep = hole_ref[block].astype(jnp.float32)
            forcing_ref[block] = forcing_ref[block] + keep * arrived.astype(jnp.float32)
    add_faces(peers, target_ref, hole_ref, received_refs, face_ref, forcing_ref)
    for n in range(NB):
        scale = COUPLING * hole_ref[n].astype(jnp.float32)
        state_ref[n] = (forcing_ref[n] - scale * image_ref[n]).astype(jnp.bfloat16)

    def two(i, carry):
        sweep(cols_ref, hole_ref, matrix_ref, forcing_ref, state_ref, other_ref)
        sweep(cols_ref, hole_ref, matrix_ref, forcing_ref, other_ref, state_ref)
        return carry

    lax.fori_loop(0, ITERS // 2 - 1, two, 0)
    sweep(cols_ref, hole_ref, matrix_ref, forcing_ref, state_ref, final_ref)
    for q in range(NB // QUAD):
        tiles = join_quad([final_ref[q * QUAD + j] for j in range(QUAD)])
        for u, tile in enumerate(tiles):
            at = (q * TILES + u) * LANES
            out_ref[:, at : at + LANES] = tile


def swapped(x, axis, first):
    size = lax.axis_size(axis)
    pairs = []
    for i in range(first, size - 1, 2):
        pairs += [(i, i + 1), (i + 1, i)]
    return lax.ppermute(x, axis, pairs)


def shape(dims, dtype):
    return jax.ShapeDtypeStruct(dims, dtype)


def shards(
    rhs, curl_blocks, block_cols, hole_mask, edge_flip, send_list, send_count, recv_list, dtn_blocks
):
    peers = send_list.shape[2]
    f32, bf16 = jnp.float32, jnp.bfloat16
    tiles = BS * BS // LANES
    cols = block_cols.T
    in_hbm = functools.partial(pltpu.with_memory_space_constraint, memory_space=pltpu.HBM)
    sends, counts, targets = send_list[0, 0], send_count[0, 0], recv_list[0, 0]
    flips = edge_flip.reshape(NB * BS // LANES, LANES)
    curl_rows = curl_blocks.reshape(NB, K, tiles, LANES).transpose(0, 2, 1, 3)
    curl_rows = curl_rows.reshape(NB, tiles * K, LANES)
    dtn_rows = dtn_blocks[0, 0].reshape(peers, F, tiles, LANES).transpose(0, 2, 1, 3)
    dtn_rows = dtn_rows.reshape(peers, tiles * F, LANES)

    block_shape = (NB, COLS, PAD)
    face = shape((F, COLS, PAD), bf16)
    ends = shape((NI, COLS, PAD), bf16)
    state, sign, *sent = pl.pallas_call(
        functools.partial(prep_kernel, peers),
        out_shape=(shape(block_shape, bf16), shape((QUAD, NB // QUAD, LANES), f32)) + (face,) * peers,
        in_specs=[HBM] * 5,
        out_specs=[VMEM] * (2 + peers),
        scratch_shapes=[
            pltpu.SMEM(sends.shape, jnp.int32),
            pltpu.SMEM(counts.shape, jnp.int32),
            pltpu.SMEM(hole_mask.shape, jnp.int32),
            pltpu.VMEM(flips.shape, jnp.int32),
            pltpu.VMEM(rhs.shape, bf16),
            pltpu.SemaphoreType.DMA((5,)),
        ],
        compiler_params=params(),
        cost_estimate=cost(10**6, 10**6),
    )(*map(in_hbm, (sends, counts, hole_mask, flips, rhs)))

    matrices, faces = pl.pallas_call(
        functools.partial(spread_kernel, peers),
        out_shape=(shape((NB, K // 2, BS, 2 * PAD), bf16), shape((peers, F // 2, BS, 2 * PAD), bf16)),
        in_specs=[HBM] * 2,
        out_specs=[VMEM] * 2,
        scratch_shapes=[
            pltpu.VMEM(curl_rows.shape, bf16),
            pltpu.VMEM(dtn_rows.shape, bf16),
            pltpu.VMEM((GROUP * K, BS, LANES), bf16),
            pltpu.VMEM((GROUP * K, BS, LANES), bf16),
            pltpu.SemaphoreType.DMA((NB // GROUP + 1,)),
        ],
        compiler_params=params(),
        cost_estimate=cost(4 * 10**9, 16 * 10**6),
    )(in_hbm(curl_rows), in_hbm(dtn_rows))

    def exchange(sent):
        pairs = [[(p, p ^ i) for p in range(peers)] for i in range(peers)]
        return [sent[0]] + [lax.ppermute(sent[i], "patch", pairs[i]) for i in range(1, peers)]

    received = exchange(sent)
    begin = state
    state, swap_in, swap_out, *sent = pl.pallas_call(
        functools.partial(first_tick_kernel, peers),
        out_shape=(shape(block_shape, bf16), ends, ends) + (face,) * peers,
        in_specs=[SMEM] * 5 + [VMEM] * (5 + peers),
        out_specs=[VMEM] * (3 + peers),
        scratch_shapes=[pltpu.VMEM(block_shape, f32), pltpu.VMEM(block_shape, bf16)],
        compiler_params=params(),
        cost_estimate=cost(10**10, 16 * 10**6),
    )(cols, hole_mask, targets, sends, counts, sign, matrices, faces, begin, begin, *received)

    received = exchange(sent)
    swap_out = swapped(swap_out, "sec", 1)
    swap_in = swapped(swap_in, "sec", 0)
    image = pl.pallas_call(
        first_image_kernel,
        out_shape=shape(block_shape, f32),
        in_specs=[SMEM] + [VMEM] * 2,
        out_specs=VMEM,
        compiler_params=params(),
        cost_estimate=cost(10**9, 8 * 10**6),
    )(cols, matrices, state)
    return pl.pallas_call(
        functools.partial(last_tick_kernel, peers),
        out_shape=shape((COLS, NB * BS), f32),
        in_specs=[SMEM] * 3 + [VMEM] * (6 + peers),
        out_specs=VMEM,
        scratch_shapes=[
            pltpu.VMEM(block_shape, f32),
            pltpu.VMEM(block_shape, bf16),
            pltpu.VMEM(block_shape, bf16),
            pltpu.VMEM(block_shape, f32),
        ],
        compiler_params=params(),
        cost_estimate=cost(10**10, 16 * 10**6),
    )(cols, hole_mask, targets, matrices, faces, begin, image, swap_in, swap_out, *received)


def solution(mesh):
    in_specs = (
        P(None, ("sec", "patch")),
        P(("sec", "patch"), None, None),
        P(("sec", "patch"), None),
        P(("sec", "patch")),
        P(("sec", "patch")),
        P("sec", "patch", None, None),
        P("sec", "patch", None),
        P("sec", "patch", None, None),
        P("sec", "patch", None, None, None),
    )
    out_specs = P(None, ("sec", "patch"))
    return jax.shard_map(shards, mesh=mesh, in_specs=in_specs, out_specs=out_specs, check_vma=False)
```

```python
import functools

import jax
import jax.numpy as jnp
from jax import lax
from jax.experimental import pallas as pl
from jax.experimental.pallas import tpu as pltpu
from jax.sharding import PartitionSpec as P

BS = 96
COLS = 24
NB = 64
K = 4
F = 8
NI = 8
ITERS = 8
TICKS = 2
COUPLING = 0.85

LANES = 128
PAD = 128
QUAD = 4
TILES = 3
VMEM_LIMIT = 30 * 2**20
STAGES = (16, 16, 16, 16)
PIECE = 8
CHUNK = 32

VMEM = pl.BlockSpec(memory_space=pltpu.VMEM)
SMEM = pl.BlockSpec(memory_space=pltpu.SMEM)
HBM = pl.BlockSpec(memory_space=pltpu.HBM)


def params():
    return pltpu.CompilerParams(vmem_limit_bytes=VMEM_LIMIT)


def cost(flops, size):
    return pl.CostEstimate(flops=flops, bytes_accessed=size, transcendentals=0)


def iota(shape, axis):
    return lax.broadcasted_iota(jnp.int32, shape, axis)


def split_quad(tiles):
    first, second, third = tiles
    lane = iota(first.shape, 1)
    parts = (
        first,
        jnp.where(lane < 64, second, first),
        jnp.where(lane < 64, third, second),
        third,
    )
    keep = lane < BS
    return [
        jnp.where(keep, pltpu.roll(part, 32 * j, 1) if j else part, 0.0)
        for j, part in enumerate(parts)
    ]


def join_quad(blocks):
    lane = iota(blocks[0].shape, 1)
    parts = [
        pltpu.roll(block, LANES - 32 * j, 1) if j else block for j, block in enumerate(blocks)
    ]
    return [
        jnp.where(lane < 96, parts[0], parts[1]),
        jnp.where(lane < 64, parts[1], parts[2]),
        jnp.where(lane < 32, parts[2], parts[3]),
    ]


def write_sent(peers, send_ref, count_ref, sign_ref, state_ref, sent_refs):
    me = lax.axis_index("patch")
    for i in range(peers):
        q = me ^ i
        for f in range(F):
            block = send_ref[q, f]
            scale = jnp.where(f < count_ref[q], 1.0, 0.0).astype(jnp.float32)
            sign = sign_ref[lax.rem(block, QUAD), pl.ds(lax.div(block, QUAD), 1), :] * scale
            picked = state_ref[block].astype(jnp.float32) * sign
            sent_refs[i][f] = picked.astype(jnp.bfloat16)


def copies(sources, targets, sems):
    started = [
        pltpu.make_async_copy(source, target, sems.at[i])
        for i, (source, target) in enumerate(zip(sources, targets))
    ]
    for one in started:
        one.start()
    return started


def prep_kernel(peers, *refs):
    sources = refs[:5]
    state_ref, sign_ref = refs[5:7]
    sent_refs = refs[7 : 7 + peers]
    held, sems = refs[7 + peers : -1], refs[-1]
    send_ref, count_ref, hole_ref, flip_ref, rhs_ref = held
    for one in copies(sources, held, sems):
        one.wait()
    quads = NB // QUAD
    flips = [
        1.0 - 2.0 * flip_ref[pl.ds(u, quads, stride=TILES), :].astype(jnp.float32)
        for u in range(TILES)
    ]
    for j, sign in enumerate(split_quad(flips)):
        sign_ref[j] = sign
    for q in range(quads):
        at = q * TILES * LANES
        tiles = [
            rhs_ref[:, at + u * LANES : at + (u + 1) * LANES].astype(jnp.float32)
            for u in range(TILES)
        ]
        for j, block in enumerate(split_quad(tiles)):
            n = q * QUAD + j
            keep = hole_ref[n].astype(jnp.float32)
            state_ref[n] = (keep * block).astype(jnp.bfloat16)
    write_sent(peers, send_ref, count_ref, sign_ref, state_ref, sent_refs)


def picker(group):
    depth = 8 * TILES * group
    row = iota((32 * group, 2 * depth), 0)
    at = iota((32 * group, 2 * depth), 1)
    member, e = row // 32, row % 32
    r, j = e // QUAD, e % QUAD
    low = jnp.where(j == 0, 0, jnp.where(j == 1, 1, 2))
    high = jnp.where(j < 2, 0, j - 1)
    want_low = (r * TILES + low) * group + member
    want_high = (r * TILES + high) * group + member + depth
    return ((at == want_low) | (at == want_high)).astype(jnp.float32).astype(jnp.bfloat16)


def stack(select, rows, group):
    depth = 8 * TILES * group
    wide = jnp.concatenate([rows[g * depth : (g + 1) * depth] for g in range(3)], axis=1)
    high = iota(wide.shape, 1) % LANES >= 64
    zero = jnp.zeros_like(wide)
    both = jnp.concatenate([jnp.where(high, zero, wide), jnp.where(high, wide, zero)], axis=0)
    return jnp.dot(select, both, preferred_element_type=jnp.float32).astype(jnp.bfloat16)


def unstack(picked, member):
    mine = picked[32 * member : 32 * (member + 1)]
    return jnp.concatenate([mine[:, g * LANES : (g + 1) * LANES] for g in range(3)], axis=0)


def turn(square):
    pad = jnp.zeros((PAD - BS, LANES), jnp.bfloat16)
    turned = jnp.concatenate([square, pad], axis=0).T
    bands = [turned[32 * a : 32 * (a + 1)] for a in range(4)]
    lane = iota((32, LANES), 1)
    for bit in (1, 2):
        odd = lane & bit == bit
        bands = [jnp.where(odd, bands[(a - bit) % 4], bands[a]) for a in range(4)]
    return jnp.concatenate(bands[: BS // 32], axis=0)


def spread_kernel(
    peers, curl_hbm, dtn_hbm, matrix_ref, face_ref, curl_ref, dtn_ref, even_ref, odd_ref, sems
):
    pieces = NB // PIECE
    started = copies(
        [curl_hbm.at[pl.ds(i * PIECE, PIECE)] for i in range(pieces)] + [dtn_hbm],
        [curl_ref.at[pl.ds(i * PIECE, PIECE)] for i in range(pieces)] + [dtn_ref],
        sems,
    )
    select, select_faces = picker(K), picker(F)
    tasks, done = [], 0
    for size in STAGES:
        waits = [started[i] for i in range(-(-done // PIECE), -(-(done + size) // PIECE))]
        tasks.append((waits, [(select, curl_ref, done + step, K) for step in range(size)]))
        done += size
    quarter = max(STAGES) * K // F
    for first in range(0, peers, quarter):
        waits = [started[pieces]] if first == 0 else []
        members = range(first, min(first + quarter, peers))
        faces = [(select_faces, dtn_ref, q, F) for q in members]
        tasks.append((waits, faces))

    def gather(task):
        waits, items = task
        for one in waits:
            one.wait()
        return [(rows, n, size, stack(pick, rows[n], size)) for pick, rows, n, size in items]

    def store(results, held_ref):
        for at, (_, _, size, picked) in enumerate(results):
            for member in range(size):
                held_ref[at * size + member] = unstack(picked, member)

    def finish(results, held_ref):
        for at, (rows, n, size, _) in enumerate(results):
            for member in range(size):
                half, side = member // 2, slice(member % 2 * PAD, (member % 2 + 1) * PAD)
                block = turn(held_ref[at * size + member])
                if rows is curl_ref:
                    matrix_ref[n, half, :, side] = block
                else:
                    face_ref[n, half, :, side] = block

    held = (even_ref, odd_ref)
    results = gather(tasks[0])
    store(results, held[0])
    for i in range(len(tasks)):
        upcoming = gather(tasks[i + 1]) if i + 1 < len(tasks) else []
        finish(results, held[i % 2])
        store(upcoming, held[(i + 1) % 2])
        results = upcoming


def paired(left, right, matrices):
    both = jnp.concatenate([left, right], axis=0)[:, :BS]
    wide = jnp.dot(both, matrices, preferred_element_type=jnp.float32)
    return wide[:COLS, :PAD], wide[COLS:, PAD:]


def add_faces(peers, target_ref, hole_ref, received_refs, face_ref, forcing_ref):
    me = lax.axis_index("patch")
    products = []
    for i in range(peers):
        q = me ^ i
        for f in range(0, F, 2):
            pair = paired(received_refs[i][f], received_refs[i][f + 1], face_ref[q, f // 2])
            for step, product in enumerate(pair):
                products.append((q, f + step, product.astype(jnp.bfloat16).astype(jnp.float32)))
    for q, f, product in products:
        n = target_ref[q, f]
        forcing_ref[n] = forcing_ref[n] + hole_ref[n].astype(jnp.float32) * product


def image_of(cols_ref, matrix_ref, old_ref, n):
    total = None
    for half in range(K // 2):
        nearby = [old_ref[cols_ref[2 * half + side, n]] for side in range(2)]
        left, right = paired(nearby[0], nearby[1], matrix_ref[n, half])
        total = left + right if total is None else total + (left + right)
    return total


def sweep(cols_ref, hole_ref, matrix_ref, forcing_ref, old_ref, new_ref):
    for first in range(0, NB, CHUNK):
        chunk = range(first, first + CHUNK)
        images = [image_of(cols_ref, matrix_ref, old_ref, n) for n in chunk]
        for n, image in zip(chunk, images):
            scale = COUPLING * hole_ref[n].astype(jnp.float32)
            new_ref[n] = (forcing_ref[n] - scale * image).astype(new_ref.dtype)


def first_tick_kernel(peers, *refs):
    cols_ref, hole_ref, target_ref, send_ref, count_ref = refs[:5]
    sign_ref, matrix_ref, face_ref, begin_ref, start_ref = refs[5:10]
    received_refs = refs[10 : 10 + peers]
    state_ref, swap_in_ref, swap_out_ref = refs[10 + peers : 13 + peers]
    sent_refs = refs[13 + peers : 13 + 2 * peers]
    forcing_ref, other_ref = refs[13 + 2 * peers :]
    forcing_ref[...] = begin_ref[...].astype(jnp.float32)
    add_faces(peers, target_ref, hole_ref, received_refs, face_ref, forcing_ref)
    state_ref[...] = start_ref[...]

    def two(i, carry):
        sweep(cols_ref, hole_ref, matrix_ref, forcing_ref, state_ref, other_ref)
        sweep(cols_ref, hole_ref, matrix_ref, forcing_ref, other_ref, state_ref)
        return carry

    lax.fori_loop(0, ITERS // 2, two, 0)
    low, high = state_ref[:NI], state_ref[NB - NI :]
    even = lax.rem(lax.axis_index("sec"), 2) == 0
    swap_in_ref[...] = jnp.where(even, high, low)
    swap_out_ref[...] = jnp.where(even, low, high)
    write_sent(peers, send_ref, count_ref, sign_ref, state_ref, sent_refs)


def first_image_kernel(cols_ref, matrix_ref, state_ref, image_ref):
    for n in range(NB):
        image_ref[n] = image_of(cols_ref, matrix_ref, state_ref, n)


def last_tick_kernel(peers, *refs):
    cols_ref, hole_ref, target_ref, matrix_ref, face_ref, begin_ref, image_ref = refs[:7]
    swap_in_ref, swap_out_ref = refs[7:9]
    received_refs = refs[9 : 9 + peers]
    out_ref, forcing_ref, state_ref, other_ref, final_ref = refs[9 + peers :]
    forcing_ref[...] = begin_ref[...].astype(jnp.float32)
    even = lax.rem(lax.axis_index("sec"), 2) == 0
    for n in range(NI):
        inner, outer = swap_in_ref[n], swap_out_ref[n]
        from_left = jnp.where(even, outer, inner)
        from_right = jnp.where(even, inner, outer)
        for block, arrived in ((n, from_left), (NB - NI + n, from_right)):
            keep = hole_ref[block].astype(jnp.float32)
            forcing_ref[block] = forcing_ref[block] + keep * arrived.astype(jnp.float32)
    add_faces(peers, target_ref, hole_ref, received_refs, face_ref, forcing_ref)
    for n in range(NB):
        scale = COUPLING * hole_ref[n].astype(jnp.float32)
        state_ref[n] = (forcing_ref[n] - scale * image_ref[n]).astype(jnp.bfloat16)

    def two(i, carry):
        sweep(cols_ref, hole_ref, matrix_ref, forcing_ref, state_ref, other_ref)
        sweep(cols_ref, hole_ref, matrix_ref, forcing_ref, other_ref, state_ref)
        return carry

    lax.fori_loop(0, ITERS // 2 - 1, two, 0)
    sweep(cols_ref, hole_ref, matrix_ref, forcing_ref, state_ref, final_ref)
    for q in range(NB // QUAD):
        tiles = join_quad([final_ref[q * QUAD + j] for j in range(QUAD)])
        for u, tile in enumerate(tiles):
            at = (q * TILES + u) * LANES
            out_ref[:, at : at + LANES] = tile


def swapped(x, axis, first):
    size = lax.axis_size(axis)
    pairs = []
    for i in range(first, size - 1, 2):
        pairs += [(i, i + 1), (i + 1, i)]
    return lax.ppermute(x, axis, pairs)


def shape(dims, dtype):
    return jax.ShapeDtypeStruct(dims, dtype)


def shards(
    rhs, curl_blocks, block_cols, hole_mask, edge_flip, send_list, send_count, recv_list, dtn_blocks
):
    peers = send_list.shape[2]
    f32, bf16 = jnp.float32, jnp.bfloat16
    tiles = BS * BS // LANES
    cols = block_cols.T
    in_hbm = functools.partial(pltpu.with_memory_space_constraint, memory_space=pltpu.HBM)
    sends, counts, targets = send_list[0, 0], send_count[0, 0], recv_list[0, 0]
    flips = edge_flip.reshape(NB * BS // LANES, LANES)
    curl_rows = curl_blocks.reshape(NB, K, tiles, LANES).transpose(0, 2, 1, 3)
    curl_rows = curl_rows.reshape(NB, tiles * K, LANES)
    dtn_rows = dtn_blocks[0, 0].reshape(peers, F, tiles, LANES).transpose(0, 2, 1, 3)
    dtn_rows = dtn_rows.reshape(peers, tiles * F, LANES)

    block_shape = (NB, COLS, PAD)
    face = shape((F, COLS, PAD), bf16)
    ends = shape((NI, COLS, PAD), bf16)
    state, sign, *sent = pl.pallas_call(
        functools.partial(prep_kernel, peers),
        out_shape=(shape(block_shape, bf16), shape((QUAD, NB // QUAD, LANES), f32)) + (face,) * peers,
        in_specs=[HBM] * 5,
        out_specs=[VMEM] * (2 + peers),
        scratch_shapes=[
            pltpu.SMEM(sends.shape, jnp.int32),
            pltpu.SMEM(counts.shape, jnp.int32),
            pltpu.SMEM(hole_mask.shape, jnp.int32),
            pltpu.VMEM(flips.shape, jnp.int32),
            pltpu.VMEM(rhs.shape, bf16),
            pltpu.SemaphoreType.DMA((5,)),
        ],
        compiler_params=params(),
        cost_estimate=cost(10**6, 10**6),
    )(*map(in_hbm, (sends, counts, hole_mask, flips, rhs)))

    matrices, faces = pl.pallas_call(
        functools.partial(spread_kernel, peers),
        out_shape=(shape((NB, K // 2, BS, 2 * PAD), bf16), shape((peers, F // 2, BS, 2 * PAD), bf16)),
        in_specs=[HBM] * 2,
        out_specs=[VMEM] * 2,
        scratch_shapes=[
            pltpu.VMEM(curl_rows.shape, bf16),
            pltpu.VMEM(dtn_rows.shape, bf16),
            pltpu.VMEM((max(STAGES) * K, BS, LANES), bf16),
            pltpu.VMEM((max(STAGES) * K, BS, LANES), bf16),
            pltpu.SemaphoreType.DMA((NB // PIECE + 1,)),
        ],
        compiler_params=params(),
        cost_estimate=cost(4 * 10**9, 16 * 10**6),
    )(in_hbm(curl_rows), in_hbm(dtn_rows))

    def exchange(sent):
        pairs = [[(p, p ^ i) for p in range(peers)] for i in range(peers)]
        arrived = {i: lax.ppermute(sent[i], "patch", pairs[i]) for i in reversed(range(1, peers))}
        return [sent[0]] + [arrived[i] for i in range(1, peers)]

    received = exchange(sent)
    begin = state
    state, swap_in, swap_out, *sent = pl.pallas_call(
        functools.partial(first_tick_kernel, peers),
        out_shape=(shape(block_shape, bf16), ends, ends) + (face,) * peers,
        in_specs=[SMEM] * 5 + [VMEM] * (5 + peers),
        out_specs=[VMEM] * (3 + peers),
        scratch_shapes=[pltpu.VMEM(block_shape, f32), pltpu.VMEM(block_shape, bf16)],
        compiler_params=params(),
        cost_estimate=cost(10**10, 16 * 10**6),
    )(cols, hole_mask, targets, sends, counts, sign, matrices, faces, begin, begin, *received)

    received = exchange(sent)
    swap_in = swapped(swap_in, "sec", 0)
    swap_out = swapped(swap_out, "sec", 1)
    image = pl.pallas_call(
        first_image_kernel,
        out_shape=shape(block_shape, f32),
        in_specs=[SMEM] + [VMEM] * 2,
        out_specs=VMEM,
        compiler_params=params(),
        cost_estimate=cost(10**9, 8 * 10**6),
    )(cols, matrices, state)
    return pl.pallas_call(
        functools.partial(last_tick_kernel, peers),
        out_shape=shape((COLS, NB * BS), f32),
        in_specs=[SMEM] * 3 + [VMEM] * (6 + peers),
        out_specs=VMEM,
        scratch_shapes=[
            pltpu.VMEM(block_shape, f32),
            pltpu.VMEM(block_shape, bf16),
            pltpu.VMEM(block_shape, bf16),
            pltpu.VMEM(block_shape, f32),
        ],
        compiler_params=params(),
        cost_estimate=cost(10**10, 16 * 10**6),
    )(cols, hole_mask, targets, matrices, faces, begin, image, swap_in, swap_out, *received)


def solution(mesh):
    in_specs = (
        P(None, ("sec", "patch")),
        P(("sec", "patch"), None, None),
        P(("sec", "patch"), None),
        P(("sec", "patch")),
        P(("sec", "patch")),
        P("sec", "patch", None, None),
        P("sec", "patch", None),
        P("sec", "patch", None, None),
        P("sec", "patch", None, None, None),
    )
    out_specs = P(None, ("sec", "patch"))
    return jax.shard_map(shards, mesh=mesh, in_specs=in_specs, out_specs=out_specs, check_vma=False)
```

```python
import functools

import jax
import jax.numpy as jnp
from jax import lax
from jax.experimental import pallas as pl
from jax.experimental.pallas import tpu as pltpu
from jax.sharding import PartitionSpec as P

BS = 96
COLS = 24
NB = 64
K = 4
F = 8
NI = 8
ITERS = 8
TICKS = 2
COUPLING = 0.85

LANES = 128
PAD = 128
QUAD = 4
TILES = 3
VMEM_LIMIT = 30 * 2**20
STAGES = (16, 16, 16, 16)
PIECE = 8
CHUNK = 32

VMEM = pl.BlockSpec(memory_space=pltpu.VMEM)
SMEM = pl.BlockSpec(memory_space=pltpu.SMEM)
HBM = pl.BlockSpec(memory_space=pltpu.HBM)


def params():
    return pltpu.CompilerParams(vmem_limit_bytes=VMEM_LIMIT)


def cost(flops, size):
    return pl.CostEstimate(flops=flops, bytes_accessed=size, transcendentals=0)


def iota(shape, axis):
    return lax.broadcasted_iota(jnp.int32, shape, axis)


def split_quad(tiles):
    first, second, third = tiles
    lane = iota(first.shape, 1)
    parts = (
        first,
        jnp.where(lane < 64, second, first),
        jnp.where(lane < 64, third, second),
        third,
    )
    keep = lane < BS
    return [
        jnp.where(keep, pltpu.roll(part, 32 * j, 1) if j else part, 0.0)
        for j, part in enumerate(parts)
    ]


def join_quad(blocks):
    lane = iota(blocks[0].shape, 1)
    parts = [
        pltpu.roll(block, LANES - 32 * j, 1) if j else block for j, block in enumerate(blocks)
    ]
    return [
        jnp.where(lane < 96, parts[0], parts[1]),
        jnp.where(lane < 64, parts[1], parts[2]),
        jnp.where(lane < 32, parts[2], parts[3]),
    ]


def arrivals(peers):
    return [peers - 1] + list(range(1, peers - 1)) + [0]


def write_sent(peers, send_ref, count_ref, sign_ref, state_ref, sent_refs):
    me = lax.axis_index("patch")
    for i in range(peers):
        q = me ^ i
        for f in range(F):
            block = send_ref[q, f]
            scale = jnp.where(f < count_ref[q], 1.0, 0.0).astype(jnp.float32)
            sign = sign_ref[lax.rem(block, QUAD), pl.ds(lax.div(block, QUAD), 1), :] * scale
            picked = state_ref[block].astype(jnp.float32) * sign
            sent_refs[i][f] = picked.astype(jnp.bfloat16)


def copies(sources, targets, sems):
    started = [
        pltpu.make_async_copy(source, target, sems.at[i])
        for i, (source, target) in enumerate(zip(sources, targets))
    ]
    for one in started:
        one.start()
    return started


def prep_kernel(peers, *refs):
    sources = refs[:5]
    state_ref, sign_ref = refs[5:7]
    sent_refs = refs[7 : 7 + peers]
    held, sems = refs[7 + peers : -1], refs[-1]
    send_ref, count_ref, hole_ref, flip_ref, rhs_ref = held
    for one in copies(sources, held, sems):
        one.wait()
    quads = NB // QUAD
    flips = [
        1.0 - 2.0 * flip_ref[pl.ds(u, quads, stride=TILES), :].astype(jnp.float32)
        for u in range(TILES)
    ]
    for j, sign in enumerate(split_quad(flips)):
        sign_ref[j] = sign
    for q in range(quads):
        at = q * TILES * LANES
        tiles = [
            rhs_ref[:, at + u * LANES : at + (u + 1) * LANES].astype(jnp.float32)
            for u in range(TILES)
        ]
        for j, block in enumerate(split_quad(tiles)):
            n = q * QUAD + j
            keep = hole_ref[n].astype(jnp.float32)
            state_ref[n] = (keep * block).astype(jnp.bfloat16)
    write_sent(peers, send_ref, count_ref, sign_ref, state_ref, sent_refs)


def picker(group):
    depth = 8 * TILES * group
    row = iota((32 * group, 2 * depth), 0)
    at = iota((32 * group, 2 * depth), 1)
    member, e = row // 32, row % 32
    r, j = e // QUAD, e % QUAD
    low = jnp.where(j == 0, 0, jnp.where(j == 1, 1, 2))
    high = jnp.where(j < 2, 0, j - 1)
    want_low = (r * TILES + low) * group + member
    want_high = (r * TILES + high) * group + member + depth
    return ((at == want_low) | (at == want_high)).astype(jnp.float32).astype(jnp.bfloat16)


def stack(select, rows, group):
    depth = 8 * TILES * group
    wide = jnp.concatenate([rows[g * depth : (g + 1) * depth] for g in range(3)], axis=1)
    high = iota(wide.shape, 1) % LANES >= 64
    zero = jnp.zeros_like(wide)
    both = jnp.concatenate([jnp.where(high, zero, wide), jnp.where(high, wide, zero)], axis=0)
    return jnp.dot(select, both, preferred_element_type=jnp.float32).astype(jnp.bfloat16)


def unstack(picked, member):
    mine = picked[32 * member : 32 * (member + 1)]
    return jnp.concatenate([mine[:, g * LANES : (g + 1) * LANES] for g in range(3)], axis=0)


def turn(square):
    pad = jnp.zeros((PAD - BS, LANES), jnp.bfloat16)
    turned = jnp.concatenate([square, pad], axis=0).T
    bands = [turned[32 * a : 32 * (a + 1)] for a in range(4)]
    lane = iota((32, LANES), 1)
    for bit in (1, 2):
        odd = lane & bit == bit
        bands = [jnp.where(odd, bands[(a - bit) % 4], bands[a]) for a in range(4)]
    return jnp.concatenate(bands[: BS // 32], axis=0)


def spread_kernel(
    peers, curl_hbm, dtn_hbm, matrix_ref, face_ref, curl_ref, dtn_ref, even_ref, odd_ref, sems
):
    pieces = NB // PIECE
    started = copies(
        [curl_hbm.at[pl.ds(i * PIECE, PIECE)] for i in range(pieces)] + [dtn_hbm],
        [curl_ref.at[pl.ds(i * PIECE, PIECE)] for i in range(pieces)] + [dtn_ref],
        sems,
    )
    select, select_faces = picker(K), picker(F)
    tasks, done = [], 0
    for size in STAGES:
        waits = [started[i] for i in range(-(-done // PIECE), -(-(done + size) // PIECE))]
        tasks.append((waits, [(select, curl_ref, done + step, K) for step in range(size)]))
        done += size
    quarter = max(STAGES) * K // F
    for first in range(0, peers, quarter):
        waits = [started[pieces]] if first == 0 else []
        members = range(first, min(first + quarter, peers))
        faces = [(select_faces, dtn_ref, q, F) for q in members]
        tasks.append((waits, faces))

    def gather(task):
        waits, items = task
        for one in waits:
            one.wait()
        return [(rows, n, size, stack(pick, rows[n], size)) for pick, rows, n, size in items]

    def store(results, held_ref):
        for at, (_, _, size, picked) in enumerate(results):
            for member in range(size):
                held_ref[at * size + member] = unstack(picked, member)

    def finish(results, held_ref):
        for at, (rows, n, size, _) in enumerate(results):
            for member in range(size):
                half, side = member // 2, slice(member % 2 * PAD, (member % 2 + 1) * PAD)
                block = turn(held_ref[at * size + member])
                if rows is curl_ref:
                    matrix_ref[n, half, :, side] = block
                else:
                    face_ref[n, half, :, side] = block

    held = (even_ref, odd_ref)
    results = gather(tasks[0])
    store(results, held[0])
    for i in range(len(tasks)):
        upcoming = gather(tasks[i + 1]) if i + 1 < len(tasks) else []
        finish(results, held[i % 2])
        store(upcoming, held[(i + 1) % 2])
        results = upcoming


def paired(left, right, matrices):
    both = jnp.concatenate([left, right], axis=0)[:, :BS]
    wide = jnp.dot(both, matrices, preferred_element_type=jnp.float32)
    return wide[:COLS, :PAD], wide[COLS:, PAD:]


def add_faces(peers, target_ref, hole_ref, received_refs, face_ref, forcing_ref):
    me = lax.axis_index("patch")
    products = []
    for i, received_ref in zip(arrivals(peers), received_refs):
        q = me ^ i
        for f in range(0, F, 2):
            pair = paired(received_ref[f], received_ref[f + 1], face_ref[q, f // 2])
            for step, product in enumerate(pair):
                products.append((q, f + step, product.astype(jnp.bfloat16).astype(jnp.float32)))
    for q, f, product in products:
        n = target_ref[q, f]
        forcing_ref[n] = forcing_ref[n] + hole_ref[n].astype(jnp.float32) * product


def image_of(cols_ref, matrix_ref, old_ref, n):
    total = None
    for half in range(K // 2):
        nearby = [old_ref[cols_ref[2 * half + side, n]] for side in range(2)]
        left, right = paired(nearby[0], nearby[1], matrix_ref[n, half])
        total = left + right if total is None else total + (left + right)
    return total


def sweep(cols_ref, hole_ref, matrix_ref, forcing_ref, old_ref, new_ref):
    for first in range(0, NB, CHUNK):
        chunk = range(first, first + CHUNK)
        images = [image_of(cols_ref, matrix_ref, old_ref, n) for n in chunk]
        for n, image in zip(chunk, images):
            scale = COUPLING * hole_ref[n].astype(jnp.float32)
            new_ref[n] = (forcing_ref[n] - scale * image).astype(new_ref.dtype)


def first_tick_kernel(peers, *refs):
    cols_ref, hole_ref, target_ref, send_ref, count_ref = refs[:5]
    sign_ref, matrix_ref, face_ref, begin_ref, start_ref = refs[5:10]
    received_refs = refs[10 : 10 + peers]
    state_ref, swap_in_ref, swap_out_ref = refs[10 + peers : 13 + peers]
    sent_refs = refs[13 + peers : 13 + 2 * peers]
    forcing_ref, other_ref = refs[13 + 2 * peers :]
    forcing_ref[...] = begin_ref[...].astype(jnp.float32)
    add_faces(peers, target_ref, hole_ref, received_refs, face_ref, forcing_ref)
    state_ref[...] = start_ref[...]

    def two(i, carry):
        sweep(cols_ref, hole_ref, matrix_ref, forcing_ref, state_ref, other_ref)
        sweep(cols_ref, hole_ref, matrix_ref, forcing_ref, other_ref, state_ref)
        return carry

    lax.fori_loop(0, ITERS // 2, two, 0)
    low, high = state_ref[:NI], state_ref[NB - NI :]
    even = lax.rem(lax.axis_index("sec"), 2) == 0
    swap_in_ref[...] = jnp.where(even, high, low)
    swap_out_ref[...] = jnp.where(even, low, high)
    write_sent(peers, send_ref, count_ref, sign_ref, state_ref, sent_refs)


def first_image_kernel(cols_ref, matrix_ref, state_ref, image_ref):
    for n in range(NB):
        image_ref[n] = image_of(cols_ref, matrix_ref, state_ref, n)


def last_tick_kernel(peers, *refs):
    cols_ref, hole_ref, target_ref, matrix_ref, face_ref, begin_ref, image_ref = refs[:7]
    received_refs = refs[7 : 7 + peers]
    swap_in_ref, swap_out_ref = refs[7 + peers : 9 + peers]
    out_ref, forcing_ref, state_ref, other_ref, final_ref = refs[9 + peers :]
    forcing_ref[...] = begin_ref[...].astype(jnp.float32)
    even = lax.rem(lax.axis_index("sec"), 2) == 0
    for n in range(NI):
        inner, outer = swap_in_ref[n], swap_out_ref[n]
        from_left = jnp.where(even, outer, inner)
        from_right = jnp.where(even, inner, outer)
        for block, arrived in ((n, from_left), (NB - NI + n, from_right)):
            keep = hole_ref[block].astype(jnp.float32)
            forcing_ref[block] = forcing_ref[block] + keep * arrived.astype(jnp.float32)
    add_faces(peers, target_ref, hole_ref, received_refs, face_ref, forcing_ref)
    for n in range(NB):
        scale = COUPLING * hole_ref[n].astype(jnp.float32)
        state_ref[n] = (forcing_ref[n] - scale * image_ref[n]).astype(jnp.bfloat16)

    def two(i, carry):
        sweep(cols_ref, hole_ref, matrix_ref, forcing_ref, state_ref, other_ref)
        sweep(cols_ref, hole_ref, matrix_ref, forcing_ref, other_ref, state_ref)
        return carry

    lax.fori_loop(0, ITERS // 2 - 1, two, 0)
    sweep(cols_ref, hole_ref, matrix_ref, forcing_ref, state_ref, final_ref)
    for q in range(NB // QUAD):
        tiles = join_quad([final_ref[q * QUAD + j] for j in range(QUAD)])
        for u, tile in enumerate(tiles):
            at = (q * TILES + u) * LANES
            out_ref[:, at : at + LANES] = tile


def swapped(x, axis, first):
    size = lax.axis_size(axis)
    pairs = []
    for i in range(first, size - 1, 2):
        pairs += [(i, i + 1), (i + 1, i)]
    return lax.ppermute(x, axis, pairs)


def shape(dims, dtype):
    return jax.ShapeDtypeStruct(dims, dtype)


def shards(
    rhs, curl_blocks, block_cols, hole_mask, edge_flip, send_list, send_count, recv_list, dtn_blocks
):
    peers = send_list.shape[2]
    f32, bf16 = jnp.float32, jnp.bfloat16
    tiles = BS * BS // LANES
    cols = block_cols.T
    in_hbm = functools.partial(pltpu.with_memory_space_constraint, memory_space=pltpu.HBM)
    sends, counts, targets = send_list[0, 0], send_count[0, 0], recv_list[0, 0]
    flips = edge_flip.reshape(NB * BS // LANES, LANES)
    curl_rows = curl_blocks.reshape(NB, K, tiles, LANES).transpose(0, 2, 1, 3)
    curl_rows = curl_rows.reshape(NB, tiles * K, LANES)
    dtn_rows = dtn_blocks[0, 0].reshape(peers, F, tiles, LANES).transpose(0, 2, 1, 3)
    dtn_rows = dtn_rows.reshape(peers, tiles * F, LANES)

    block_shape = (NB, COLS, PAD)
    face = shape((F, COLS, PAD), bf16)
    ends = shape((NI, COLS, PAD), bf16)
    state, sign, *sent = pl.pallas_call(
        functools.partial(prep_kernel, peers),
        out_shape=(shape(block_shape, bf16), shape((QUAD, NB // QUAD, LANES), f32)) + (face,) * peers,
        in_specs=[HBM] * 5,
        out_specs=[VMEM] * (2 + peers),
        scratch_shapes=[
            pltpu.SMEM(sends.shape, jnp.int32),
            pltpu.SMEM(counts.shape, jnp.int32),
            pltpu.SMEM(hole_mask.shape, jnp.int32),
            pltpu.VMEM(flips.shape, jnp.int32),
            pltpu.VMEM(rhs.shape, bf16),
            pltpu.SemaphoreType.DMA((5,)),
        ],
        compiler_params=params(),
        cost_estimate=cost(10**6, 10**6),
    )(*map(in_hbm, (sends, counts, hole_mask, flips, rhs)))

    matrices, faces = pl.pallas_call(
        functools.partial(spread_kernel, peers),
        out_shape=(shape((NB, K // 2, BS, 2 * PAD), bf16), shape((peers, F // 2, BS, 2 * PAD), bf16)),
        in_specs=[HBM] * 2,
        out_specs=[VMEM] * 2,
        scratch_shapes=[
            pltpu.VMEM(curl_rows.shape, bf16),
            pltpu.VMEM(dtn_rows.shape, bf16),
            pltpu.VMEM((max(STAGES) * K, BS, LANES), bf16),
            pltpu.VMEM((max(STAGES) * K, BS, LANES), bf16),
            pltpu.SemaphoreType.DMA((NB // PIECE + 1,)),
        ],
        compiler_params=params(),
        cost_estimate=cost(4 * 10**9, 16 * 10**6),
    )(in_hbm(curl_rows), in_hbm(dtn_rows))

    def exchange(sent):
        pairs = [[(p, p ^ i) for p in range(peers)] for i in range(peers)]
        return [lax.ppermute(sent[i], "patch", pairs[i]) if i else sent[0] for i in arrivals(peers)]

    received = exchange(sent)
    begin = state
    state, swap_in, swap_out, *sent = pl.pallas_call(
        functools.partial(first_tick_kernel, peers),
        out_shape=(shape(block_shape, bf16), ends, ends) + (face,) * peers,
        in_specs=[SMEM] * 5 + [VMEM] * (5 + peers),
        out_specs=[VMEM] * (3 + peers),
        scratch_shapes=[pltpu.VMEM(block_shape, f32), pltpu.VMEM(block_shape, bf16)],
        compiler_params=params(),
        cost_estimate=cost(10**10, 16 * 10**6),
    )(cols, hole_mask, targets, sends, counts, sign, matrices, faces, begin, begin, *received)

    received = exchange(sent)
    swap_in = swapped(swap_in, "sec", 0)
    swap_out = swapped(swap_out, "sec", 1)
    image = pl.pallas_call(
        first_image_kernel,
        out_shape=shape(block_shape, f32),
        in_specs=[SMEM] + [VMEM] * 2,
        out_specs=VMEM,
        compiler_params=params(),
        cost_estimate=cost(10**9, 8 * 10**6),
    )(cols, matrices, state)
    return pl.pallas_call(
        functools.partial(last_tick_kernel, peers),
        out_shape=shape((COLS, NB * BS), f32),
        in_specs=[SMEM] * 3 + [VMEM] * (6 + peers),
        out_specs=VMEM,
        scratch_shapes=[
            pltpu.VMEM(block_shape, f32),
            pltpu.VMEM(block_shape, bf16),
            pltpu.VMEM(block_shape, bf16),
            pltpu.VMEM(block_shape, f32),
        ],
        compiler_params=params(),
        cost_estimate=cost(10**10, 16 * 10**6),
    )(cols, hole_mask, targets, matrices, faces, begin, image, *received, swap_in, swap_out)


def solution(mesh):
    in_specs = (
        P(None, ("sec", "patch")),
        P(("sec", "patch"), None, None),
        P(("sec", "patch"), None),
        P(("sec", "patch")),
        P(("sec", "patch")),
        P("sec", "patch", None, None),
        P("sec", "patch", None),
        P("sec", "patch", None, None),
        P("sec", "patch", None, None, None),
    )
    out_specs = P(None, ("sec", "patch"))
    return jax.shard_map(shards, mesh=mesh, in_specs=in_specs, out_specs=out_specs, check_vma=False)
```

```python
import functools

import jax
import jax.numpy as jnp
from jax import lax
from jax.experimental import pallas as pl
from jax.experimental.pallas import tpu as pltpu
from jax.sharding import PartitionSpec as P

BS = 96
COLS = 24
NB = 64
K = 4
F = 8
NI = 8
ITERS = 8
TICKS = 2
COUPLING = 0.85

LANES = 128
PAD = 128
QUAD = 4
TILES = 3
VMEM_LIMIT = 30 * 2**20
STAGES = (16, 16, 16, 16)
PIECE = 8
CHUNK = 4

VMEM = pl.BlockSpec(memory_space=pltpu.VMEM)
SMEM = pl.BlockSpec(memory_space=pltpu.SMEM)
HBM = pl.BlockSpec(memory_space=pltpu.HBM)


def params():
    return pltpu.CompilerParams(vmem_limit_bytes=VMEM_LIMIT)


def cost(flops, size):
    return pl.CostEstimate(flops=flops, bytes_accessed=size, transcendentals=0)


def iota(shape, axis):
    return lax.broadcasted_iota(jnp.int32, shape, axis)


def segments(tiles):
    first, second, third = tiles
    lane = iota(first.shape, 1)
    low = lane < 64
    return first, jnp.where(low, second, first), jnp.where(low, third, second), third


def turned_by(x, lanes):
    return pltpu.roll(x, lanes % LANES, 1) if lanes % LANES else x


def split_quad(tiles):
    return [turned_by(part, 32 * j) for j, part in enumerate(segments(tiles))]


def shift_quad(tiles):
    return [turned_by(part, 32 * j + BS) for j, part in enumerate(segments(tiles))]


def join_quad(blocks):
    lane = iota(blocks[0].shape, 1)
    parts = [turned_by(block, LANES - 32 * j) for j, block in enumerate(blocks)]
    return [
        jnp.where(lane < 96, parts[0], parts[1]),
        jnp.where(lane < 64, parts[1], parts[2]),
        jnp.where(lane < 32, parts[2], parts[3]),
    ]


def store_quad(state_ref, q, tiles):
    near, far = split_quad(tiles), shift_quad(tiles)
    for j in range(QUAD):
        state_ref[0, q * QUAD + j] = near[j].astype(jnp.bfloat16)
        state_ref[1, q * QUAD + j] = far[j].astype(jnp.bfloat16)


def tall(row_tile):
    return jnp.concatenate([row_tile] * (COLS // 8), axis=0)


def arrivals(peers):
    return [peers - 1] + list(range(1, peers - 1)) + [0]


def write_sent(peers, send_ref, count_ref, sign_ref, state_ref, sent_refs):
    me = lax.axis_index("patch")
    for i in range(peers):
        q = me ^ i
        for f in range(F):
            block = send_ref[q, f]
            scale = jnp.where(f < count_ref[q], 1.0, 0.0).astype(jnp.float32)
            sign = sign_ref[lax.rem(block, QUAD), pl.ds(lax.div(block, QUAD), 1), :] * scale
            picked = state_ref[0, block].astype(jnp.float32) * sign
            sent_refs[i][f] = picked.astype(jnp.bfloat16)


def copies(sources, targets, sems):
    started = [
        pltpu.make_async_copy(source, target, sems.at[i])
        for i, (source, target) in enumerate(zip(sources, targets))
    ]
    for one in started:
        one.start()
    return started


def prep_kernel(peers, *refs):
    sources = refs[:5]
    state_ref, sign_ref, source_ref, scale_ref = refs[5:9]
    sent_refs = refs[9 : 9 + peers]
    held, sems = refs[9 + peers : -1], refs[-1]
    send_ref, count_ref, hole_ref, flip_ref, rhs_ref = held
    for one in copies(sources, held, sems):
        one.wait()
    quads = NB // QUAD
    flips = [
        1.0 - 2.0 * flip_ref[pl.ds(u, quads, stride=TILES), :].astype(jnp.float32)
        for u in range(TILES)
    ]
    for j, sign in enumerate(split_quad(flips)):
        sign_ref[j] = sign
    lane = iota((8, LANES), 1)
    for q in range(quads):
        keeps = [hole_ref[q * QUAD + j].astype(jnp.float32) for j in range(QUAD)]
        tiles = []
        for u in range(TILES):
            at = (q * TILES + u) * LANES
            keep = jnp.where(lane < BS - 32 * u, keeps[u], keeps[u + 1])
            scale_ref[q * TILES + u] = COUPLING * keep
            tile = tall(keep) * rhs_ref[:, at : at + LANES].astype(jnp.float32)
            source_ref[q * TILES + u] = tile.astype(jnp.bfloat16)
            tiles.append(tile)
        store_quad(state_ref, q, tiles)
    write_sent(peers, send_ref, count_ref, sign_ref, state_ref, sent_refs)


def picker(group):
    depth = 8 * TILES * group
    row = iota((32 * group, 2 * depth), 0)
    at = iota((32 * group, 2 * depth), 1)
    member, e = row // 32, row % 32
    r, j = e // QUAD, e % QUAD
    low = jnp.where(j == 0, 0, jnp.where(j == 1, 1, 2))
    high = jnp.where(j < 2, 0, j - 1)
    want_low = (r * TILES + low) * group + member
    want_high = (r * TILES + high) * group + member + depth
    return ((at == want_low) | (at == want_high)).astype(jnp.float32).astype(jnp.bfloat16)


def stack(select, rows, group):
    depth = 8 * TILES * group
    wide = jnp.concatenate([rows[g * depth : (g + 1) * depth] for g in range(3)], axis=1)
    high = iota(wide.shape, 1) % LANES >= 64
    zero = jnp.zeros_like(wide)
    both = jnp.concatenate([jnp.where(high, zero, wide), jnp.where(high, wide, zero)], axis=0)
    return jnp.dot(select, both, preferred_element_type=jnp.float32).astype(jnp.bfloat16)


def unstack(picked, member):
    mine = picked[32 * member : 32 * (member + 1)]
    return jnp.concatenate([mine[:, g * LANES : (g + 1) * LANES] for g in range(3)], axis=0)


def turn(square):
    turned = square.T
    bands = [turned[32 * a : 32 * (a + 1)] for a in range(4)]
    lane = iota((32, LANES), 1)
    for bit in (1, 2):
        odd = lane & bit == bit
        bands = [jnp.where(odd, bands[(a - bit) % 4], bands[a]) for a in range(4)]
    return jnp.concatenate(bands[: BS // 32], axis=0)


def spread_kernel(
    peers, curl_hbm, dtn_hbm, matrix_ref, face_ref, curl_ref, dtn_ref, even_ref, odd_ref, sems
):
    pieces = NB // PIECE
    started = copies(
        [curl_hbm.at[pl.ds(i * PIECE, PIECE)] for i in range(pieces)] + [dtn_hbm],
        [curl_ref.at[pl.ds(i * PIECE, PIECE)] for i in range(pieces)] + [dtn_ref],
        sems,
    )
    select, select_faces = picker(K), picker(F)
    tasks, done = [], 0
    for size in STAGES:
        waits = [started[i] for i in range(-(-done // PIECE), -(-(done + size) // PIECE))]
        tasks.append((waits, [(select, curl_ref, done + step, K) for step in range(size)]))
        done += size
    quarter = max(STAGES) * K // F
    for first in range(0, peers, quarter):
        waits = [started[pieces]] if first == 0 else []
        members = range(first, min(first + quarter, peers))
        faces = [(select_faces, dtn_ref, q, F) for q in members]
        tasks.append((waits, faces))

    def gather(task):
        waits, items = task
        for one in waits:
            one.wait()
        return [(rows, n, size, stack(pick, rows[n], size)) for pick, rows, n, size in items]

    def store(results, held_ref):
        for at, (rows, _, size, picked) in enumerate(results):
            for member in range(size):
                square = unstack(picked, member)
                if rows is curl_ref:
                    slot, place = at // QUAD * K + member, at % QUAD
                else:
                    slot, place = (at * size + member) // QUAD, member % QUAD
                held_ref[slot, place * BS : (place + 1) * BS] = square

    def finish(results, held_ref):
        for at, (rows, n, size, _) in enumerate(results):
            if rows is dtn_ref:
                for member in range(size):
                    half, side = member // 2, slice(member % 2 * PAD, (member % 2 + 1) * PAD)
                    slot, place = (at * size + member) // QUAD, member % QUAD
                    pad = jnp.zeros((PAD - BS, LANES), jnp.bfloat16)
                    square = held_ref[slot, place * BS : (place + 1) * BS]
                    face_ref[n, half, :, side] = turn(jnp.concatenate([square, pad], axis=0))
            elif at % QUAD == 0:
                q = n // QUAD
                for k in range(K):
                    depth = slice(k % 2 * BS, (k % 2 + 1) * BS)
                    for u in range(TILES):
                        left = (q % 2 * TILES + u) * LANES
                        square = held_ref[at // QUAD * K + k, u * LANES : (u + 1) * LANES]
                        matrix_ref[q // 2, k // 2, depth, left : left + LANES] = turn(square)

    held = (even_ref, odd_ref)
    results = gather(tasks[0])
    store(results, held[0])
    for i in range(len(tasks)):
        upcoming = gather(tasks[i + 1]) if i + 1 < len(tasks) else []
        finish(results, held[i % 2])
        store(upcoming, held[(i + 1) % 2])
        results = upcoming


def paired(left, right, matrices):
    both = jnp.concatenate([left, right], axis=0)[:, :BS]
    wide = jnp.dot(both, matrices, preferred_element_type=jnp.float32)
    return wide[:COLS, :PAD], wide[COLS:, PAD:]


def add_faces(peers, target_ref, received_refs, face_ref, extra_ref):
    me = lax.axis_index("patch")
    products = []
    for i, received_ref in zip(arrivals(peers), received_refs):
        q = me ^ i
        for f in range(0, F, 2):
            pair = paired(received_ref[f], received_ref[f + 1], face_ref[q, f // 2])
            for step, product in enumerate(pair):
                products.append((q, f + step, product.astype(jnp.bfloat16).astype(jnp.float32)))
    for q, f, product in products:
        n = target_ref[q, f]
        extra_ref[n] = extra_ref[n] + product


def set_forcing(source_ref, scale_ref, extra_ref, forcing_ref):
    for q in range(NB // QUAD):
        tiles = join_quad([extra_ref[q * QUAD + j] for j in range(QUAD)])
        for u, tile in enumerate(tiles):
            at = q * TILES + u
            kept = jnp.where(tall(scale_ref[at]) > 0, tile, 0.0)
            forcing_ref[at] = source_ref[at].astype(jnp.float32) + kept


def images_of(cols_ref, matrix_ref, old_ref, group):
    lane = iota((COLS, LANES), 1)

    def nearby(n, half):
        near = old_ref[0, cols_ref[2 * half, n]]
        far = old_ref[1, cols_ref[2 * half + 1, n]]
        return jnp.concatenate([jnp.where(lane < BS, near, far), far], axis=1)

    totals = [None] * (2 * TILES)
    for third, rows in enumerate(((0, 1, 2), (2, 3, 4, 5), (5, 6, 7))):
        columns = slice(third * 2 * LANES, (third + 1) * 2 * LANES)
        for half in range(K // 2):
            left = jnp.concatenate([nearby(group * 2 * QUAD + j, half) for j in rows], axis=0)
            wide = jnp.dot(
                left[:, : 2 * BS], matrix_ref[group, half, :, columns],
                preferred_element_type=jnp.float32,
            )
            for side in range(2):
                tile = third * 2 + side
                first = tile * LANES // BS
                cut = (first + 1) * BS - tile * LANES
                at = rows.index(first) * COLS
                part = wide[:, side * LANES : (side + 1) * LANES]
                picked = jnp.where(lane < cut, part[at : at + COLS], part[at + COLS : at + 2 * COLS])
                totals[tile] = picked if half == 0 else totals[tile] + picked
    return totals


def step_tile(forcing_ref, scale_ref, image, at):
    return forcing_ref[at] - tall(scale_ref[at]) * image


def sweep(cols_ref, scale_ref, matrix_ref, forcing_ref, old_ref, new_ref):
    groups = NB // (2 * QUAD)
    for first in range(0, groups, CHUNK):
        chunk = range(first, first + CHUNK)
        images = [images_of(cols_ref, matrix_ref, old_ref, group) for group in chunk]
        for group, parts in zip(chunk, images):
            tiles = [
                step_tile(forcing_ref, scale_ref, part, group * 2 * TILES + i)
                for i, part in enumerate(parts)
            ]
            for side in range(2):
                store_quad(new_ref, group * 2 + side, tiles[side * TILES : (side + 1) * TILES])


def first_tick_kernel(peers, *refs):
    cols_ref, target_ref, send_ref, count_ref = refs[:4]
    sign_ref, scale_ref, matrix_ref, face_ref, source_ref, start_ref = refs[4:10]
    received_refs = refs[10 : 10 + peers]
    state_ref, swap_in_ref, swap_out_ref = refs[10 + peers : 13 + peers]
    sent_refs = refs[13 + peers : 13 + 2 * peers]
    forcing_ref, extra_ref, other_ref = refs[13 + 2 * peers :]
    extra_ref[...] = jnp.zeros_like(extra_ref)
    add_faces(peers, target_ref, received_refs, face_ref, extra_ref)
    set_forcing(source_ref, scale_ref, extra_ref, forcing_ref)
    state_ref[...] = start_ref[...]

    def two(i, carry):
        sweep(cols_ref, scale_ref, matrix_ref, forcing_ref, state_ref, other_ref)
        sweep(cols_ref, scale_ref, matrix_ref, forcing_ref, other_ref, state_ref)
        return carry

    lax.fori_loop(0, ITERS // 2, two, 0)
    low, high = state_ref[0, :NI], state_ref[0, NB - NI :]
    even = lax.rem(lax.axis_index("sec"), 2) == 0
    swap_in_ref[...] = jnp.where(even, high, low)
    swap_out_ref[...] = jnp.where(even, low, high)
    write_sent(peers, send_ref, count_ref, sign_ref, state_ref, sent_refs)


def first_image_kernel(cols_ref, matrix_ref, state_ref, image_ref):
    for group in range(NB // (2 * QUAD)):
        for i, part in enumerate(images_of(cols_ref, matrix_ref, state_ref, group)):
            image_ref[group * 2 * TILES + i] = part


def last_tick_kernel(peers, *refs):
    cols_ref, target_ref, scale_ref, matrix_ref, face_ref, source_ref, image_ref = refs[:7]
    received_refs = refs[7 : 7 + peers]
    swap_in_ref, swap_out_ref = refs[7 + peers : 9 + peers]
    out_ref, forcing_ref, extra_ref, state_ref, other_ref = refs[9 + peers :]
    even = lax.rem(lax.axis_index("sec"), 2) == 0
    extra_ref[NI : NB - NI] = jnp.zeros((NB - 2 * NI, COLS, PAD), jnp.float32)
    inner = swap_in_ref[...].astype(jnp.float32)
    outer = swap_out_ref[...].astype(jnp.float32)
    extra_ref[:NI] = jnp.where(even, outer, inner)
    extra_ref[NB - NI :] = jnp.where(even, inner, outer)
    add_faces(peers, target_ref, received_refs, face_ref, extra_ref)
    set_forcing(source_ref, scale_ref, extra_ref, forcing_ref)
    for q in range(NB // QUAD):
        tiles = range(q * TILES, (q + 1) * TILES)
        store_quad(state_ref, q, [step_tile(forcing_ref, scale_ref, image_ref[i], i) for i in tiles])

    def two(i, carry):
        sweep(cols_ref, scale_ref, matrix_ref, forcing_ref, state_ref, other_ref)
        sweep(cols_ref, scale_ref, matrix_ref, forcing_ref, other_ref, state_ref)
        return carry

    lax.fori_loop(0, ITERS // 2 - 1, two, 0)
    for group in range(NB // (2 * QUAD)):
        for i, part in enumerate(images_of(cols_ref, matrix_ref, state_ref, group)):
            at = group * 2 * TILES + i
            out_ref[:, at * LANES : (at + 1) * LANES] = step_tile(forcing_ref, scale_ref, part, at)


def swapped(x, axis, first):
    size = lax.axis_size(axis)
    pairs = []
    for i in range(first, size - 1, 2):
        pairs += [(i, i + 1), (i + 1, i)]
    return lax.ppermute(x, axis, pairs)


def shape(dims, dtype):
    return jax.ShapeDtypeStruct(dims, dtype)


def shards(
    rhs, curl_blocks, block_cols, hole_mask, edge_flip, send_list, send_count, recv_list, dtn_blocks
):
    peers = send_list.shape[2]
    f32, bf16 = jnp.float32, jnp.bfloat16
    tiles = BS * BS // LANES
    cols = block_cols.T
    in_hbm = functools.partial(pltpu.with_memory_space_constraint, memory_space=pltpu.HBM)
    sends, counts, targets = send_list[0, 0], send_count[0, 0], recv_list[0, 0]
    flips = edge_flip.reshape(NB * BS // LANES, LANES)
    curl_rows = curl_blocks.reshape(NB, K, tiles, LANES).transpose(0, 2, 1, 3)
    curl_rows = curl_rows.reshape(NB, tiles * K, LANES)
    dtn_rows = dtn_blocks[0, 0].reshape(peers, F, tiles, LANES).transpose(0, 2, 1, 3)
    dtn_rows = dtn_rows.reshape(peers, tiles * F, LANES)

    count = NB * BS // LANES
    block_shape = (NB, COLS, PAD)
    tile_shape = (count, COLS, LANES)
    state_shape = (2, NB, COLS, PAD)
    face = shape((F, COLS, PAD), bf16)
    ends = shape((NI, COLS, PAD), bf16)
    state, sign, source, scale, *sent = pl.pallas_call(
        functools.partial(prep_kernel, peers),
        out_shape=(
            shape(state_shape, bf16),
            shape((QUAD, NB // QUAD, LANES), f32),
            shape(tile_shape, bf16),
            shape((count, 8, LANES), f32),
        )
        + (face,) * peers,
        in_specs=[HBM] * 5,
        out_specs=[VMEM] * (4 + peers),
        scratch_shapes=[
            pltpu.SMEM(sends.shape, jnp.int32),
            pltpu.SMEM(counts.shape, jnp.int32),
            pltpu.SMEM(hole_mask.shape, jnp.int32),
            pltpu.VMEM(flips.shape, jnp.int32),
            pltpu.VMEM(rhs.shape, bf16),
            pltpu.SemaphoreType.DMA((5,)),
        ],
        compiler_params=params(),
        cost_estimate=cost(10**6, 10**6),
    )(*map(in_hbm, (sends, counts, hole_mask, flips, rhs)))

    matrices, faces = pl.pallas_call(
        functools.partial(spread_kernel, peers),
        out_shape=(
            shape((NB // (2 * QUAD), K // 2, 2 * BS, 2 * TILES * LANES), bf16),
            shape((peers, F // 2, BS, 2 * PAD), bf16),
        ),
        in_specs=[HBM] * 2,
        out_specs=[VMEM] * 2,
        scratch_shapes=[
            pltpu.VMEM(curl_rows.shape, bf16),
            pltpu.VMEM(dtn_rows.shape, bf16),
            pltpu.VMEM((max(STAGES) * K // QUAD, QUAD * BS, LANES), bf16),
            pltpu.VMEM((max(STAGES) * K // QUAD, QUAD * BS, LANES), bf16),
            pltpu.SemaphoreType.DMA((NB // PIECE + 1,)),
        ],
        compiler_params=params(),
        cost_estimate=cost(4 * 10**9, 16 * 10**6),
    )(in_hbm(curl_rows), in_hbm(dtn_rows))

    def exchange(sent):
        pairs = [[(p, p ^ i) for p in range(peers)] for i in range(peers)]
        return [lax.ppermute(sent[i], "patch", pairs[i]) if i else sent[0] for i in arrivals(peers)]

    received = exchange(sent)
    state, swap_in, swap_out, *sent = pl.pallas_call(
        functools.partial(first_tick_kernel, peers),
        out_shape=(shape(state_shape, bf16), ends, ends) + (face,) * peers,
        in_specs=[SMEM] * 4 + [VMEM] * (6 + peers),
        out_specs=[VMEM] * (3 + peers),
        scratch_shapes=[
            pltpu.VMEM(tile_shape, f32),
            pltpu.VMEM(block_shape, f32),
            pltpu.VMEM(state_shape, bf16),
        ],
        compiler_params=params(),
        cost_estimate=cost(10**10, 16 * 10**6),
    )(cols, targets, sends, counts, sign, scale, matrices, faces, source, state, *received)

    received = exchange(sent)
    swap_in = swapped(swap_in, "sec", 0)
    swap_out = swapped(swap_out, "sec", 1)
    image = pl.pallas_call(
        first_image_kernel,
        out_shape=shape(tile_shape, f32),
        in_specs=[SMEM] + [VMEM] * 2,
        out_specs=VMEM,
        compiler_params=params(),
        cost_estimate=cost(10**9, 8 * 10**6),
    )(cols, matrices, state)
    return pl.pallas_call(
        functools.partial(last_tick_kernel, peers),
        out_shape=shape((COLS, NB * BS), f32),
        in_specs=[SMEM] * 2 + [VMEM] * (7 + peers),
        out_specs=VMEM,
        scratch_shapes=[
            pltpu.VMEM(tile_shape, f32),
            pltpu.VMEM(block_shape, f32),
            pltpu.VMEM(state_shape, bf16),
            pltpu.VMEM(state_shape, bf16),
        ],
        compiler_params=params(),
        cost_estimate=cost(10**10, 16 * 10**6),
    )(cols, targets, scale, matrices, faces, source, image, *received, swap_in, swap_out)


def solution(mesh):
    in_specs = (
        P(None, ("sec", "patch")),
        P(("sec", "patch"), None, None),
        P(("sec", "patch"), None),
        P(("sec", "patch")),
        P(("sec", "patch")),
        P("sec", "patch", None, None),
        P("sec", "patch", None),
        P("sec", "patch", None, None),
        P("sec", "patch", None, None, None),
    )
    out_specs = P(None, ("sec", "patch"))
    return jax.shard_map(shards, mesh=mesh, in_specs=in_specs, out_specs=out_specs, check_vma=False)
```

```python
import functools

import jax
import jax.numpy as jnp
from jax import lax
from jax.experimental import pallas as pl
from jax.experimental.pallas import tpu as pltpu
from jax.sharding import PartitionSpec as P

BS = 96
COLS = 24
NB = 64
K = 4
F = 8
NI = 8
ITERS = 8
TICKS = 2
COUPLING = 0.85

LANES = 128
PAD = 128
QUAD = 4
TILES = 3
VMEM_LIMIT = 30 * 2**20
STAGES = (16, 16, 16, 16)
PIECE = 8
CHUNK = 4

VMEM = pl.BlockSpec(memory_space=pltpu.VMEM)
SMEM = pl.BlockSpec(memory_space=pltpu.SMEM)
HBM = pl.BlockSpec(memory_space=pltpu.HBM)


def params():
    return pltpu.CompilerParams(vmem_limit_bytes=VMEM_LIMIT)


def cost(flops, size):
    return pl.CostEstimate(flops=flops, bytes_accessed=size, transcendentals=0)


def iota(shape, axis):
    return lax.broadcasted_iota(jnp.int32, shape, axis)


def segments(tiles):
    first, second, third = tiles
    lane = iota(first.shape, 1)
    low = lane < 64
    return first, jnp.where(low, second, first), jnp.where(low, third, second), third


def turned_by(x, lanes):
    return pltpu.roll(x, lanes % LANES, 1) if lanes % LANES else x


def split_quad(tiles):
    return [turned_by(part, 32 * j) for j, part in enumerate(segments(tiles))]


def shift_quad(tiles):
    return [turned_by(part, 32 * j + BS) for j, part in enumerate(segments(tiles))]


def join_quad(blocks):
    lane = iota(blocks[0].shape, 1)
    parts = [turned_by(block, LANES - 32 * j) for j, block in enumerate(blocks)]
    return [
        jnp.where(lane < 96, parts[0], parts[1]),
        jnp.where(lane < 64, parts[1], parts[2]),
        jnp.where(lane < 32, parts[2], parts[3]),
    ]


def store_quad(state_ref, q, tiles):
    near, far = split_quad(tiles), shift_quad(tiles)
    for j in range(QUAD):
        state_ref[0, q * QUAD + j] = near[j].astype(jnp.bfloat16)
        state_ref[1, q * QUAD + j] = far[j].astype(jnp.bfloat16)


def tall(row_tile):
    return jnp.concatenate([row_tile] * (COLS // 8), axis=0)


def arrivals(peers):
    return [peers - 1] + list(range(1, peers - 1)) + [0]


def write_sent(peers, send_ref, count_ref, sign_ref, state_ref, sent_refs):
    me = lax.axis_index("patch")
    for i in range(peers):
        q = me ^ i
        for f in range(F):
            block = send_ref[q, f]
            scale = jnp.where(f < count_ref[q], 1.0, 0.0).astype(jnp.float32)
            sign = sign_ref[lax.rem(block, QUAD), pl.ds(lax.div(block, QUAD), 1), :] * scale
            picked = state_ref[0, block].astype(jnp.float32) * sign
            sent_refs[i][f] = picked.astype(jnp.bfloat16)


def copies(sources, targets, sems):
    started = [
        pltpu.make_async_copy(source, target, sems.at[i])
        for i, (source, target) in enumerate(zip(sources, targets))
    ]
    for one in started:
        one.start()
    return started


def prep_kernel(peers, *refs):
    sources, curl_hbm = refs[:5], refs[5]
    state_ref, sign_ref, source_ref, scale_ref, head_ref = refs[6:11]
    sent_refs = refs[11 : 11 + peers]
    held, sems = refs[11 + peers : -1], refs[-1]
    send_ref, count_ref, hole_ref, flip_ref, rhs_ref = held
    *needed, ahead = copies(
        sources + (curl_hbm.at[pl.ds(0, STAGES[0])],), held + (head_ref,), sems
    )
    for one in needed:
        one.wait()
    quads = NB // QUAD
    flips = [
        1.0 - 2.0 * flip_ref[pl.ds(u, quads, stride=TILES), :].astype(jnp.float32)
        for u in range(TILES)
    ]
    for j, sign in enumerate(split_quad(flips)):
        sign_ref[j] = sign
    lane = iota((8, LANES), 1)
    for q in range(quads):
        keeps = [hole_ref[q * QUAD + j].astype(jnp.float32) for j in range(QUAD)]
        tiles = []
        for u in range(TILES):
            at = (q * TILES + u) * LANES
            keep = jnp.where(lane < BS - 32 * u, keeps[u], keeps[u + 1])
            scale_ref[q * TILES + u] = COUPLING * keep
            tile = tall(keep) * rhs_ref[:, at : at + LANES].astype(jnp.float32)
            source_ref[q * TILES + u] = tile.astype(jnp.bfloat16)
            tiles.append(tile)
        store_quad(state_ref, q, tiles)
    write_sent(peers, send_ref, count_ref, sign_ref, state_ref, sent_refs)
    ahead.wait()


def picker(group):
    depth = 8 * TILES * group
    row = iota((32 * group, 2 * depth), 0)
    at = iota((32 * group, 2 * depth), 1)
    member, e = row // 32, row % 32
    r, j = e // QUAD, e % QUAD
    low = jnp.where(j == 0, 0, jnp.where(j == 1, 1, 2))
    high = jnp.where(j < 2, 0, j - 1)
    want_low = (r * TILES + low) * group + member
    want_high = (r * TILES + high) * group + member + depth
    return ((at == want_low) | (at == want_high)).astype(jnp.float32).astype(jnp.bfloat16)


def stack(select, rows, group):
    depth = 8 * TILES * group
    wide = jnp.concatenate([rows[g * depth : (g + 1) * depth] for g in range(3)], axis=1)
    high = iota(wide.shape, 1) % LANES >= 64
    zero = jnp.zeros_like(wide)
    both = jnp.concatenate([jnp.where(high, zero, wide), jnp.where(high, wide, zero)], axis=0)
    return jnp.dot(select, both, preferred_element_type=jnp.float32).astype(jnp.bfloat16)


def unstack(picked, member):
    mine = picked[32 * member : 32 * (member + 1)]
    return jnp.concatenate([mine[:, g * LANES : (g + 1) * LANES] for g in range(3)], axis=0)


def turn(square):
    turned = square.T
    bands = [turned[32 * a : 32 * (a + 1)] for a in range(4)]
    lane = iota((32, LANES), 1)
    for bit in (1, 2):
        odd = lane & bit == bit
        bands = [jnp.where(odd, bands[(a - bit) % 4], bands[a]) for a in range(4)]
    return jnp.concatenate(bands[: BS // 32], axis=0)


def spread_kernel(
    peers, curl_hbm, dtn_hbm, head_ref, matrix_ref, face_ref, curl_ref, dtn_ref, even_ref, odd_ref,
    sems,
):
    ahead = STAGES[0]
    pieces = (NB - ahead) // PIECE
    started = copies(
        [curl_hbm.at[pl.ds(ahead + i * PIECE, PIECE)] for i in range(pieces)] + [dtn_hbm],
        [curl_ref.at[pl.ds(i * PIECE, PIECE)] for i in range(pieces)] + [dtn_ref],
        sems,
    )
    select, select_faces = picker(K), picker(F)
    tasks, done = [([], [(select, head_ref, step, K) for step in range(ahead)])], 0
    for size in STAGES[1:]:
        waits = [started[i] for i in range(-(-done // PIECE), -(-(done + size) // PIECE))]
        tasks.append((waits, [(select, curl_ref, done + step, K) for step in range(size)]))
        done += size
    quarter = max(STAGES) * K // F
    for first in range(0, peers, quarter):
        waits = [started[pieces]] if first == 0 else []
        members = range(first, min(first + quarter, peers))
        faces = [(select_faces, dtn_ref, q, F) for q in members]
        tasks.append((waits, faces))

    def gather(task):
        waits, items = task
        for one in waits:
            one.wait()
        return [(rows, n, size, stack(pick, rows[n], size)) for pick, rows, n, size in items]

    def store(results, held_ref):
        for at, (rows, _, size, picked) in enumerate(results):
            for member in range(size):
                square = unstack(picked, member)
                if rows is dtn_ref:
                    slot, place = (at * size + member) // QUAD, member % QUAD
                else:
                    slot, place = at // QUAD * K + member, at % QUAD
                held_ref[slot, place * BS : (place + 1) * BS] = square

    def finish(results, held_ref):
        for at, (rows, n, size, _) in enumerate(results):
            if rows is dtn_ref:
                for member in range(size):
                    half, side = member // 2, slice(member % 2 * PAD, (member % 2 + 1) * PAD)
                    slot, place = (at * size + member) // QUAD, member % QUAD
                    pad = jnp.zeros((PAD - BS, LANES), jnp.bfloat16)
                    square = held_ref[slot, place * BS : (place + 1) * BS]
                    face_ref[n, half, :, side] = turn(jnp.concatenate([square, pad], axis=0))
            elif at % QUAD == 0:
                q = (n if rows is head_ref else ahead + n) // QUAD
                for k in range(K):
                    depth = slice(k % 2 * BS, (k % 2 + 1) * BS)
                    for u in range(TILES):
                        left = (q % 2 * TILES + u) * LANES
                        square = held_ref[at // QUAD * K + k, u * LANES : (u + 1) * LANES]
                        matrix_ref[q // 2, k // 2, depth, left : left + LANES] = turn(square)

    held = (even_ref, odd_ref)
    results = gather(tasks[0])
    store(results, held[0])
    for i in range(len(tasks)):
        upcoming = gather(tasks[i + 1]) if i + 1 < len(tasks) else []
        finish(results, held[i % 2])
        store(upcoming, held[(i + 1) % 2])
        results = upcoming


def paired(left, right, matrices):
    both = jnp.concatenate([left, right], axis=0)[:, :BS]
    wide = jnp.dot(both, matrices, preferred_element_type=jnp.float32)
    return wide[:COLS, :PAD], wide[COLS:, PAD:]


def add_faces(peers, target_ref, received_refs, face_ref, extra_ref):
    me = lax.axis_index("patch")
    products = []
    for i, received_ref in zip(arrivals(peers), received_refs):
        q = me ^ i
        for f in range(0, F, 2):
            pair = paired(received_ref[f], received_ref[f + 1], face_ref[q, f // 2])
            for step, product in enumerate(pair):
                products.append((q, f + step, product.astype(jnp.bfloat16).astype(jnp.float32)))
    for q, f, product in products:
        n = target_ref[q, f]
        extra_ref[f % 2, n] = extra_ref[f % 2, n] + product


def set_forcing(source_ref, scale_ref, extra_ref, forcing_ref):
    for q in range(NB // QUAD):
        blocks = range(q * QUAD, (q + 1) * QUAD)
        tiles = join_quad([extra_ref[0, n] + extra_ref[1, n] for n in blocks])
        for u, tile in enumerate(tiles):
            at = q * TILES + u
            kept = jnp.where(tall(scale_ref[at]) > 0, tile, 0.0)
            forcing_ref[at] = source_ref[at].astype(jnp.float32) + kept


def images_of(cols_ref, matrix_ref, old_ref, group):
    lane = iota((COLS, LANES), 1)

    def nearby(n, half):
        near = old_ref[0, cols_ref[2 * half, n]]
        far = old_ref[1, cols_ref[2 * half + 1, n]]
        return jnp.concatenate([jnp.where(lane < BS, near, far), far], axis=1)

    totals = [None] * (2 * TILES)
    for third, rows in enumerate(((0, 1, 2), (2, 3, 4, 5), (5, 6, 7))):
        columns = slice(third * 2 * LANES, (third + 1) * 2 * LANES)
        for half in range(K // 2):
            left = jnp.concatenate([nearby(group * 2 * QUAD + j, half) for j in rows], axis=0)
            wide = jnp.dot(
                left[:, : 2 * BS], matrix_ref[group, half, :, columns],
                preferred_element_type=jnp.float32,
            )
            for side in range(2):
                tile = third * 2 + side
                first = tile * LANES // BS
                cut = (first + 1) * BS - tile * LANES
                at = rows.index(first) * COLS
                part = wide[:, side * LANES : (side + 1) * LANES]
                picked = jnp.where(lane < cut, part[at : at + COLS], part[at + COLS : at + 2 * COLS])
                totals[tile] = picked if half == 0 else totals[tile] + picked
    return totals


def step_tile(forcing_ref, scale_ref, image, at):
    return forcing_ref[at] - tall(scale_ref[at]) * image


def sweep(cols_ref, scale_ref, matrix_ref, forcing_ref, old_ref, new_ref):
    groups = NB // (2 * QUAD)
    for first in range(0, groups, CHUNK):
        chunk = range(first, first + CHUNK)
        images = [images_of(cols_ref, matrix_ref, old_ref, group) for group in chunk]
        for group, parts in zip(chunk, images):
            tiles = [
                step_tile(forcing_ref, scale_ref, part, group * 2 * TILES + i)
                for i, part in enumerate(parts)
            ]
            for side in range(2):
                store_quad(new_ref, group * 2 + side, tiles[side * TILES : (side + 1) * TILES])


def end_blocks():
    odd = lax.rem(lax.axis_index("sec"), 2)
    return (1 - odd) * (NB - NI), odd * (NB - NI)


def first_tick_kernel(peers, *refs):
    cols_ref, target_ref, send_ref, count_ref = refs[:4]
    sign_ref, scale_ref, matrix_ref, face_ref, source_ref = refs[4:9]
    received_refs = refs[10 : 10 + peers]
    state_ref, swap_in_ref, swap_out_ref = refs[10 + peers : 13 + peers]
    sent_refs = refs[13 + peers : 13 + 2 * peers]
    forcing_ref, extra_ref, other_ref = refs[13 + 2 * peers :]
    extra_ref[...] = jnp.zeros_like(extra_ref)
    add_faces(peers, target_ref, received_refs, face_ref, extra_ref)
    set_forcing(source_ref, scale_ref, extra_ref, forcing_ref)

    def two(i, carry):
        sweep(cols_ref, scale_ref, matrix_ref, forcing_ref, state_ref, other_ref)
        sweep(cols_ref, scale_ref, matrix_ref, forcing_ref, other_ref, state_ref)
        return carry

    lax.fori_loop(0, ITERS // 2, two, 0)
    inner, outer = end_blocks()
    swap_in_ref[...] = state_ref[0, pl.ds(inner, NI)]
    swap_out_ref[...] = state_ref[0, pl.ds(outer, NI)]
    write_sent(peers, send_ref, count_ref, sign_ref, state_ref, sent_refs)


def first_image_kernel(cols_ref, matrix_ref, state_ref, image_ref):
    for group in range(NB // (2 * QUAD)):
        for i, part in enumerate(images_of(cols_ref, matrix_ref, state_ref, group)):
            image_ref[group * 2 * TILES + i] = part


def last_tick_kernel(peers, *refs):
    cols_ref, target_ref, scale_ref, matrix_ref, face_ref, source_ref, image_ref = refs[:7]
    received_refs = refs[7 : 7 + peers]
    swap_in_ref, swap_out_ref = refs[7 + peers : 9 + peers]
    out_ref, forcing_ref, extra_ref, state_ref, other_ref = refs[9 + peers :]
    inner, outer = end_blocks()
    extra_ref[...] = jnp.zeros_like(extra_ref)
    extra_ref[0, pl.ds(inner, NI)] = swap_in_ref[...].astype(jnp.float32)
    extra_ref[0, pl.ds(outer, NI)] = swap_out_ref[...].astype(jnp.float32)
    add_faces(peers, target_ref, received_refs, face_ref, extra_ref)
    set_forcing(source_ref, scale_ref, extra_ref, forcing_ref)
    for q in range(NB // QUAD):
        tiles = range(q * TILES, (q + 1) * TILES)
        store_quad(state_ref, q, [step_tile(forcing_ref, scale_ref, image_ref[i], i) for i in tiles])

    def two(i, carry):
        sweep(cols_ref, scale_ref, matrix_ref, forcing_ref, state_ref, other_ref)
        sweep(cols_ref, scale_ref, matrix_ref, forcing_ref, other_ref, state_ref)
        return carry

    lax.fori_loop(0, ITERS // 2 - 1, two, 0)
    for group in range(NB // (2 * QUAD)):
        for i, part in enumerate(images_of(cols_ref, matrix_ref, state_ref, group)):
            at = group * 2 * TILES + i
            out_ref[:, at * LANES : (at + 1) * LANES] = step_tile(forcing_ref, scale_ref, part, at)


def swapped(x, axis, first):
    size = lax.axis_size(axis)
    pairs = []
    for i in range(first, size - 1, 2):
        pairs += [(i, i + 1), (i + 1, i)]
    return lax.ppermute(x, axis, pairs)


def shape(dims, dtype):
    return jax.ShapeDtypeStruct(dims, dtype)


def shards(
    rhs, curl_blocks, block_cols, hole_mask, edge_flip, send_list, send_count, recv_list, dtn_blocks
):
    peers = send_list.shape[2]
    f32, bf16 = jnp.float32, jnp.bfloat16
    tiles = BS * BS // LANES
    cols = block_cols.T
    in_hbm = functools.partial(pltpu.with_memory_space_constraint, memory_space=pltpu.HBM)
    sends, counts, targets = send_list[0, 0], send_count[0, 0], recv_list[0, 0]
    flips = edge_flip.reshape(NB * BS // LANES, LANES)
    curl_rows = curl_blocks.reshape(NB, K, tiles, LANES).transpose(0, 2, 1, 3)
    curl_rows = curl_rows.reshape(NB, tiles * K, LANES)
    dtn_rows = dtn_blocks[0, 0].reshape(peers, F, tiles, LANES).transpose(0, 2, 1, 3)
    dtn_rows = dtn_rows.reshape(peers, tiles * F, LANES)

    count = NB * BS // LANES
    block_shape = (NB, COLS, PAD)
    tile_shape = (count, COLS, LANES)
    state_shape = (2, NB, COLS, PAD)
    face = shape((F, COLS, PAD), bf16)
    ends = shape((NI, COLS, PAD), bf16)
    state, sign, source, scale, head, *sent = pl.pallas_call(
        functools.partial(prep_kernel, peers),
        out_shape=(
            shape(state_shape, bf16),
            shape((QUAD, NB // QUAD, LANES), f32),
            shape(tile_shape, bf16),
            shape((count, 8, LANES), f32),
            shape((STAGES[0],) + curl_rows.shape[1:], bf16),
        )
        + (face,) * peers,
        in_specs=[HBM] * 6,
        out_specs=[VMEM] * (5 + peers),
        scratch_shapes=[
            pltpu.SMEM(sends.shape, jnp.int32),
            pltpu.SMEM(counts.shape, jnp.int32),
            pltpu.SMEM(hole_mask.shape, jnp.int32),
            pltpu.VMEM(flips.shape, jnp.int32),
            pltpu.VMEM(rhs.shape, bf16),
            pltpu.SemaphoreType.DMA((6,)),
        ],
        compiler_params=params(),
        cost_estimate=cost(10**6, 10**6),
    )(*map(in_hbm, (sends, counts, hole_mask, flips, rhs, curl_rows)))

    matrices, faces = pl.pallas_call(
        functools.partial(spread_kernel, peers),
        out_shape=(
            shape((NB // (2 * QUAD), K // 2, 2 * BS, 2 * TILES * LANES), bf16),
            shape((peers, F // 2, BS, 2 * PAD), bf16),
        ),
        in_specs=[HBM] * 2 + [VMEM],
        out_specs=[VMEM] * 2,
        scratch_shapes=[
            pltpu.VMEM((NB - STAGES[0],) + curl_rows.shape[1:], bf16),
            pltpu.VMEM(dtn_rows.shape, bf16),
            pltpu.VMEM((max(STAGES) * K // QUAD, QUAD * BS, LANES), bf16),
            pltpu.VMEM((max(STAGES) * K // QUAD, QUAD * BS, LANES), bf16),
            pltpu.SemaphoreType.DMA(((NB - STAGES[0]) // PIECE + 1,)),
        ],
        compiler_params=params(),
        cost_estimate=cost(4 * 10**9, 16 * 10**6),
    )(in_hbm(curl_rows), in_hbm(dtn_rows), head)

    def exchange(sent):
        pairs = [[(p, p ^ i) for p in range(peers)] for i in range(peers)]
        return [lax.ppermute(sent[i], "patch", pairs[i]) if i else sent[0] for i in arrivals(peers)]

    received = exchange(sent)
    state, swap_in, swap_out, *sent = pl.pallas_call(
        functools.partial(first_tick_kernel, peers),
        out_shape=(shape(state_shape, bf16), ends, ends) + (face,) * peers,
        in_specs=[SMEM] * 4 + [VMEM] * (6 + peers),
        out_specs=[VMEM] * (3 + peers),
        scratch_shapes=[
            pltpu.VMEM(tile_shape, f32),
            pltpu.VMEM((2,) + block_shape, f32),
            pltpu.VMEM(state_shape, bf16),
        ],
        input_output_aliases={9: 0},
        compiler_params=params(),
        cost_estimate=cost(10**10, 16 * 10**6),
    )(cols, targets, sends, counts, sign, scale, matrices, faces, source, state, *received)

    received = exchange(sent)
    swap_in = swapped(swap_in, "sec", 0)
    swap_out = swapped(swap_out, "sec", 1)
    image = pl.pallas_call(
        first_image_kernel,
        out_shape=shape(tile_shape, f32),
        in_specs=[SMEM] + [VMEM] * 2,
        out_specs=VMEM,
        compiler_params=params(),
        cost_estimate=cost(10**9, 8 * 10**6),
    )(cols, matrices, state)
    return pl.pallas_call(
        functools.partial(last_tick_kernel, peers),
        out_shape=shape((COLS, NB * BS), f32),
        in_specs=[SMEM] * 2 + [VMEM] * (7 + peers),
        out_specs=VMEM,
        scratch_shapes=[
            pltpu.VMEM(tile_shape, f32),
            pltpu.VMEM((2,) + block_shape, f32),
            pltpu.VMEM(state_shape, bf16),
            pltpu.VMEM(state_shape, bf16),
        ],
        compiler_params=params(),
        cost_estimate=cost(10**10, 16 * 10**6),
    )(cols, targets, scale, matrices, faces, source, image, *received, swap_in, swap_out)


def solution(mesh):
    in_specs = (
        P(None, ("sec", "patch")),
        P(("sec", "patch"), None, None),
        P(("sec", "patch"), None),
        P(("sec", "patch")),
        P(("sec", "patch")),
        P("sec", "patch", None, None),
        P("sec", "patch", None),
        P("sec", "patch", None, None),
        P("sec", "patch", None, None, None),
    )
    out_specs = P(None, ("sec", "patch"))
    return jax.shard_map(shards, mesh=mesh, in_specs=in_specs, out_specs=out_specs, check_vma=False)
```

```python
import functools

import jax
import jax.numpy as jnp
from jax import lax
from jax.experimental import pallas as pl
from jax.experimental.pallas import tpu as pltpu
from jax.sharding import PartitionSpec as P

BS = 96
COLS = 24
NB = 64
K = 4
F = 8
NI = 8
ITERS = 8
TICKS = 2
COUPLING = 0.85

LANES = 128
PAD = 128
QUAD = 4
TILES = 3
VMEM_LIMIT = 30 * 2**20
STAGES = (16, 16, 16, 16)
PIECE = 8
OUT_PIECES = 4
CHUNK = 4

VMEM = pl.BlockSpec(memory_space=pltpu.VMEM)
SMEM = pl.BlockSpec(memory_space=pltpu.SMEM)
HBM = pl.BlockSpec(memory_space=pltpu.HBM)


def params():
    return pltpu.CompilerParams(vmem_limit_bytes=VMEM_LIMIT)


def cost(flops, size):
    return pl.CostEstimate(flops=flops, bytes_accessed=size, transcendentals=0)


def iota(shape, axis):
    return lax.broadcasted_iota(jnp.int32, shape, axis)


def segments(tiles):
    first, second, third = tiles
    lane = iota(first.shape, 1)
    low = lane < 64
    return first, jnp.where(low, second, first), jnp.where(low, third, second), third


def turned_by(x, lanes):
    return pltpu.roll(x, lanes % LANES, 1) if lanes % LANES else x


def split_quad(tiles):
    return [turned_by(part, 32 * j) for j, part in enumerate(segments(tiles))]


def shift_quad(tiles):
    return [turned_by(part, 32 * j + BS) for j, part in enumerate(segments(tiles))]


def join_quad(blocks):
    lane = iota(blocks[0].shape, 1)
    parts = [turned_by(block, LANES - 32 * j) for j, block in enumerate(blocks)]
    return [
        jnp.where(lane < 96, parts[0], parts[1]),
        jnp.where(lane < 64, parts[1], parts[2]),
        jnp.where(lane < 32, parts[2], parts[3]),
    ]


def store_quad(state_ref, q, tiles):
    near, far = split_quad(tiles), shift_quad(tiles)
    for j in range(QUAD):
        state_ref[0, q * QUAD + j] = near[j].astype(jnp.bfloat16)
        state_ref[1, q * QUAD + j] = far[j].astype(jnp.bfloat16)


def tall(row_tile):
    return jnp.concatenate([row_tile] * (COLS // 8), axis=0)


def arrivals(peers):
    return [peers - 1] + list(range(1, peers - 1)) + [0]


def write_sent(peers, send_ref, count_ref, sign_ref, state_ref, sent_refs):
    me = lax.axis_index("patch")
    for i in range(peers):
        q = me ^ i
        for f in range(F):
            block = send_ref[q, f]
            scale = jnp.where(f < count_ref[q], 1.0, 0.0).astype(jnp.float32)
            sign = sign_ref[lax.rem(block, QUAD), pl.ds(lax.div(block, QUAD), 1), :] * scale
            picked = state_ref[0, block].astype(jnp.float32) * sign
            sent_refs[i][f] = picked.astype(jnp.bfloat16)


def copies(sources, targets, sems):
    started = [
        pltpu.make_async_copy(source, target, sems.at[i])
        for i, (source, target) in enumerate(zip(sources, targets))
    ]
    for one in started:
        one.start()
    return started


def prep_kernel(peers, *refs):
    sources, curl_hbm = refs[:5], refs[5]
    state_ref, sign_ref, source_ref, scale_ref, head_ref = refs[6:11]
    sent_refs = refs[11 : 11 + peers]
    held, sems = refs[11 + peers : -1], refs[-1]
    send_ref, count_ref, hole_ref, flip_ref, rhs_ref = held
    *needed, ahead = copies(
        sources + (curl_hbm.at[pl.ds(0, STAGES[0])],), held + (head_ref,), sems
    )
    for one in needed:
        one.wait()
    quads = NB // QUAD
    flips = [
        1.0 - 2.0 * flip_ref[pl.ds(u, quads, stride=TILES), :].astype(jnp.float32)
        for u in range(TILES)
    ]
    for j, sign in enumerate(split_quad(flips)):
        sign_ref[j] = sign
    lane = iota((8, LANES), 1)
    for q in range(quads):
        keeps = [hole_ref[q * QUAD + j].astype(jnp.float32) for j in range(QUAD)]
        tiles = []
        for u in range(TILES):
            at = (q * TILES + u) * LANES
            keep = jnp.where(lane < BS - 32 * u, keeps[u], keeps[u + 1])
            scale_ref[q * TILES + u] = COUPLING * keep
            tile = tall(keep) * rhs_ref[:, at : at + LANES].astype(jnp.float32)
            source_ref[q * TILES + u] = tile.astype(jnp.bfloat16)
            tiles.append(tile)
        store_quad(state_ref, q, tiles)
    write_sent(peers, send_ref, count_ref, sign_ref, state_ref, sent_refs)
    ahead.wait()


def picker(group):
    depth = 8 * TILES * group
    row = iota((32 * group, 2 * depth), 0)
    at = iota((32 * group, 2 * depth), 1)
    member, e = row // 32, row % 32
    r, j = e // QUAD, e % QUAD
    low = jnp.where(j == 0, 0, jnp.where(j == 1, 1, 2))
    high = jnp.where(j < 2, 0, j - 1)
    want_low = (r * TILES + low) * group + member
    want_high = (r * TILES + high) * group + member + depth
    return ((at == want_low) | (at == want_high)).astype(jnp.float32).astype(jnp.bfloat16)


def stack(select, first, second, group):
    depth = 8 * TILES * group
    parts = [rows[g * depth : (g + 1) * depth] for rows in (first, second) for g in range(3)]
    wide = jnp.concatenate(parts, axis=1)
    high = iota(wide.shape, 1) % LANES >= 64
    zero = jnp.zeros_like(wide)
    both = jnp.concatenate([jnp.where(high, zero, wide), jnp.where(high, wide, zero)], axis=0)
    picked = jnp.dot(select, both, preferred_element_type=jnp.float32).astype(jnp.bfloat16)
    return picked[:, : 3 * LANES], picked[:, 3 * LANES :]


def unstack(picked, member):
    mine = picked[32 * member : 32 * (member + 1)]
    return jnp.concatenate([mine[:, g * LANES : (g + 1) * LANES] for g in range(3)], axis=0)


def turn(square):
    turned = square.T
    bands = [turned[32 * a : 32 * (a + 1)] for a in range(4)]
    lane = iota((32, LANES), 1)
    for bit in (1, 2):
        odd = lane & bit == bit
        bands = [jnp.where(odd, bands[(a - bit) % 4], bands[a]) for a in range(4)]
    return jnp.concatenate(bands[: BS // 32], axis=0)


def spread_kernel(
    peers, curl_hbm, dtn_hbm, head_ref, matrix_ref, face_ref, curl_ref, dtn_ref, even_ref, odd_ref,
    sems,
):
    ahead = STAGES[0]
    pieces = (NB - ahead) // PIECE
    started = copies(
        [curl_hbm.at[pl.ds(ahead + i * PIECE, PIECE)] for i in range(pieces)] + [dtn_hbm],
        [curl_ref.at[pl.ds(i * PIECE, PIECE)] for i in range(pieces)] + [dtn_ref],
        sems,
    )
    select, select_faces = picker(K), picker(F)
    tasks, done = [([], [(select, head_ref, step, K) for step in range(ahead)])], 0
    for size in STAGES[1:]:
        waits = [started[i] for i in range(-(-done // PIECE), -(-(done + size) // PIECE))]
        tasks.append((waits, [(select, curl_ref, done + step, K) for step in range(size)]))
        done += size
    quarter = max(STAGES) * K // F
    for first in range(0, peers, quarter):
        waits = [started[pieces]] if first == 0 else []
        members = range(first, min(first + quarter, peers))
        faces = [(select_faces, dtn_ref, q, F) for q in members]
        tasks.append((waits, faces))

    def gather(task):
        waits, items = task
        for one in waits:
            one.wait()
        results = []
        for (pick, rows, n, size), (*_, other, _) in zip(items[::2], items[1::2]):
            pair = stack(pick, rows[n], rows[other], size)
            results += [(rows, n, size, pair[0]), (rows, other, size, pair[1])]
        return results

    def store(results, held_ref):
        for at, (rows, _, size, picked) in enumerate(results):
            for member in range(size):
                square = unstack(picked, member)
                if rows is dtn_ref:
                    slot, place = (at * size + member) // QUAD, member % QUAD
                else:
                    slot, place = at // QUAD * K + member, at % QUAD
                held_ref[slot, place * BS : (place + 1) * BS] = square

    def finish(results, held_ref):
        for at, (rows, n, size, _) in enumerate(results):
            if rows is dtn_ref:
                for member in range(size):
                    half, side = member // 2, slice(member % 2 * PAD, (member % 2 + 1) * PAD)
                    slot, place = (at * size + member) // QUAD, member % QUAD
                    pad = jnp.zeros((PAD - BS, LANES), jnp.bfloat16)
                    square = held_ref[slot, place * BS : (place + 1) * BS]
                    face_ref[n, half, :, side] = turn(jnp.concatenate([square, pad], axis=0))
            elif at % QUAD == 0:
                q = (n if rows is head_ref else ahead + n) // QUAD
                for k in range(K):
                    depth = slice(k % 2 * BS, (k % 2 + 1) * BS)
                    for u in range(TILES):
                        left = (q % 2 * TILES + u) * LANES
                        square = held_ref[at // QUAD * K + k, u * LANES : (u + 1) * LANES]
                        matrix_ref[q // 2, k // 2, depth, left : left + LANES] = turn(square)

    held = (even_ref, odd_ref)
    results = gather(tasks[0])
    store(results, held[0])
    for i in range(len(tasks)):
        upcoming = gather(tasks[i + 1]) if i + 1 < len(tasks) else []
        finish(results, held[i % 2])
        store(upcoming, held[(i + 1) % 2])
        results = upcoming


def paired(left, right, matrices):
    both = jnp.concatenate([left, right], axis=0)[:, :BS]
    wide = jnp.dot(both, matrices, preferred_element_type=jnp.float32)
    return wide[:COLS, :PAD], wide[COLS:, PAD:]


def add_faces(peers, target_ref, received_refs, face_ref, extra_ref):
    me = lax.axis_index("patch")
    products = []
    for i, received_ref in zip(arrivals(peers), received_refs):
        q = me ^ i
        for f in range(0, F, 2):
            pair = paired(received_ref[f], received_ref[f + 1], face_ref[q, f // 2])
            for step, product in enumerate(pair):
                products.append((q, f + step, product.astype(jnp.bfloat16).astype(jnp.float32)))
    for q, f, product in products:
        n = target_ref[q, f]
        extra_ref[f % 2, n] = extra_ref[f % 2, n] + product


def set_forcing(source_ref, scale_ref, extra_ref, forcing_ref):
    for q in range(NB // QUAD):
        blocks = range(q * QUAD, (q + 1) * QUAD)
        tiles = join_quad([extra_ref[0, n] + extra_ref[1, n] for n in blocks])
        for u, tile in enumerate(tiles):
            at = q * TILES + u
            kept = jnp.where(tall(scale_ref[at]) > 0, tile, 0.0)
            forcing_ref[at] = source_ref[at].astype(jnp.float32) + kept


def images_of(cols_ref, matrix_ref, old_ref, group):
    lane = iota((COLS, LANES), 1)

    def nearby(n, half):
        near = old_ref[0, cols_ref[2 * half, n]]
        far = old_ref[1, cols_ref[2 * half + 1, n]]
        return jnp.concatenate([jnp.where(lane < BS, near, far), far], axis=1)

    totals = [None] * (2 * TILES)
    for third, rows in enumerate(((0, 1, 2), (2, 3, 4, 5), (5, 6, 7))):
        columns = slice(third * 2 * LANES, (third + 1) * 2 * LANES)
        for half in range(K // 2):
            left = jnp.concatenate([nearby(group * 2 * QUAD + j, half) for j in rows], axis=0)
            wide = jnp.dot(
                left[:, : 2 * BS], matrix_ref[group, half, :, columns],
                preferred_element_type=jnp.float32,
            )
            for side in range(2):
                tile = third * 2 + side
                first = tile * LANES // BS
                cut = (first + 1) * BS - tile * LANES
                at = rows.index(first) * COLS
                part = wide[:, side * LANES : (side + 1) * LANES]
                picked = jnp.where(lane < cut, part[at : at + COLS], part[at + COLS : at + 2 * COLS])
                totals[tile] = picked if half == 0 else totals[tile] + picked
    return totals


def step_tile(forcing_ref, scale_ref, image, at):
    return forcing_ref[at] - tall(scale_ref[at]) * image


def sweep(cols_ref, scale_ref, matrix_ref, forcing_ref, old_ref, new_ref):
    groups = NB // (2 * QUAD)
    for first in range(0, groups, CHUNK):
        chunk = range(first, first + CHUNK)
        images = [images_of(cols_ref, matrix_ref, old_ref, group) for group in chunk]
        for group, parts in zip(chunk, images):
            tiles = [
                step_tile(forcing_ref, scale_ref, part, group * 2 * TILES + i)
                for i, part in enumerate(parts)
            ]
            for side in range(2):
                store_quad(new_ref, group * 2 + side, tiles[side * TILES : (side + 1) * TILES])


def end_blocks():
    odd = lax.rem(lax.axis_index("sec"), 2)
    return (1 - odd) * (NB - NI), odd * (NB - NI)


def first_tick_kernel(peers, *refs):
    cols_ref, target_ref, send_ref, count_ref = refs[:4]
    sign_ref, scale_ref, matrix_ref, face_ref, source_ref = refs[4:9]
    received_refs = refs[10 : 10 + peers]
    state_ref, swap_in_ref, swap_out_ref = refs[10 + peers : 13 + peers]
    sent_refs = refs[13 + peers : 13 + 2 * peers]
    forcing_ref, extra_ref, other_ref = refs[13 + 2 * peers :]
    extra_ref[...] = jnp.zeros_like(extra_ref)
    add_faces(peers, target_ref, received_refs, face_ref, extra_ref)
    set_forcing(source_ref, scale_ref, extra_ref, forcing_ref)

    def two(i, carry):
        sweep(cols_ref, scale_ref, matrix_ref, forcing_ref, state_ref, other_ref)
        sweep(cols_ref, scale_ref, matrix_ref, forcing_ref, other_ref, state_ref)
        return carry

    lax.fori_loop(0, ITERS // 2, two, 0)
    inner, outer = end_blocks()
    swap_in_ref[...] = state_ref[0, pl.ds(inner, NI)]
    swap_out_ref[...] = state_ref[0, pl.ds(outer, NI)]
    write_sent(peers, send_ref, count_ref, sign_ref, state_ref, sent_refs)


def first_image_kernel(cols_ref, matrix_ref, state_ref, image_ref):
    for group in range(NB // (2 * QUAD)):
        for i, part in enumerate(images_of(cols_ref, matrix_ref, state_ref, group)):
            image_ref[group * 2 * TILES + i] = part


def last_tick_kernel(peers, *refs):
    cols_ref, target_ref, scale_ref, matrix_ref, face_ref, source_ref, image_ref = refs[:7]
    received_refs = refs[7 : 7 + peers]
    swap_in_ref, swap_out_ref = refs[7 + peers : 9 + peers]
    out_hbm, forcing_ref, extra_ref, state_ref, other_ref, out_ref, sems = refs[9 + peers :]
    inner, outer = end_blocks()
    extra_ref[...] = jnp.zeros_like(extra_ref)
    extra_ref[0, pl.ds(inner, NI)] = swap_in_ref[...].astype(jnp.float32)
    extra_ref[0, pl.ds(outer, NI)] = swap_out_ref[...].astype(jnp.float32)
    add_faces(peers, target_ref, received_refs, face_ref, extra_ref)
    set_forcing(source_ref, scale_ref, extra_ref, forcing_ref)
    for q in range(NB // QUAD):
        tiles = range(q * TILES, (q + 1) * TILES)
        store_quad(state_ref, q, [step_tile(forcing_ref, scale_ref, image_ref[i], i) for i in tiles])

    def two(i, carry):
        sweep(cols_ref, scale_ref, matrix_ref, forcing_ref, state_ref, other_ref)
        sweep(cols_ref, scale_ref, matrix_ref, forcing_ref, other_ref, state_ref)
        return carry

    lax.fori_loop(0, ITERS // 2 - 1, two, 0)
    groups = NB // (2 * QUAD)
    width = 2 * groups // OUT_PIECES * TILES * LANES
    leaving = []
    for group in range(groups):
        for i, part in enumerate(images_of(cols_ref, matrix_ref, state_ref, group)):
            at = group * 2 * TILES + i
            out_ref[:, at * LANES : (at + 1) * LANES] = step_tile(forcing_ref, scale_ref, part, at)
        if (group + 1) % (groups // OUT_PIECES) == 0:
            piece = len(leaving)
            columns = pl.ds(piece * width, width)
            leaving.append(
                pltpu.make_async_copy(out_ref.at[:, columns], out_hbm.at[:, columns], sems.at[piece])
            )
            leaving[-1].start()
    for one in leaving:
        one.wait()


def swapped(x, axis, first):
    size = lax.axis_size(axis)
    pairs = []
    for i in range(first, size - 1, 2):
        pairs += [(i, i + 1), (i + 1, i)]
    return lax.ppermute(x, axis, pairs)


def shape(dims, dtype):
    return jax.ShapeDtypeStruct(dims, dtype)


def shards(
    rhs, curl_blocks, block_cols, hole_mask, edge_flip, send_list, send_count, recv_list, dtn_blocks
):
    peers = send_list.shape[2]
    f32, bf16 = jnp.float32, jnp.bfloat16
    tiles = BS * BS // LANES
    cols = block_cols.T
    in_hbm = functools.partial(pltpu.with_memory_space_constraint, memory_space=pltpu.HBM)
    sends, counts, targets = send_list[0, 0], send_count[0, 0], recv_list[0, 0]
    flips = edge_flip.reshape(NB * BS // LANES, LANES)
    curl_rows = curl_blocks.reshape(NB, K, tiles, LANES).transpose(0, 2, 1, 3)
    curl_rows = curl_rows.reshape(NB, tiles * K, LANES)
    dtn_rows = dtn_blocks[0, 0].reshape(peers, F, tiles, LANES).transpose(0, 2, 1, 3)
    dtn_rows = dtn_rows.reshape(peers, tiles * F, LANES)

    count = NB * BS // LANES
    block_shape = (NB, COLS, PAD)
    tile_shape = (count, COLS, LANES)
    state_shape = (2, NB, COLS, PAD)
    face = shape((F, COLS, PAD), bf16)
    ends = shape((NI, COLS, PAD), bf16)
    state, sign, source, scale, head, *sent = pl.pallas_call(
        functools.partial(prep_kernel, peers),
        out_shape=(
            shape(state_shape, bf16),
            shape((QUAD, NB // QUAD, LANES), f32),
            shape(tile_shape, bf16),
            shape((count, 8, LANES), f32),
            shape((STAGES[0],) + curl_rows.shape[1:], bf16),
        )
        + (face,) * peers,
        in_specs=[HBM] * 6,
        out_specs=[VMEM] * (5 + peers),
        scratch_shapes=[
            pltpu.SMEM(sends.shape, jnp.int32),
            pltpu.SMEM(counts.shape, jnp.int32),
            pltpu.SMEM(hole_mask.shape, jnp.int32),
            pltpu.VMEM(flips.shape, jnp.int32),
            pltpu.VMEM(rhs.shape, bf16),
            pltpu.SemaphoreType.DMA((6,)),
        ],
        compiler_params=params(),
        cost_estimate=cost(10**6, 10**6),
    )(*map(in_hbm, (sends, counts, hole_mask, flips, rhs, curl_rows)))

    matrices, faces = pl.pallas_call(
        functools.partial(spread_kernel, peers),
        out_shape=(
            shape((NB // (2 * QUAD), K // 2, 2 * BS, 2 * TILES * LANES), bf16),
            shape((peers, F // 2, BS, 2 * PAD), bf16),
        ),
        in_specs=[HBM] * 2 + [VMEM],
        out_specs=[VMEM] * 2,
        scratch_shapes=[
            pltpu.VMEM((NB - STAGES[0],) + curl_rows.shape[1:], bf16),
            pltpu.VMEM(dtn_rows.shape, bf16),
            pltpu.VMEM((max(STAGES) * K // QUAD, QUAD * BS, LANES), bf16),
            pltpu.VMEM((max(STAGES) * K // QUAD, QUAD * BS, LANES), bf16),
            pltpu.SemaphoreType.DMA(((NB - STAGES[0]) // PIECE + 1,)),
        ],
        compiler_params=params(),
        cost_estimate=cost(4 * 10**9, 16 * 10**6),
    )(in_hbm(curl_rows), in_hbm(dtn_rows), head)

    def exchange(sent):
        pairs = [[(p, p ^ i) for p in range(peers)] for i in range(peers)]
        return [lax.ppermute(sent[i], "patch", pairs[i]) if i else sent[0] for i in arrivals(peers)]

    received = exchange(sent)
    state, swap_in, swap_out, *sent = pl.pallas_call(
        functools.partial(first_tick_kernel, peers),
        out_shape=(shape(state_shape, bf16), ends, ends) + (face,) * peers,
        in_specs=[SMEM] * 4 + [VMEM] * (6 + peers),
        out_specs=[VMEM] * (3 + peers),
        scratch_shapes=[
            pltpu.VMEM(tile_shape, f32),
            pltpu.VMEM((2,) + block_shape, f32),
            pltpu.VMEM(state_shape, bf16),
        ],
        input_output_aliases={9: 0},
        compiler_params=params(),
        cost_estimate=cost(10**10, 16 * 10**6),
    )(cols, targets, sends, counts, sign, scale, matrices, faces, source, state, *received)

    received = exchange(sent)
    swap_in = swapped(swap_in, "sec", 0)
    swap_out = swapped(swap_out, "sec", 1)
    image = pl.pallas_call(
        first_image_kernel,
        out_shape=shape(tile_shape, f32),
        in_specs=[SMEM] + [VMEM] * 2,
        out_specs=VMEM,
        compiler_params=params(),
        cost_estimate=cost(10**9, 8 * 10**6),
    )(cols, matrices, state)
    return pl.pallas_call(
        functools.partial(last_tick_kernel, peers),
        out_shape=shape((COLS, NB * BS), f32),
        in_specs=[SMEM] * 2 + [VMEM] * (7 + peers),
        out_specs=HBM,
        scratch_shapes=[
            pltpu.VMEM(tile_shape, f32),
            pltpu.VMEM((2,) + block_shape, f32),
            pltpu.VMEM(state_shape, bf16),
            pltpu.VMEM(state_shape, bf16),
            pltpu.VMEM((COLS, NB * BS), f32),
            pltpu.SemaphoreType.DMA((OUT_PIECES,)),
        ],
        compiler_params=params(),
        cost_estimate=cost(10**10, 16 * 10**6),
    )(cols, targets, scale, matrices, faces, source, image, *received, swap_in, swap_out)


def solution(mesh):
    in_specs = (
        P(None, ("sec", "patch")),
        P(("sec", "patch"), None, None),
        P(("sec", "patch"), None),
        P(("sec", "patch")),
        P(("sec", "patch")),
        P("sec", "patch", None, None),
        P("sec", "patch", None),
        P("sec", "patch", None, None),
        P("sec", "patch", None, None, None),
    )
    out_specs = P(None, ("sec", "patch"))
    return jax.shard_map(shards, mesh=mesh, in_specs=in_specs, out_specs=out_specs, check_vma=False)
```

```python
import functools

import jax
import jax.numpy as jnp
from jax import lax
from jax.experimental import pallas as pl
from jax.experimental.pallas import tpu as pltpu
from jax.sharding import PartitionSpec as P

BS = 96
COLS = 24
NB = 64
K = 4
F = 8
NI = 8
ITERS = 8
TICKS = 2
COUPLING = 0.85

LANES = 128
PAD = 128
QUAD = 4
TILES = 3
VMEM_LIMIT = 30 * 2**20
STAGES = (16, 16, 16, 16)
PIECE = 8
OUT_PIECES = 4
CHUNK = 4

VMEM = pl.BlockSpec(memory_space=pltpu.VMEM)
SMEM = pl.BlockSpec(memory_space=pltpu.SMEM)
HBM = pl.BlockSpec(memory_space=pltpu.HBM)


def params():
    return pltpu.CompilerParams(vmem_limit_bytes=VMEM_LIMIT)


def cost(flops, size):
    return pl.CostEstimate(flops=flops, bytes_accessed=size, transcendentals=0)


def iota(shape, axis):
    return lax.broadcasted_iota(jnp.int32, shape, axis)


def segments(tiles):
    first, second, third = tiles
    lane = iota(first.shape, 1)
    low = lane < 64
    return first, jnp.where(low, second, first), jnp.where(low, third, second), third


def turned_by(x, lanes):
    return pltpu.roll(x, lanes % LANES, 1) if lanes % LANES else x


def split_quad(tiles):
    return [turned_by(part, 32 * j) for j, part in enumerate(segments(tiles))]


def shift_quad(tiles):
    return [turned_by(part, 32 * j + BS) for j, part in enumerate(segments(tiles))]


def join_quad(blocks):
    lane = iota(blocks[0].shape, 1)
    parts = [turned_by(block, LANES - 32 * j) for j, block in enumerate(blocks)]
    return [
        jnp.where(lane < 96, parts[0], parts[1]),
        jnp.where(lane < 64, parts[1], parts[2]),
        jnp.where(lane < 32, parts[2], parts[3]),
    ]


def store_quad(state_ref, q, tiles):
    near, far = split_quad(tiles), shift_quad(tiles)
    for j in range(QUAD):
        state_ref[0, q * QUAD + j] = near[j].astype(jnp.bfloat16)
        state_ref[1, q * QUAD + j] = far[j].astype(jnp.bfloat16)


def tall(row_tile):
    return jnp.concatenate([row_tile] * (COLS // 8), axis=0)


def arrivals(peers):
    return [peers - 1] + list(range(1, peers - 1)) + [0]


def write_sent(peers, send_ref, count_ref, sign_ref, state_ref, sent_refs):
    me = lax.axis_index("patch")
    for i in range(peers):
        q = me ^ i
        for f in range(F):
            block = send_ref[q, f]
            scale = jnp.where(f < count_ref[q], 1.0, 0.0).astype(jnp.float32)
            sign = sign_ref[lax.rem(block, QUAD), pl.ds(lax.div(block, QUAD), 1), :] * scale
            picked = state_ref[0, block].astype(jnp.float32) * sign
            sent_refs[i][f] = picked.astype(jnp.bfloat16)


def copies(sources, targets, sems):
    started = [
        pltpu.make_async_copy(source, target, sems.at[i])
        for i, (source, target) in enumerate(zip(sources, targets))
    ]
    for one in started:
        one.start()
    return started


def prep_kernel(peers, *refs):
    sources, curl_hbm = refs[:5], refs[5]
    state_ref, sign_ref, source_ref, scale_ref, head_ref = refs[6:11]
    sent_refs = refs[11 : 11 + peers]
    held, sems = refs[11 + peers : -1], refs[-1]
    send_ref, count_ref, hole_ref, flip_ref, rhs_ref = held
    *needed, ahead = copies(
        sources + (curl_hbm.at[pl.ds(0, STAGES[0])],), held + (head_ref,), sems
    )
    for one in needed:
        one.wait()
    quads = NB // QUAD
    flips = [
        1.0 - 2.0 * flip_ref[pl.ds(u, quads, stride=TILES), :].astype(jnp.float32)
        for u in range(TILES)
    ]
    for j, sign in enumerate(split_quad(flips)):
        sign_ref[j] = sign
    lane = iota((8, LANES), 1)
    for q in range(quads):
        keeps = [hole_ref[q * QUAD + j].astype(jnp.float32) for j in range(QUAD)]
        tiles = []
        for u in range(TILES):
            at = (q * TILES + u) * LANES
            keep = jnp.where(lane < BS - 32 * u, keeps[u], keeps[u + 1])
            scale_ref[q * TILES + u] = COUPLING * keep
            tile = tall(keep) * rhs_ref[:, at : at + LANES].astype(jnp.float32)
            source_ref[q * TILES + u] = tile.astype(jnp.bfloat16)
            tiles.append(tile)
        store_quad(state_ref, q, tiles)
    write_sent(peers, send_ref, count_ref, sign_ref, state_ref, sent_refs)
    ahead.wait()


def picker(group):
    depth = 8 * TILES * group
    row = iota((32 * group, 2 * depth), 0)
    at = iota((32 * group, 2 * depth), 1)
    member, e = row // 32, row % 32
    r, j = e // QUAD, e % QUAD
    low = jnp.where(j == 0, 0, jnp.where(j == 1, 1, 2))
    high = jnp.where(j < 2, 0, j - 1)
    want_low = (r * TILES + low) * group + member
    want_high = (r * TILES + high) * group + member + depth
    return ((at == want_low) | (at == want_high)).astype(jnp.float32).astype(jnp.bfloat16)


def stack(select, first, second, group):
    depth = 8 * TILES * group
    parts = [rows[g * depth : (g + 1) * depth] for rows in (first, second) for g in range(3)]
    wide = jnp.concatenate(parts, axis=1)
    high = iota(wide.shape, 1) % LANES >= 64
    zero = jnp.zeros_like(wide)
    both = jnp.concatenate([jnp.where(high, zero, wide), jnp.where(high, wide, zero)], axis=0)
    picked = jnp.dot(select, both, preferred_element_type=jnp.float32).astype(jnp.bfloat16)
    return picked[:, : 3 * LANES], picked[:, 3 * LANES :]


def unstack(picked, member):
    mine = picked[32 * member : 32 * (member + 1)]
    return jnp.concatenate([mine[:, g * LANES : (g + 1) * LANES] for g in range(3)], axis=0)


def turn(square):
    turned = square.T
    bands = [turned[32 * a : 32 * (a + 1)] for a in range(4)]
    lane = iota((32, LANES), 1)
    for bit in (1, 2):
        odd = lane & bit == bit
        bands = [jnp.where(odd, bands[(a - bit) % 4], bands[a]) for a in range(4)]
    return jnp.concatenate(bands[: BS // 32], axis=0)


def spread_kernel(
    peers, curl_hbm, dtn_hbm, head_ref, matrix_ref, face_ref, curl_ref, dtn_ref, even_ref, odd_ref,
    sems,
):
    ahead = STAGES[0]
    pieces = (NB - ahead) // PIECE
    started = copies(
        [curl_hbm.at[pl.ds(ahead + i * PIECE, PIECE)] for i in range(pieces)] + [dtn_hbm],
        [curl_ref.at[pl.ds(i * PIECE, PIECE)] for i in range(pieces)] + [dtn_ref],
        sems,
    )
    select, select_faces = picker(K), picker(F)
    tasks, done = [([], [(select, head_ref, step, K) for step in range(ahead)])], 0
    for size in STAGES[1:]:
        waits = [started[i] for i in range(-(-done // PIECE), -(-(done + size) // PIECE))]
        tasks.append((waits, [(select, curl_ref, done + step, K) for step in range(size)]))
        done += size
    quarter = max(STAGES) * K // F
    for first in range(0, peers, quarter):
        waits = [started[pieces]] if first == 0 else []
        members = range(first, min(first + quarter, peers))
        faces = [(select_faces, dtn_ref, q, F) for q in members]
        tasks.append((waits, faces))

    def gather(task):
        waits, items = task
        for one in waits:
            one.wait()
        results = []
        for (pick, rows, n, size), (*_, other, _) in zip(items[::2], items[1::2]):
            pair = stack(pick, rows[n], rows[other], size)
            results += [(rows, n, size, pair[0]), (rows, other, size, pair[1])]
        return results

    def store(results, held_ref):
        for at, (rows, _, size, picked) in enumerate(results):
            for member in range(size):
                square = unstack(picked, member)
                if rows is dtn_ref:
                    slot, place = (at * size + member) // QUAD, member % QUAD
                else:
                    slot, place = at // QUAD * K + member, at % QUAD
                held_ref[slot, place * BS : (place + 1) * BS] = square

    def finish(results, held_ref):
        for at, (rows, n, size, _) in enumerate(results):
            if rows is dtn_ref:
                for member in range(size):
                    half, side = member // 2, slice(member % 2 * PAD, (member % 2 + 1) * PAD)
                    slot, place = (at * size + member) // QUAD, member % QUAD
                    pad = jnp.zeros((PAD - BS, LANES), jnp.bfloat16)
                    square = held_ref[slot, place * BS : (place + 1) * BS]
                    face_ref[n, half, :, side] = turn(jnp.concatenate([square, pad], axis=0))
            elif at % QUAD == 0:
                q = (n if rows is head_ref else ahead + n) // QUAD
                for k in range(K):
                    depth = slice(k % 2 * BS, (k % 2 + 1) * BS)
                    for u in range(TILES):
                        left = (q % 2 * TILES + u) * LANES
                        square = held_ref[at // QUAD * K + k, u * LANES : (u + 1) * LANES]
                        matrix_ref[q // 2, k // 2, depth, left : left + LANES] = turn(square)

    held = (even_ref, odd_ref)
    results = gather(tasks[0])
    store(results, held[0])
    for i in range(len(tasks)):
        upcoming = gather(tasks[i + 1]) if i + 1 < len(tasks) else []
        finish(results, held[i % 2])
        store(upcoming, held[(i + 1) % 2])
        results = upcoming


def paired(left, right, matrices):
    both = jnp.concatenate([left, right], axis=0)[:, :BS]
    wide = jnp.dot(both, matrices, preferred_element_type=jnp.float32)
    return wide[:COLS, :PAD], wide[COLS:, PAD:]


def add_faces(peers, target_ref, received_refs, face_ref, extra_ref):
    me = lax.axis_index("patch")
    products = []
    for i, received_ref in zip(arrivals(peers), received_refs):
        q = me ^ i
        for f in range(0, F, 2):
            pair = paired(received_ref[f], received_ref[f + 1], face_ref[q, f // 2])
            for step, product in enumerate(pair):
                products.append((q, f + step, product.astype(jnp.bfloat16).astype(jnp.float32)))
    for q, f, product in products:
        n = target_ref[q, f]
        extra_ref[f % 2, n] = extra_ref[f % 2, n] + product


def set_forcing(source_ref, scale_ref, extra_ref, forcing_ref):
    for q in range(NB // QUAD):
        blocks = range(q * QUAD, (q + 1) * QUAD)
        tiles = join_quad([extra_ref[0, n] + extra_ref[1, n] for n in blocks])
        for u, tile in enumerate(tiles):
            at = q * TILES + u
            kept = jnp.where(tall(scale_ref[at]) > 0, tile, 0.0)
            forcing_ref[at] = source_ref[at].astype(jnp.float32) + kept


def images_of(cols_ref, matrix_ref, old_ref, group):
    lane = iota((COLS, LANES), 1)

    def nearby(n, half):
        near = old_ref[0, cols_ref[2 * half, n]]
        far = old_ref[1, cols_ref[2 * half + 1, n]]
        return jnp.concatenate([jnp.where(lane < BS, near, far), far], axis=1)

    totals = [None] * (2 * TILES)
    for third, rows in enumerate(((0, 1, 2), (2, 3, 4, 5), (5, 6, 7))):
        columns = slice(third * 2 * LANES, (third + 1) * 2 * LANES)
        for half in range(K // 2):
            left = jnp.concatenate([nearby(group * 2 * QUAD + j, half) for j in rows], axis=0)
            wide = jnp.dot(
                left[:, : 2 * BS], matrix_ref[group, half, :, columns],
                preferred_element_type=jnp.float32,
            )
            for side in range(2):
                tile = third * 2 + side
                first = tile * LANES // BS
                cut = (first + 1) * BS - tile * LANES
                at = rows.index(first) * COLS
                part = wide[:, side * LANES : (side + 1) * LANES]
                picked = jnp.where(lane < cut, part[at : at + COLS], part[at + COLS : at + 2 * COLS])
                totals[tile] = picked if half == 0 else totals[tile] + picked
    return totals


def step_tile(forcing_ref, scale_ref, image, at):
    return forcing_ref[at] - tall(scale_ref[at]) * image


def sweep(cols_ref, scale_ref, matrix_ref, forcing_ref, old_ref, new_ref):
    groups = NB // (2 * QUAD)
    for first in range(0, groups, CHUNK):
        chunk = range(first, first + CHUNK)
        images = [images_of(cols_ref, matrix_ref, old_ref, group) for group in chunk]
        for group, parts in zip(chunk, images):
            tiles = [
                step_tile(forcing_ref, scale_ref, part, group * 2 * TILES + i)
                for i, part in enumerate(parts)
            ]
            for side in range(2):
                store_quad(new_ref, group * 2 + side, tiles[side * TILES : (side + 1) * TILES])


def end_blocks():
    odd = lax.rem(lax.axis_index("sec"), 2)
    return (1 - odd) * (NB - NI), odd * (NB - NI)


def first_tick_kernel(peers, *refs):
    cols_ref, target_ref, send_ref, count_ref = refs[:4]
    sign_ref, scale_ref, matrix_ref, face_ref, source_ref = refs[4:9]
    received_refs = refs[10 : 10 + peers]
    state_ref, swap_in_ref, swap_out_ref = refs[10 + peers : 13 + peers]
    sent_refs = refs[13 + peers : 13 + 2 * peers]
    forcing_ref, extra_ref, other_ref = refs[13 + 2 * peers :]
    extra_ref[...] = jnp.zeros_like(extra_ref)
    add_faces(peers, target_ref, received_refs, face_ref, extra_ref)
    set_forcing(source_ref, scale_ref, extra_ref, forcing_ref)

    def two(i, carry):
        sweep(cols_ref, scale_ref, matrix_ref, forcing_ref, state_ref, other_ref)
        sweep(cols_ref, scale_ref, matrix_ref, forcing_ref, other_ref, state_ref)
        return carry

    lax.fori_loop(0, ITERS // 2, two, 0)
    inner, outer = end_blocks()
    swap_in_ref[...] = state_ref[0, pl.ds(inner, NI)]
    swap_out_ref[...] = state_ref[0, pl.ds(outer, NI)]
    write_sent(peers, send_ref, count_ref, sign_ref, state_ref, sent_refs)


def first_step_kernel(peers, *refs):
    cols_ref, target_ref, scale_ref, matrix_ref, face_ref, source_ref, start_ref = refs[:7]
    received_refs, swap_in_ref = refs[7 : 7 + peers], refs[7 + peers]
    forcing_ref, state_ref, end_ref, extra_ref = refs[8 + peers :]
    inner, _ = end_blocks()
    extra_ref[...] = jnp.zeros_like(extra_ref)
    extra_ref[0, pl.ds(inner, NI)] = swap_in_ref[...].astype(jnp.float32)
    add_faces(peers, target_ref, received_refs, face_ref, extra_ref)
    set_forcing(source_ref, scale_ref, extra_ref, forcing_ref)
    groups = NB // (2 * QUAD)
    for group in range(groups):
        parts = images_of(cols_ref, matrix_ref, start_ref, group)
        tiles = [
            step_tile(forcing_ref, scale_ref, part, group * 2 * TILES + i)
            for i, part in enumerate(parts)
        ]
        for side in range(2):
            store_quad(state_ref, group * 2 + side, tiles[side * TILES : (side + 1) * TILES])
        if group in (0, groups - 1):
            for i, tile in enumerate(tiles):
                end_ref[group // (groups - 1), i] = tile


def last_tick_kernel(*refs):
    cols_ref, scale_ref, matrix_ref, end_ref, swap_out_ref = refs[:5]
    out_hbm, forcing_ref, state_ref, other_ref, out_ref, sems = refs[7:]
    odd = lax.rem(lax.axis_index("sec"), 2)
    for side in range(2):
        blocks = range(side * QUAD, (side + 1) * QUAD)
        arrived = join_quad([swap_out_ref[n].astype(jnp.float32) for n in blocks])
        stepped = []
        for u, tile in enumerate(arrived):
            i = side * TILES + u
            at = odd * ((NB - NI) * BS // LANES) + i
            kept = jnp.where(tall(scale_ref[at]) > 0, tile, 0.0)
            forcing_ref[at] = forcing_ref[at] + kept
            stepped.append(end_ref[odd, i] + kept)
        store_quad(state_ref, odd * ((NB - NI) // QUAD) + side, stepped)

    def two(i, carry):
        sweep(cols_ref, scale_ref, matrix_ref, forcing_ref, state_ref, other_ref)
        sweep(cols_ref, scale_ref, matrix_ref, forcing_ref, other_ref, state_ref)
        return carry

    lax.fori_loop(0, ITERS // 2 - 1, two, 0)
    groups = NB // (2 * QUAD)
    width = 2 * groups // OUT_PIECES * TILES * LANES
    leaving = []
    for group in range(groups):
        for i, part in enumerate(images_of(cols_ref, matrix_ref, state_ref, group)):
            at = group * 2 * TILES + i
            out_ref[:, at * LANES : (at + 1) * LANES] = step_tile(forcing_ref, scale_ref, part, at)
        if (group + 1) % (groups // OUT_PIECES) == 0:
            piece = len(leaving)
            columns = pl.ds(piece * width, width)
            leaving.append(
                pltpu.make_async_copy(out_ref.at[:, columns], out_hbm.at[:, columns], sems.at[piece])
            )
            leaving[-1].start()
    for one in leaving:
        one.wait()


def swapped(x, axis, first):
    size = lax.axis_size(axis)
    pairs = []
    for i in range(first, size - 1, 2):
        pairs += [(i, i + 1), (i + 1, i)]
    return lax.ppermute(x, axis, pairs)


def shape(dims, dtype):
    return jax.ShapeDtypeStruct(dims, dtype)


def shards(
    rhs, curl_blocks, block_cols, hole_mask, edge_flip, send_list, send_count, recv_list, dtn_blocks
):
    peers = send_list.shape[2]
    f32, bf16 = jnp.float32, jnp.bfloat16
    tiles = BS * BS // LANES
    cols = block_cols.T
    in_hbm = functools.partial(pltpu.with_memory_space_constraint, memory_space=pltpu.HBM)
    sends, counts, targets = send_list[0, 0], send_count[0, 0], recv_list[0, 0]
    flips = edge_flip.reshape(NB * BS // LANES, LANES)
    curl_rows = curl_blocks.reshape(NB, K, tiles, LANES).transpose(0, 2, 1, 3)
    curl_rows = curl_rows.reshape(NB, tiles * K, LANES)
    dtn_rows = dtn_blocks[0, 0].reshape(peers, F, tiles, LANES).transpose(0, 2, 1, 3)
    dtn_rows = dtn_rows.reshape(peers, tiles * F, LANES)

    count = NB * BS // LANES
    block_shape = (NB, COLS, PAD)
    tile_shape = (count, COLS, LANES)
    state_shape = (2, NB, COLS, PAD)
    face = shape((F, COLS, PAD), bf16)
    ends = shape((NI, COLS, PAD), bf16)
    state, sign, source, scale, head, *sent = pl.pallas_call(
        functools.partial(prep_kernel, peers),
        out_shape=(
            shape(state_shape, bf16),
            shape((QUAD, NB // QUAD, LANES), f32),
            shape(tile_shape, bf16),
            shape((count, 8, LANES), f32),
            shape((STAGES[0],) + curl_rows.shape[1:], bf16),
        )
        + (face,) * peers,
        in_specs=[HBM] * 6,
        out_specs=[VMEM] * (5 + peers),
        scratch_shapes=[
            pltpu.SMEM(sends.shape, jnp.int32),
            pltpu.SMEM(counts.shape, jnp.int32),
            pltpu.SMEM(hole_mask.shape, jnp.int32),
            pltpu.VMEM(flips.shape, jnp.int32),
            pltpu.VMEM(rhs.shape, bf16),
            pltpu.SemaphoreType.DMA((6,)),
        ],
        compiler_params=params(),
        cost_estimate=cost(10**6, 10**6),
    )(*map(in_hbm, (sends, counts, hole_mask, flips, rhs, curl_rows)))

    matrices, faces = pl.pallas_call(
        functools.partial(spread_kernel, peers),
        out_shape=(
            shape((NB // (2 * QUAD), K // 2, 2 * BS, 2 * TILES * LANES), bf16),
            shape((peers, F // 2, BS, 2 * PAD), bf16),
        ),
        in_specs=[HBM] * 2 + [VMEM],
        out_specs=[VMEM] * 2,
        scratch_shapes=[
            pltpu.VMEM((NB - STAGES[0],) + curl_rows.shape[1:], bf16),
            pltpu.VMEM(dtn_rows.shape, bf16),
            pltpu.VMEM((max(STAGES) * K // QUAD, QUAD * BS, LANES), bf16),
            pltpu.VMEM((max(STAGES) * K // QUAD, QUAD * BS, LANES), bf16),
            pltpu.SemaphoreType.DMA(((NB - STAGES[0]) // PIECE + 1,)),
        ],
        compiler_params=params(),
        cost_estimate=cost(4 * 10**9, 16 * 10**6),
    )(in_hbm(curl_rows), in_hbm(dtn_rows), head)

    def exchange(sent):
        pairs = [[(p, p ^ i) for p in range(peers)] for i in range(peers)]
        return [lax.ppermute(sent[i], "patch", pairs[i]) if i else sent[0] for i in arrivals(peers)]

    received = exchange(sent)
    state, swap_in, swap_out, *sent = pl.pallas_call(
        functools.partial(first_tick_kernel, peers),
        out_shape=(shape(state_shape, bf16), ends, ends) + (face,) * peers,
        in_specs=[SMEM] * 4 + [VMEM] * (6 + peers),
        out_specs=[VMEM] * (3 + peers),
        scratch_shapes=[
            pltpu.VMEM(tile_shape, f32),
            pltpu.VMEM((2,) + block_shape, f32),
            pltpu.VMEM(state_shape, bf16),
        ],
        input_output_aliases={9: 0},
        compiler_params=params(),
        cost_estimate=cost(10**10, 16 * 10**6),
    )(cols, targets, sends, counts, sign, scale, matrices, faces, source, state, *received)

    received = exchange(sent)
    swap_in = swapped(swap_in, "sec", 0)
    swap_out = swapped(swap_out, "sec", 1)
    forcing, state, end = pl.pallas_call(
        functools.partial(first_step_kernel, peers),
        out_shape=(
            shape(tile_shape, f32),
            shape(state_shape, bf16),
            shape((2, 2 * TILES, COLS, LANES), f32),
        ),
        in_specs=[SMEM] * 2 + [VMEM] * (6 + peers),
        out_specs=[VMEM] * 3,
        scratch_shapes=[pltpu.VMEM((2,) + block_shape, f32)],
        compiler_params=params(),
        cost_estimate=cost(10**9, 8 * 10**6),
    )(cols, targets, scale, matrices, faces, source, state, *received, swap_in)
    out, _, _ = pl.pallas_call(
        last_tick_kernel,
        out_shape=(shape((COLS, NB * BS), f32), shape(tile_shape, f32), shape(state_shape, bf16)),
        in_specs=[SMEM] + [VMEM] * 6,
        out_specs=[HBM] + [VMEM] * 2,
        scratch_shapes=[
            pltpu.VMEM(state_shape, bf16),
            pltpu.VMEM((COLS, NB * BS), f32),
            pltpu.SemaphoreType.DMA((OUT_PIECES,)),
        ],
        input_output_aliases={5: 1, 6: 2},
        compiler_params=params(),
        cost_estimate=cost(10**10, 16 * 10**6),
    )(cols, scale, matrices, end, swap_out, forcing, state)
    return out


def solution(mesh):
    in_specs = (
        P(None, ("sec", "patch")),
        P(("sec", "patch"), None, None),
        P(("sec", "patch"), None),
        P(("sec", "patch")),
        P(("sec", "patch")),
        P("sec", "patch", None, None),
        P("sec", "patch", None),
        P("sec", "patch", None, None),
        P("sec", "patch", None, None, None),
    )
    out_specs = P(None, ("sec", "patch"))
    return jax.shard_map(shards, mesh=mesh, in_specs=in_specs, out_specs=out_specs, check_vma=False)
```

```python
import functools

import jax
import jax.numpy as jnp
from jax import lax
from jax.experimental import pallas as pl
from jax.experimental.pallas import tpu as pltpu
from jax.sharding import PartitionSpec as P

BS = 96
COLS = 24
NB = 64
K = 4
F = 8
NI = 8
ITERS = 8
TICKS = 2
COUPLING = 0.85

LANES = 128
PAD = 128
QUAD = 4
TILES = 3
VMEM_LIMIT = 30 * 2**20
STAGES = (16, 16, 16, 16)
PIECE = 8
OUT_PIECES = 4
CHUNK = 4

VMEM = pl.BlockSpec(memory_space=pltpu.VMEM)
SMEM = pl.BlockSpec(memory_space=pltpu.SMEM)
HBM = pl.BlockSpec(memory_space=pltpu.HBM)


def params():
    return pltpu.CompilerParams(vmem_limit_bytes=VMEM_LIMIT)


def cost(flops, size):
    return pl.CostEstimate(flops=flops, bytes_accessed=size, transcendentals=0)


def iota(shape, axis):
    return lax.broadcasted_iota(jnp.int32, shape, axis)


def segments(tiles):
    first, second, third = tiles
    lane = iota(first.shape, 1)
    low = lane < 64
    return first, jnp.where(low, second, first), jnp.where(low, third, second), third


def turned_by(x, lanes):
    return pltpu.roll(x, lanes % LANES, 1) if lanes % LANES else x


def split_quad(tiles):
    return [turned_by(part, 32 * j) for j, part in enumerate(segments(tiles))]


def shift_quad(tiles):
    return [turned_by(part, 32 * j + BS) for j, part in enumerate(segments(tiles))]


def join_quad(blocks):
    lane = iota(blocks[0].shape, 1)
    parts = [turned_by(block, LANES - 32 * j) for j, block in enumerate(blocks)]
    return [
        jnp.where(lane < 96, parts[0], parts[1]),
        jnp.where(lane < 64, parts[1], parts[2]),
        jnp.where(lane < 32, parts[2], parts[3]),
    ]


def store_quad(state_ref, q, tiles):
    near, far = split_quad(tiles), shift_quad(tiles)
    for j in range(QUAD):
        state_ref[0, q * QUAD + j] = near[j].astype(jnp.bfloat16)
        state_ref[1, q * QUAD + j] = far[j].astype(jnp.bfloat16)


def tall(row_tile):
    return jnp.concatenate([row_tile] * (COLS // 8), axis=0)


def arrivals(peers):
    return [peers - 1] + list(range(1, peers - 1)) + [0]


def write_sent(peers, send_ref, count_ref, sign_ref, state_ref, sent_refs):
    me = lax.axis_index("patch")
    for i in range(peers):
        q = me ^ i
        for f in range(F):
            block = send_ref[q, f]
            scale = jnp.where(f < count_ref[q], 1.0, 0.0).astype(jnp.float32)
            sign = sign_ref[lax.rem(block, QUAD), pl.ds(lax.div(block, QUAD), 1), :] * scale
            picked = state_ref[0, block].astype(jnp.float32) * sign
            sent_refs[i][f] = picked.astype(jnp.bfloat16)


def copies(sources, targets, sems):
    started = [
        pltpu.make_async_copy(source, target, sems.at[i])
        for i, (source, target) in enumerate(zip(sources, targets))
    ]
    for one in started:
        one.start()
    return started


def prep_kernel(peers, *refs):
    sources, curl_hbm = refs[:5], refs[5]
    state_ref, sign_ref, source_ref, scale_ref, head_ref = refs[6:11]
    sent_refs = refs[11 : 11 + peers]
    held, sems = refs[11 + peers : -1], refs[-1]
    send_ref, count_ref, hole_ref, flip_ref, rhs_ref = held
    *needed, ahead = copies(
        sources + (curl_hbm.at[pl.ds(0, STAGES[0])],), held + (head_ref,), sems
    )
    for one in needed:
        one.wait()
    quads = NB // QUAD
    flips = [
        1.0 - 2.0 * flip_ref[pl.ds(u, quads, stride=TILES), :].astype(jnp.float32)
        for u in range(TILES)
    ]
    for j, sign in enumerate(split_quad(flips)):
        sign_ref[j] = sign
    lane = iota((8, LANES), 1)
    for q in range(quads):
        keeps = [hole_ref[q * QUAD + j].astype(jnp.float32) for j in range(QUAD)]
        tiles = []
        for u in range(TILES):
            at = (q * TILES + u) * LANES
            keep = jnp.where(lane < BS - 32 * u, keeps[u], keeps[u + 1])
            scale_ref[q * TILES + u] = COUPLING * keep
            tile = tall(keep) * rhs_ref[:, at : at + LANES].astype(jnp.float32)
            source_ref[q * TILES + u] = tile.astype(jnp.bfloat16)
            tiles.append(tile)
        store_quad(state_ref, q, tiles)
    write_sent(peers, send_ref, count_ref, sign_ref, state_ref, sent_refs)
    ahead.wait()


def picker(group):
    depth = 8 * TILES * group
    row = iota((32 * group, 2 * depth), 0)
    at = iota((32 * group, 2 * depth), 1)
    member, e = row // 32, row % 32
    r, j = e // QUAD, e % QUAD
    low = jnp.where(j == 0, 0, jnp.where(j == 1, 1, 2))
    high = jnp.where(j < 2, 0, j - 1)
    want_low = (r * TILES + low) * group + member
    want_high = (r * TILES + high) * group + member + depth
    return ((at == want_low) | (at == want_high)).astype(jnp.float32).astype(jnp.bfloat16)


def stack(select, first, second, group):
    depth = 8 * TILES * group
    parts = [rows[g * depth : (g + 1) * depth] for rows in (first, second) for g in range(3)]
    wide = jnp.concatenate(parts, axis=1)
    high = iota(wide.shape, 1) % LANES >= 64
    zero = jnp.zeros_like(wide)
    both = jnp.concatenate([jnp.where(high, zero, wide), jnp.where(high, wide, zero)], axis=0)
    picked = jnp.dot(select, both, preferred_element_type=jnp.float32).astype(jnp.bfloat16)
    return picked[:, : 3 * LANES], picked[:, 3 * LANES :]


def unstack(picked, member):
    mine = picked[32 * member : 32 * (member + 1)]
    return jnp.concatenate([mine[:, g * LANES : (g + 1) * LANES] for g in range(3)], axis=0)


def turn(square):
    turned = square.T
    bands = [turned[32 * a : 32 * (a + 1)] for a in range(4)]
    lane = iota((32, LANES), 1)
    for bit in (1, 2):
        odd = lane & bit == bit
        bands = [jnp.where(odd, bands[(a - bit) % 4], bands[a]) for a in range(4)]
    return jnp.concatenate(bands[: BS // 32], axis=0)


def spread_kernel(
    peers, curl_hbm, dtn_hbm, head_ref, matrix_ref, face_ref, curl_ref, dtn_ref, even_ref, odd_ref,
    sems,
):
    ahead = STAGES[0]
    pieces = (NB - ahead) // PIECE
    started = copies(
        [curl_hbm.at[pl.ds(ahead + i * PIECE, PIECE)] for i in range(pieces)] + [dtn_hbm],
        [curl_ref.at[pl.ds(i * PIECE, PIECE)] for i in range(pieces)] + [dtn_ref],
        sems,
    )
    select, select_faces = picker(K), picker(F)
    tasks, done = [([], [(select, head_ref, step, K) for step in range(ahead)])], 0
    for size in STAGES[1:]:
        waits = [started[i] for i in range(-(-done // PIECE), -(-(done + size) // PIECE))]
        tasks.append((waits, [(select, curl_ref, done + step, K) for step in range(size)]))
        done += size
    quarter = max(STAGES) * K // F
    for first in range(0, peers, quarter):
        waits = [started[pieces]] if first == 0 else []
        members = range(first, min(first + quarter, peers))
        faces = [(select_faces, dtn_ref, q, F) for q in members]
        tasks.append((waits, faces))

    def gather(task):
        waits, items = task
        for one in waits:
            one.wait()
        results = []
        for (pick, rows, n, size), (*_, other, _) in zip(items[::2], items[1::2]):
            pair = stack(pick, rows[n], rows[other], size)
            results += [(rows, n, size, pair[0]), (rows, other, size, pair[1])]
        return results

    def store(results, held_ref):
        for at, (rows, _, size, picked) in enumerate(results):
            for member in range(size):
                square = unstack(picked, member)
                if rows is dtn_ref:
                    slot, place = (at * size + member) // QUAD, member % QUAD
                else:
                    slot, place = at // QUAD * K + member, at % QUAD
                held_ref[slot, place * BS : (place + 1) * BS] = square

    def finish(results, held_ref):
        for at, (rows, n, size, _) in enumerate(results):
            if rows is dtn_ref:
                for member in range(size):
                    half, side = member // 2, slice(member % 2 * PAD, (member % 2 + 1) * PAD)
                    slot, place = (at * size + member) // QUAD, member % QUAD
                    pad = jnp.zeros((PAD - BS, LANES), jnp.bfloat16)
                    square = held_ref[slot, place * BS : (place + 1) * BS]
                    face_ref[n, half, :, side] = turn(jnp.concatenate([square, pad], axis=0))
            elif at % QUAD == 0:
                q = (n if rows is head_ref else ahead + n) // QUAD
                for k in range(K):
                    depth = slice(k % 2 * BS, (k % 2 + 1) * BS)
                    for u in range(TILES):
                        left = (q % 2 * TILES + u) * LANES
                        square = held_ref[at // QUAD * K + k, u * LANES : (u + 1) * LANES]
                        matrix_ref[q // 2, k // 2, depth, left : left + LANES] = turn(square)

    held = (even_ref, odd_ref)
    results = gather(tasks[0])
    store(results, held[0])
    for i in range(len(tasks)):
        upcoming = gather(tasks[i + 1]) if i + 1 < len(tasks) else []
        finish(results, held[i % 2])
        store(upcoming, held[(i + 1) % 2])
        results = upcoming


def paired(left, right, matrices):
    both = jnp.concatenate([left, right], axis=0)[:, :BS]
    wide = jnp.dot(both, matrices, preferred_element_type=jnp.float32)
    return wide[:COLS, :PAD], wide[COLS:, PAD:]


def add_faces(peers, target_ref, received_refs, face_ref, extra_ref):
    me = lax.axis_index("patch")
    products = []
    for i, received_ref in zip(arrivals(peers), received_refs):
        q = me ^ i
        for f in range(0, F, 2):
            pair = paired(received_ref[f], received_ref[f + 1], face_ref[q, f // 2])
            for step, product in enumerate(pair):
                products.append((q, f + step, product.astype(jnp.bfloat16).astype(jnp.float32)))
    for q, f, product in products:
        n = target_ref[q, f]
        extra_ref[f % 2, n] = extra_ref[f % 2, n] + product


def set_forcing(source_ref, scale_ref, extra_ref, forcing_ref):
    for q in range(NB // QUAD):
        blocks = range(q * QUAD, (q + 1) * QUAD)
        tiles = join_quad([extra_ref[0, n] + extra_ref[1, n] for n in blocks])
        for u, tile in enumerate(tiles):
            at = q * TILES + u
            kept = jnp.where(tall(scale_ref[at]) > 0, tile, 0.0)
            forcing_ref[at] = source_ref[at].astype(jnp.float32) + kept


def images_of(cols_ref, matrix_ref, old_ref, group):
    lane = iota((COLS, LANES), 1)

    def nearby(n, half):
        near = old_ref[0, cols_ref[2 * half, n]]
        far = old_ref[1, cols_ref[2 * half + 1, n]]
        return jnp.concatenate([jnp.where(lane < BS, near, far), far], axis=1)

    totals = [None] * (2 * TILES)
    for third, rows in enumerate(((0, 1, 2), (2, 3, 4, 5), (5, 6, 7))):
        columns = slice(third * 2 * LANES, (third + 1) * 2 * LANES)
        for half in range(K // 2):
            left = jnp.concatenate([nearby(group * 2 * QUAD + j, half) for j in rows], axis=0)
            wide = jnp.dot(
                left[:, : 2 * BS], matrix_ref[group, half, :, columns],
                preferred_element_type=jnp.float32,
            )
            for side in range(2):
                tile = third * 2 + side
                first = tile * LANES // BS
                cut = (first + 1) * BS - tile * LANES
                at = rows.index(first) * COLS
                part = wide[:, side * LANES : (side + 1) * LANES]
                picked = jnp.where(lane < cut, part[at : at + COLS], part[at + COLS : at + 2 * COLS])
                totals[tile] = picked if half == 0 else totals[tile] + picked
    return totals


def step_tile(forcing_ref, scale_ref, image, at):
    return forcing_ref[at] - tall(scale_ref[at]) * image


def sweep(cols_ref, scale_ref, matrix_ref, forcing_ref, old_ref, new_ref):
    groups = NB // (2 * QUAD)
    for first in range(0, groups, CHUNK):
        chunk = range(first, first + CHUNK)
        images = [images_of(cols_ref, matrix_ref, old_ref, group) for group in chunk]
        for group, parts in zip(chunk, images):
            tiles = [
                step_tile(forcing_ref, scale_ref, part, group * 2 * TILES + i)
                for i, part in enumerate(parts)
            ]
            for side in range(2):
                store_quad(new_ref, group * 2 + side, tiles[side * TILES : (side + 1) * TILES])


def end_blocks():
    odd = lax.rem(lax.axis_index("sec"), 2)
    return (1 - odd) * (NB - NI), odd * (NB - NI)


def first_tick_kernel(peers, *refs):
    cols_ref, target_ref, send_ref, count_ref = refs[:4]
    sign_ref, scale_ref, matrix_ref, face_ref, source_ref = refs[4:9]
    received_refs = refs[10 : 10 + peers]
    state_ref, swap_in_ref, swap_out_ref = refs[10 + peers : 13 + peers]
    sent_refs = refs[13 + peers : 13 + 2 * peers]
    forcing_ref, extra_ref, other_ref = refs[13 + 2 * peers :]
    extra_ref[...] = jnp.zeros_like(extra_ref)
    add_faces(peers, target_ref, received_refs, face_ref, extra_ref)
    set_forcing(source_ref, scale_ref, extra_ref, forcing_ref)

    def two(i, carry):
        sweep(cols_ref, scale_ref, matrix_ref, forcing_ref, state_ref, other_ref)
        sweep(cols_ref, scale_ref, matrix_ref, forcing_ref, other_ref, state_ref)
        return carry

    lax.fori_loop(0, ITERS // 2, two, 0)
    inner, outer = end_blocks()
    swap_in_ref[...] = state_ref[0, pl.ds(inner, NI)]
    swap_out_ref[...] = state_ref[0, pl.ds(outer, NI)]
    write_sent(peers, send_ref, count_ref, sign_ref, state_ref, sent_refs)


def first_image_kernel(cols_ref, matrix_ref, state_ref, image_ref):
    for group in range(NB // (2 * QUAD)):
        for i, part in enumerate(images_of(cols_ref, matrix_ref, state_ref, group)):
            image_ref[group * 2 * TILES + i] = part


def first_step_kernel(peers, *refs):
    target_ref, scale_ref, face_ref, source_ref, image_ref = refs[:5]
    received_refs, swap_in_ref = refs[5 : 5 + peers], refs[5 + peers]
    forcing_ref, state_ref, end_ref, extra_ref = refs[6 + peers :]
    inner, _ = end_blocks()
    extra_ref[...] = jnp.zeros_like(extra_ref)
    extra_ref[0, pl.ds(inner, NI)] = swap_in_ref[...].astype(jnp.float32)
    add_faces(peers, target_ref, received_refs, face_ref, extra_ref)
    set_forcing(source_ref, scale_ref, extra_ref, forcing_ref)
    groups = NB // (2 * QUAD)
    for group in range(groups):
        first = group * 2 * TILES
        tiles = [
            step_tile(forcing_ref, scale_ref, image_ref[at], at)
            for at in range(first, first + 2 * TILES)
        ]
        for side in range(2):
            store_quad(state_ref, group * 2 + side, tiles[side * TILES : (side + 1) * TILES])
        if group in (0, groups - 1):
            for i, tile in enumerate(tiles):
                end_ref[group // (groups - 1), i] = tile


def last_tick_kernel(*refs):
    cols_ref, scale_ref, matrix_ref, end_ref, swap_out_ref = refs[:5]
    out_hbm, forcing_ref, state_ref, other_ref, out_ref, sems = refs[7:]
    odd = lax.rem(lax.axis_index("sec"), 2)
    for side in range(2):
        blocks = range(side * QUAD, (side + 1) * QUAD)
        arrived = join_quad([swap_out_ref[n].astype(jnp.float32) for n in blocks])
        stepped = []
        for u, tile in enumerate(arrived):
            i = side * TILES + u
            at = odd * ((NB - NI) * BS // LANES) + i
            kept = jnp.where(tall(scale_ref[at]) > 0, tile, 0.0)
            forcing_ref[at] = forcing_ref[at] + kept
            stepped.append(end_ref[odd, i] + kept)
        store_quad(state_ref, odd * ((NB - NI) // QUAD) + side, stepped)

    def two(i, carry):
        sweep(cols_ref, scale_ref, matrix_ref, forcing_ref, state_ref, other_ref)
        sweep(cols_ref, scale_ref, matrix_ref, forcing_ref, other_ref, state_ref)
        return carry

    lax.fori_loop(0, ITERS // 2 - 1, two, 0)
    groups = NB // (2 * QUAD)
    width = 2 * groups // OUT_PIECES * TILES * LANES
    leaving = []
    for group in range(groups):
        for i, part in enumerate(images_of(cols_ref, matrix_ref, state_ref, group)):
            at = group * 2 * TILES + i
            out_ref[:, at * LANES : (at + 1) * LANES] = step_tile(forcing_ref, scale_ref, part, at)
        if (group + 1) % (groups // OUT_PIECES) == 0:
            piece = len(leaving)
            columns = pl.ds(piece * width, width)
            leaving.append(
                pltpu.make_async_copy(out_ref.at[:, columns], out_hbm.at[:, columns], sems.at[piece])
            )
            leaving[-1].start()
    for one in leaving:
        one.wait()


def swapped(x, axis, first):
    size = lax.axis_size(axis)
    pairs = []
    for i in range(first, size - 1, 2):
        pairs += [(i, i + 1), (i + 1, i)]
    return lax.ppermute(x, axis, pairs)


def shape(dims, dtype):
    return jax.ShapeDtypeStruct(dims, dtype)


def shards(
    rhs, curl_blocks, block_cols, hole_mask, edge_flip, send_list, send_count, recv_list, dtn_blocks
):
    peers = send_list.shape[2]
    f32, bf16 = jnp.float32, jnp.bfloat16
    tiles = BS * BS // LANES
    cols = block_cols.T
    in_hbm = functools.partial(pltpu.with_memory_space_constraint, memory_space=pltpu.HBM)
    sends, counts, targets = send_list[0, 0], send_count[0, 0], recv_list[0, 0]
    flips = edge_flip.reshape(NB * BS // LANES, LANES)
    curl_rows = curl_blocks.reshape(NB, K, tiles, LANES).transpose(0, 2, 1, 3)
    curl_rows = curl_rows.reshape(NB, tiles * K, LANES)
    dtn_rows = dtn_blocks[0, 0].reshape(peers, F, tiles, LANES).transpose(0, 2, 1, 3)
    dtn_rows = dtn_rows.reshape(peers, tiles * F, LANES)

    count = NB * BS // LANES
    block_shape = (NB, COLS, PAD)
    tile_shape = (count, COLS, LANES)
    state_shape = (2, NB, COLS, PAD)
    face = shape((F, COLS, PAD), bf16)
    ends = shape((NI, COLS, PAD), bf16)
    state, sign, source, scale, head, *sent = pl.pallas_call(
        functools.partial(prep_kernel, peers),
        out_shape=(
            shape(state_shape, bf16),
            shape((QUAD, NB // QUAD, LANES), f32),
            shape(tile_shape, bf16),
            shape((count, 8, LANES), f32),
            shape((STAGES[0],) + curl_rows.shape[1:], bf16),
        )
        + (face,) * peers,
        in_specs=[HBM] * 6,
        out_specs=[VMEM] * (5 + peers),
        scratch_shapes=[
            pltpu.SMEM(sends.shape, jnp.int32),
            pltpu.SMEM(counts.shape, jnp.int32),
            pltpu.SMEM(hole_mask.shape, jnp.int32),
            pltpu.VMEM(flips.shape, jnp.int32),
            pltpu.VMEM(rhs.shape, bf16),
            pltpu.SemaphoreType.DMA((6,)),
        ],
        compiler_params=params(),
        cost_estimate=cost(10**6, 10**6),
    )(*map(in_hbm, (sends, counts, hole_mask, flips, rhs, curl_rows)))

    matrices, faces = pl.pallas_call(
        functools.partial(spread_kernel, peers),
        out_shape=(
            shape((NB // (2 * QUAD), K // 2, 2 * BS, 2 * TILES * LANES), bf16),
            shape((peers, F // 2, BS, 2 * PAD), bf16),
        ),
        in_specs=[HBM] * 2 + [VMEM],
        out_specs=[VMEM] * 2,
        scratch_shapes=[
            pltpu.VMEM((NB - STAGES[0],) + curl_rows.shape[1:], bf16),
            pltpu.VMEM(dtn_rows.shape, bf16),
            pltpu.VMEM((max(STAGES) * K // QUAD, QUAD * BS, LANES), bf16),
            pltpu.VMEM((max(STAGES) * K // QUAD, QUAD * BS, LANES), bf16),
            pltpu.SemaphoreType.DMA(((NB - STAGES[0]) // PIECE + 1,)),
        ],
        compiler_params=params(),
        cost_estimate=cost(4 * 10**9, 16 * 10**6),
    )(in_hbm(curl_rows), in_hbm(dtn_rows), head)

    def exchange(sent):
        pairs = [[(p, p ^ i) for p in range(peers)] for i in range(peers)]
        return [lax.ppermute(sent[i], "patch", pairs[i]) if i else sent[0] for i in arrivals(peers)]

    received = exchange(sent)
    state, swap_in, swap_out, *sent = pl.pallas_call(
        functools.partial(first_tick_kernel, peers),
        out_shape=(shape(state_shape, bf16), ends, ends) + (face,) * peers,
        in_specs=[SMEM] * 4 + [VMEM] * (6 + peers),
        out_specs=[VMEM] * (3 + peers),
        scratch_shapes=[
            pltpu.VMEM(tile_shape, f32),
            pltpu.VMEM((2,) + block_shape, f32),
            pltpu.VMEM(state_shape, bf16),
        ],
        input_output_aliases={9: 0},
        compiler_params=params(),
        cost_estimate=cost(10**10, 16 * 10**6),
    )(cols, targets, sends, counts, sign, scale, matrices, faces, source, state, *received)

    received = exchange(sent)
    swap_in = swapped(swap_in, "sec", 0)
    swap_out = swapped(swap_out, "sec", 1)
    image = pl.pallas_call(
        first_image_kernel,
        out_shape=shape(tile_shape, f32),
        in_specs=[SMEM] + [VMEM] * 2,
        out_specs=VMEM,
        compiler_params=params(),
        cost_estimate=cost(10**9, 8 * 10**6),
    )(cols, matrices, state)
    forcing, state, end = pl.pallas_call(
        functools.partial(first_step_kernel, peers),
        out_shape=(
            shape(tile_shape, f32),
            shape(state_shape, bf16),
            shape((2, 2 * TILES, COLS, LANES), f32),
        ),
        in_specs=[SMEM] + [VMEM] * (5 + peers),
        out_specs=[VMEM] * 3,
        scratch_shapes=[pltpu.VMEM((2,) + block_shape, f32)],
        compiler_params=params(),
        cost_estimate=cost(10**9, 8 * 10**6),
    )(targets, scale, faces, source, image, *received, swap_in)
    out, _, _ = pl.pallas_call(
        last_tick_kernel,
        out_shape=(shape((COLS, NB * BS), f32), shape(tile_shape, f32), shape(state_shape, bf16)),
        in_specs=[SMEM] + [VMEM] * 6,
        out_specs=[HBM] + [VMEM] * 2,
        scratch_shapes=[
            pltpu.VMEM(state_shape, bf16),
            pltpu.VMEM((COLS, NB * BS), f32),
            pltpu.SemaphoreType.DMA((OUT_PIECES,)),
        ],
        input_output_aliases={5: 1, 6: 2},
        compiler_params=params(),
        cost_estimate=cost(10**10, 16 * 10**6),
    )(cols, scale, matrices, end, swap_out, forcing, state)
    return out


def solution(mesh):
    in_specs = (
        P(None, ("sec", "patch")),
        P(("sec", "patch"), None, None),
        P(("sec", "patch"), None),
        P(("sec", "patch")),
        P(("sec", "patch")),
        P("sec", "patch", None, None),
        P("sec", "patch", None),
        P("sec", "patch", None, None),
        P("sec", "patch", None, None, None),
    )
    out_specs = P(None, ("sec", "patch"))
    return jax.shard_map(shards, mesh=mesh, in_specs=in_specs, out_specs=out_specs, check_vma=False)
```
